32 devices in a mesh: expert: 8 (over z, y), context: 4 (over x, core).
Axes of the slice: x: 2, y: 2, z: 4, core: 2. Of those that a mesh axis runs over, the one named last changes fastest.
Arguments:
- tokens: bfloat16 [8, 512, 2048], P('expert', 'context'), may hold values from -6 to 6
- route: int32 [8, 512, 1], P('expert'), may hold values from 0 to 7; in each aligned block of 128 rows (0 to 127, 128 to 255, ..., all dimensions but the last counted through in order) at most 32 rows name the same one
- w_inner: bfloat16 [8, 2048, 2, 4096], P('expert', None, None, 'context'), may hold values from -0.125 to 0.125
- w_state: bfloat16 [8, 2048, 128], P('expert'), may hold values from -0.015625 to 0.015625
- w_step: bfloat16 [8, 2048, 64], P('expert', None, 'context'), may hold values from -0.125 to 0.125
- step_bias: float32 [64], P('context'), may hold values from -2 to 0.5
- decay_log: float32 [64], P('context'), may hold values from -7 to -2.5
- skip_gain: float32 [64], P('context'), may hold values from 0.5 to 1.5
- conv_weight: float32 [4, 4096], P(None, 'context'), may hold values from -3 to 3
- conv_bias: float32 [4096], P('context'), may hold values from -1.5 to 1.5
- w_out: bfloat16 [8, 4096, 2048], P('expert', 'context'), may hold values from -0.09375 to 0.09375
Outputs:
- mixed: bfloat16 [8, 512, 2048], P('expert', 'context')
The draws below stay inside these ranges and needn't reach their ends.
Inputs may be any that keep to these rules, and one draw needn't show every extreme that they name: `route`: in each aligned block of 128 positions (the rows of one device) no expert is named more than 32 times, a bound that some block reaches.
All inputs are finite; a program needn't handle non-finite values.
Results may differ from the reference program's by a relative error of at most 0.014.
Values may be sent and summed in bfloat16 or wider, within the bound.
No kernel may reach another device: no remote copies, remote signals or barrier semaphores. Data moves between devices by JAX's collectives and lax.ppermute only.
A program may use at most 128 MiB of HBM per device.

```python
import math
import jax
import jax.numpy as jnp
import numpy as np
from jax import lax

D = 2048
DI = 4096
NSTATE = 64
HEAD_DIM = 64
CONV = 4
TOK_DEV = 128
EXPERTS = 8
SEQS = 8
SEQLEN = 512
HEADS = 64
CAP = 32
N_CONTEXT = 4


def steps_of(stream_key, shape, cuts, smallest, high):
    level, own = 1.0, jax.random.fold_in(stream_key, 6)
    for position, blocks in cuts:
        draws = jnp.exp(jax.random.uniform(jax.random.fold_in(own, position), (blocks,), jnp.float32, smallest / len(cuts), high / len(cuts)))
        level = level * jnp.repeat(draws, shape[position] // blocks).reshape([-1 if axis == position else 1 for axis in range(len(shape))])
    return level


def routed_block(rng, own, number, rows, amount, top, most, lean):
    sequence = jax.random.permutation(rng, amount)
    heavy_load, ordinary = load_shares(amount, rows * top, most, lean, True), load_shares(amount, rows * top, most, lean, False)
    places = jnp.arange(amount)

    def named(lengths, rotation):
        used = int((lengths > 0).sum())
        fixed = max(1, used // 4)
        moved = fixed + (places - fixed + rotation * (used - fixed)) % max(1, amount - fixed)
        return jnp.zeros((amount,), jnp.int32).at[sequence[jnp.where(places < fixed, places, moved)]].set(jnp.asarray(lengths, jnp.int32))

    lengths = jnp.where(number % 4 == 0, named(heavy_load, number // 4), named(ordinary, number - number // 4 - 1))
    mixed = jax.random.permutation(jax.random.fold_in(own, 3), amount)
    source_of, sink = mixed[0:amount // 2 * 2:2], mixed[1:amount // 2 * 2:2]
    slack = jnp.minimum(lengths[source_of] - 1, most - lengths[sink]) // 2
    slack = jnp.where((source_of == sequence[0]) | (sink == sequence[0]) | (lengths[sink] == 0), 0, jnp.maximum(slack, 0))
    moved = jax.random.randint(jax.random.fold_in(own, 4), (amount // 2,), 0, 1 << 20) % (slack + 1)
    lengths = lengths.at[source_of].add(-moved).at[sink].add(moved)
    members = jnp.searchsorted(jnp.cumsum(lengths), jnp.arange(rows * top), side="right").astype(jnp.int32)
    table = members.reshape(top, rows).T
    table = table[jax.random.permutation(jax.random.fold_in(own, 1), rows)]
    rotation = jax.random.randint(jax.random.fold_in(own, 2), (rows, 1), 0, top)
    return jnp.take_along_axis(table, (jnp.arange(top)[None, :] + rotation) % top, axis=1)


def load_shares(count, total, most, skew, full):
    loads = [(1 << 20) // math.isqrt(rank ** skew) + 1 for rank in range(1, count + 1)]
    largest = most if full else min(most, max(-(-total // count), total * loads[0] // sum(loads)))
    least = 1 if total - largest >= count - 1 else 0
    holding, spare = [largest] + [least] * (count - 1), total - largest - least * (count - 1)
    while spare > 0:
        candidates = [i for i in range(1, count) if holding[i] < largest] or [i for i in range(1, count) if holding[i] < most]
        mass, remaining = sum([loads[i] for i in candidates]), spare
        for i in candidates:
            addition = min(most - holding[i], max(1, remaining * loads[i] // mass), spare)
            holding[i] = holding[i] + addition
            spare = spare - addition
    return np.array(holding)


def noise(stream_key, extent, spread, limit, shards=(), kind=jnp.bfloat16):
    drawn = spread * jax.random.normal(stream_key, extent, jnp.float32)
    if shards:
        drawn = drawn * steps_of(stream_key, extent, shards, -0.22, 0.18)
    return jnp.clip(drawn, -limit, limit).astype(kind)


def setup_inputs(seed: int = 0) -> dict:
    streams_of = jax.random.split(jax.random.key(seed), 12)
    tokens = noise(streams_of[0], (SEQS, SEQLEN, D), 1.0, 6.0, ((0, 8), (1, 4)))
    route_keys = jax.random.split(jax.random.fold_in(streams_of[1], 1), SEQS * SEQLEN // TOK_DEV)
    route_turns = jax.random.permutation(jax.random.fold_in(streams_of[1], 3), SEQS * SEQLEN // TOK_DEV)
    route = jax.vmap(lambda own, number: routed_block(jax.random.fold_in(streams_of[1], 2), own, number, TOK_DEV, EXPERTS, 1, CAP, 1))(route_keys, route_turns).reshape((SEQS, SEQLEN, 1))
    w_inner = noise(streams_of[2], (EXPERTS, D, 2, DI), D ** -0.5, 0.125, ((0, 8), (3, 4)))
    w_state = noise(streams_of[3], (EXPERTS, D, 2 * NSTATE), (D * NSTATE) ** -0.5, 0.015625, ((0, 8),))
    w_step = noise(streams_of[4], (EXPERTS, D, HEADS), D ** -0.5, 0.125, ((0, 8), (2, 4)))
    step_bias = jnp.clip(-2.0 + 2.5 * jax.random.uniform(streams_of[5], (HEADS,), jnp.float32) ** steps_of(streams_of[5], (HEADS,), ((0, 4),), -0.2, 0.2), -2.0, 0.5)
    decay_log = jnp.clip(-7.0 + 4.5 * jax.random.uniform(streams_of[6], (HEADS,), jnp.float32) ** steps_of(streams_of[6], (HEADS,), ((0, 4),), -0.2, 0.2), -7.0, -2.5)
    skip_gain = jnp.clip(0.5 + 1.0 * jax.random.uniform(streams_of[7], (HEADS,), jnp.float32) ** steps_of(streams_of[7], (HEADS,), ((0, 4),), -0.2, 0.2), 0.5, 1.5)
    conv_weight = noise(streams_of[8], (CONV, DI), CONV ** -0.5, 3.0, ((1, 4),), jnp.float32)
    conv_bias = noise(streams_of[9], (DI,), 0.3, 1.5, ((0, 4),), jnp.float32)
    w_out = noise(streams_of[10], (EXPERTS, DI, D), DI ** -0.5, 0.09375, ((0, 8), (1, 4)))
    return {"tokens": tokens, "route": route, "w_inner": w_inner, "w_state": w_state, "w_step": w_step, "step_bias": step_bias, "decay_log": decay_log, "skip_gain": skip_gain, "conv_weight": conv_weight, "conv_bias": conv_bias, "w_out": w_out}


def block_ranks(ids_flat, experts, tok_rows):
    blocks = ids_flat.reshape(-1, tok_rows)
    onehot = (blocks[:, :, None] == jnp.arange(experts, dtype=jnp.int32)[None, None, :]).astype(jnp.int32)
    before = jnp.cumsum(onehot, axis=1) - 1
    return jnp.sum(onehot * before, axis=2).astype(jnp.int32)


def causal_conv(values, conv_weight, conv_bias):
    taps = conv_weight.shape[0]
    length = values.shape[0]
    padded = jnp.pad(values, ((taps - 1, 0), (0, 0)))
    total = conv_bias[None, :] + jnp.zeros_like(values)
    for shift in range(taps):
        total = total + conv_weight[shift][None, :] * padded[shift:shift + length]
    return total


def state_scan(signal_heads, steps, rates, in_vecs, out_vecs):
    length, heads, head_dim = signal_heads.shape
    nstate = in_vecs.shape[1]
    block = math.gcd(length, 128)
    count = length // block
    exact = lax.Precision.HIGHEST
    logs = steps * rates[None, :]
    pieces = (signal_heads.reshape(count, block, heads, head_dim), steps.reshape(count, block, heads),
              logs.reshape(count, block, heads), in_vecs.reshape(count, block, nstate),
              out_vecs.reshape(count, block, nstate))
    lower = jnp.arange(block)[:, None] >= jnp.arange(block)[None, :]

    def advance(state, piece):
        values, step_now, log_now, keys, queries = piece
        summed = jnp.cumsum(log_now, axis=0)
        gaps = summed[:, None, :] - summed[None, :, :]
        decay = jnp.exp(jnp.where(lower[:, :, None], gaps, -jnp.inf))
        scores = jnp.dot(queries, keys.T, precision=exact)
        weights = scores[:, :, None] * decay * step_now[None, :, :]
        local = jnp.einsum("tuh,uhp->thp", weights, values, precision=exact)
        carried = jnp.exp(summed)[:, :, None] * jnp.einsum("tn,hpn->thp", queries, state, precision=exact)
        tail = jnp.exp(summed[-1][None, :] - summed) * step_now
        state = jnp.exp(summed[-1])[:, None, None] * state + jnp.einsum("uh,uhp,un->hpn", tail, values, keys, precision=exact)
        return state, local + carried

    start = jnp.zeros((heads, head_dim, nstate), jnp.float32)
    final_state, outputs = lax.scan(advance, start, pieces)
    return outputs.reshape(length, heads, head_dim)


def mix_sequence(gate_inner, state_in_out, step_raw, conv_weight, conv_bias, step_bias, decay_log, skip_gain, head_dim):
    length = gate_inner.shape[0]
    gate_part = gate_inner[:, 0].astype(jnp.float32)
    inner_part = gate_inner[:, 1].astype(jnp.float32)
    signal = jax.nn.silu(causal_conv(inner_part, conv_weight, conv_bias))
    heads = step_raw.shape[1]
    steps = jax.nn.softplus(step_raw.astype(jnp.float32) + step_bias[None, :])
    rates = -jnp.exp(decay_log)
    nstate = state_in_out.shape[1] // 2
    in_vecs = state_in_out[:, :nstate].astype(jnp.float32)
    out_vecs = state_in_out[:, nstate:].astype(jnp.float32)
    signal_heads = signal.reshape(length, heads, head_dim)
    scanned = state_scan(signal_heads, steps, rates, in_vecs, out_vecs)
    scanned = scanned + skip_gain[None, :, None] * signal_heads
    return (scanned.reshape(length, heads * head_dim) * jax.nn.silu(gate_part)).astype(jnp.bfloat16)


def reference(tokens, route, w_inner, w_state, w_step, step_bias, decay_log, skip_gain, conv_weight, conv_bias, w_out):
    seqs, length, width = tokens.shape
    experts = w_inner.shape[0]
    inner = w_inner.shape[3]
    total = seqs * length
    ids = route.reshape(total).astype(jnp.int32)
    ranks = block_ranks(ids, experts, TOK_DEV).reshape(total)
    blocks_all = total // TOK_DEV
    block_of = jnp.arange(total, dtype=jnp.int32) // TOK_DEV
    slot = (ids * blocks_all + block_of) * CAP + ranks
    table = jnp.full((experts * blocks_all * CAP,), total, jnp.int32).at[slot].set(jnp.arange(total, dtype=jnp.int32))
    table = table.reshape(experts, blocks_all * CAP)
    flat = tokens.reshape(total, width)
    nboth = w_state.shape[2]
    heads = w_step.shape[2]

    def project(carry, item):
        rows_index, weight_inner, weight_state, weight_step = item
        rows = jnp.take(flat, rows_index, axis=0, mode="fill", fill_value=0)
        gate_inner = jnp.dot(rows, weight_inner.reshape(width, 2 * inner), preferred_element_type=jnp.float32).astype(jnp.bfloat16)
        state_part = jnp.dot(rows, weight_state, preferred_element_type=jnp.float32).astype(jnp.bfloat16)
        step_part = jnp.dot(rows, weight_step, preferred_element_type=jnp.float32).astype(jnp.bfloat16)
        return (carry[0].at[rows_index].set(gate_inner, mode="drop"),
                carry[1].at[rows_index].set(state_part, mode="drop"),
                carry[2].at[rows_index].set(step_part, mode="drop")), None

    start = (jnp.zeros((total, 2 * inner), jnp.bfloat16), jnp.zeros((total, nboth), jnp.bfloat16), jnp.zeros((total, heads), jnp.bfloat16))
    projected, unused = lax.scan(project, start, (table, w_inner, w_state, w_step))
    gate_all = projected[0].reshape(seqs, length, 2, inner)
    state_all = projected[1].reshape(seqs, length, nboth)
    step_all = projected[2].reshape(seqs, length, heads)

    def one_sequence(parts):
        return mix_sequence(parts[0], parts[1], parts[2], conv_weight, conv_bias, step_bias, decay_log, skip_gain, HEAD_DIM)

    gated = lax.map(one_sequence, (gate_all, state_all, step_all)).reshape(total, inner)
    group = inner // N_CONTEXT

    def output_rows(carry, item):
        rows_index, weight_out = item
        rows = jnp.take(gated, rows_index, axis=0, mode="fill", fill_value=0)
        summed = jnp.zeros((rows.shape[0], width), jnp.float32)
        for shard in range(N_CONTEXT):
            part = jnp.dot(rows[:, shard * group:(shard + 1) * group], weight_out[shard * group:(shard + 1) * group], preferred_element_type=jnp.float32).astype(jnp.bfloat16)
            summed = summed + lax.optimization_barrier(part).astype(jnp.float32)
        return carry.at[rows_index].set(summed.astype(jnp.bfloat16), mode="drop"), None

    result, unused_two = lax.scan(output_rows, jnp.zeros((total, width), jnp.bfloat16), (table, w_out))
    return result.reshape(seqs, length, width)
```

```python
import functools

import jax
import jax.numpy as jnp
from jax import lax
from jax.experimental import pallas as pl
from jax.experimental.pallas import tpu as pltpu
from jax.sharding import PartitionSpec as P

HEAD_DIM = 64
LANES = 128
BF16 = jnp.bfloat16
F32 = jnp.float32


def iota(shape, axis):
    return lax.broadcasted_iota(jnp.int32, shape, axis)


def dot(a, b):
    return jnp.dot(a, b, preferred_element_type=F32)


def flat_rows(pieces):
    count, rows, lanes = pieces.shape
    if rows % 16:
        return pieces.astype(F32).reshape(count * rows, lanes).astype(BF16)
    return pieces.reshape(count * rows, lanes)


def slot_rows(ids, experts, cap):
    tok_rows = ids.shape[1]
    onehot = jnp.where(iota((experts, tok_rows), 0) == ids, 1.0, 0.0)
    upto = jnp.where(iota((tok_rows, tok_rows), 0) <= iota((tok_rows, tok_rows), 1), 1.0, 0.0)
    before = dot(onehot.astype(BF16), upto.astype(BF16))
    rank = jnp.sum(onehot * before, axis=0, keepdims=True) - 1.0
    slot = ids * cap + rank.astype(jnp.int32)
    return jnp.where(iota((experts * cap, tok_rows), 0) == slot, 1.0, 0.0)


VMEM = pl.BlockSpec(memory_space=pltpu.VMEM)
SMEM = pl.BlockSpec(memory_space=pltpu.SMEM)
ANY = pl.BlockSpec(memory_space=pl.ANY)


def call(kernel, inputs, outputs, after=(), scratch=(), flops=0, exps=0):
    moved = sum(2 * a.size for a in inputs[1:]) + sum(2 * o.size for o in outputs)
    count = len(inputs)

    def body(*refs):
        kernel(*refs[:count], *refs[count + len(after) :])

    return pl.pallas_call(
        body,
        out_shape=outputs,
        in_specs=[SMEM] + [VMEM] * (count - 1) + [ANY] * len(after),
        out_specs=[VMEM] * len(outputs),
        scratch_shapes=list(scratch),
        compiler_params=pltpu.CompilerParams(vmem_limit_bytes=24 << 20),
        cost_estimate=pl.CostEstimate(flops=flops, bytes_accessed=moved, transcendentals=exps),
    )(*inputs, *after)


def shape(*dims):
    return jax.ShapeDtypeStruct(dims, BF16)


def tie(value, *after):
    return pl.pallas_call(
        lambda *refs: None,
        out_shape=jax.ShapeDtypeStruct(value.shape, value.dtype),
        in_specs=[ANY] * (1 + len(after)),
        out_specs=ANY,
        input_output_aliases={0: 0},
    )(value, *after)


def dispatch_kernel(experts, cap, info_ref, ids_ref, tokens_ref, out_ref):
    place = slot_rows(ids_ref[info_ref[0]], experts, cap).astype(BF16)
    out_ref[...] = dot(place, tokens_ref[...]).astype(BF16)


def collect_kernel(experts, cap, info_ref, ids_ref, rows_ref, out_ref):
    place = slot_rows(ids_ref[info_ref[0]], experts, cap).T.astype(BF16)
    out_ref[...] = dot(place, rows_ref[...]).astype(BF16)


def side_kernel(experts, cap, chans, info_ref, ids_ref, near_ref, out_ref):
    place = slot_rows(ids_ref[info_ref[0]], experts, cap).T.astype(BF16)
    for i in range(2):
        rows = flat_rows(near_ref[:, i, :, chans:])
        out_ref[:, i * LANES : (i + 1) * LANES] = dot(place, rows).astype(BF16)


def sum_kernel(info_ref, *refs):
    total = refs[0][...].astype(F32)
    for ref in refs[1:-1]:
        total = total + ref[...].astype(F32)
    refs[-1][...] = total.astype(BF16)


def project_kernel(places, experts, cap, chans, info_ref, *refs):
    rows, weight, out_ref = refs[:places], refs[places], refs[-1]
    tile = 256
    for lo in range(0, chans, tile):
        for at in range(places):
            made = dot(rows[at][...], weight[:, chans + lo : chans + lo + tile]).astype(BF16)
            for e in range(experts):
                out_ref[e, at, :, lo : lo + tile] = made[e * cap : (e + 1) * cap, :]
    if len(refs) > places + 2:
        made = dot(rows[0][...], refs[places + 1][...]).astype(BF16)
        for at in range(2):
            for e in range(experts):
                out_ref[e, at, :, chans:] = made[
                    e * cap : (e + 1) * cap, at * LANES : (at + 1) * LANES
                ]


def gate_kernel(places, chans, info_ref, *refs):
    rows, weight, outs = refs[:places], refs[places], refs[-places:]
    tile = 256
    for lo in range(0, chans, tile):
        for at in range(places):
            outs[at][:, lo : lo + tile] = dot(rows[at][...], weight[:, lo : lo + tile]).astype(BF16)


def output_kernel(places, first, info_ref, scanned_ref, *refs):
    gates, weight, outs = refs[:places], refs[places], refs[-places:]
    width = weight.shape[1]
    for at in range(places):
        scanned = flat_rows(scanned_ref[:, first + at])
        gate = jax.nn.silu(gates[at][...].astype(F32))
        gated = (scanned.astype(F32) * gate).astype(BF16)
        tile = 512
        for lo in range(0, width, tile):
            outs[at][:, lo : lo + tile] = dot(gated, weight[:, lo : lo + tile]).astype(BF16)


def scan_kernel(
    cfg,
    info_ref,
    ids_ref,
    side_ref,
    head_ref,
    chan_ref,
    near_ref,
    far_ref,
    out_near_ref,
    out_far_ref,
    rows_ref,
    state_ref,
    last_ref,
):
    blocks = ids_ref.shape[0]
    state_ref[...] = jnp.zeros_like(state_ref)
    last_ref[...] = jnp.zeros_like(last_ref)
    block = functools.partial(
        scan_block, cfg, info_ref, ids_ref, side_ref, head_ref, chan_ref, near_ref, far_ref,
        out_near_ref, out_far_ref, rows_ref, state_ref, last_ref,
    )
    pl.loop(0, blocks)(block)


def scan_block(
    cfg,
    info_ref,
    ids_ref,
    side_ref,
    head_ref,
    chan_ref,
    near_ref,
    far_ref,
    out_near_ref,
    out_far_ref,
    rows_ref,
    state_ref,
    last_ref,
    b,
):
    experts, cap, tok_rows, nstate, chn, heads = cfg
    q = info_ref[1 + b]

    def load(ref, at):
        for e in range(experts):
            rows_ref[e * cap : (e + 1) * cap, :] = ref[e, at, :, :chn].astype(rows_ref.dtype)

    @pl.when(q < 2)
    def _():
        load(near_ref, q)

    @pl.when(q >= 2)
    def _():
        load(far_ref, q - 2)

    place_t = slot_rows(ids_ref[b], experts, cap)
    place = place_t.T.astype(BF16)
    place_t = place_t.astype(BF16)

    inner = dot(place, rows_ref[...].astype(BF16))
    both = side_ref[q, :, :LANES]
    own_head = iota((LANES, LANES), 0) == iota((LANES, LANES), 1) + info_ref[1 + ids_ref.shape[0] + b] * heads
    own_head = jnp.where(own_head & (iota((LANES, LANES), 1) < heads), 1.0, 0.0)
    raw = dot(side_ref[q, :, LANES:], own_head.astype(BF16))

    taps = 4
    padded = jnp.concatenate([last_ref[...], inner], axis=0)
    total = chan_ref[taps : taps + 1, :]
    for j in range(taps):
        start = 8 - (taps - 1) + j
        total = total + chan_ref[j : j + 1, :] * padded[start : start + tok_rows, :]
    last_ref[...] = inner[tok_rows - 8 :, :]
    signal = jax.nn.silu(total)

    step = jax.nn.softplus(raw + head_ref[0:1, :])
    logs = step * head_ref[1:2, :]
    lower = iota((tok_rows, tok_rows), 0) >= iota((tok_rows, tok_rows), 1)
    summed = jnp.dot(
        jnp.where(lower, 1.0, 0.0),
        logs,
        preferred_element_type=F32,
        precision=lax.Precision.HIGHEST,
    )
    summed_t = summed.T
    tail = jnp.exp(summed[tok_rows - 1 :, :] - summed) * step

    spread = jnp.where(
        iota((LANES, chn), 0) == iota((LANES, chn), 1) // HEAD_DIM, 1.0, 0.0
    ).astype(BF16)
    spread = jnp.concatenate([spread, spread], axis=0)

    def widen(values):
        high = values.astype(BF16)
        low = (values - high.astype(F32)).astype(BF16)
        return dot(jnp.concatenate([high, low], axis=1), spread)

    step_wide = widen(step)
    kept_wide = widen(jnp.exp(summed))
    tail_wide = widen(tail)

    both_t = both.astype(F32).T.astype(BF16)
    keys_t = both_t[:nstate, :]
    queries = both[:, nstate:]
    scores = dot(queries, keys_t)

    state = state_ref[...]
    carried = dot(queries, state.astype(BF16)) * kept_wide
    rest = carried + chan_ref[taps + 1 : taps + 2, :] * signal
    scaled = (signal * step_wide).astype(BF16)
    state_ref[...] = kept_wide[tok_rows - 1 :, :] * state + dot(
        keys_t, (signal * tail_wide).astype(BF16)
    )

    first = iota((tok_rows, LANES), 1) < HEAD_DIM
    made = []
    for pair in range(heads // 2):
        values = scaled[:, pair * LANES : (pair + 1) * LANES]
        two = []
        for h in (2 * pair, 2 * pair + 1):
            gaps = summed[:, h : h + 1] - summed_t[h : h + 1, :]
            decay = jnp.exp(jnp.where(lower, gaps, -jnp.inf))
            two.append(dot((scores * decay).astype(BF16), values))
        made.append(jnp.where(first, two[0], two[1]))
    scanned = (rest + jnp.concatenate(made, axis=1)).astype(BF16)
    leaving = dot(place_t, scanned).astype(BF16)

    def store(ref, at):
        for e in range(experts):
            ref[e, at] = leaving[e * cap : (e + 1) * cap, :]

    @pl.when(q < 2)
    def _():
        store(out_near_ref, q)

    @pl.when(q >= 2)
    def _():
        store(out_far_ref, q - 2)


def per_device(
    tokens,
    route,
    w_inner,
    w_state,
    w_step,
    step_bias,
    decay_log,
    skip_gain,
    conv_weight,
    conv_bias,
    w_out,
):
    tok_rows, width = tokens.shape[1], tokens.shape[2]
    experts = lax.axis_size("expert")
    shards = lax.axis_size("context")
    cap = 2 * tok_rows // experts
    slots = experts * cap
    chans = w_inner.shape[3]
    heads = w_step.shape[2]
    nstate = w_state.shape[2] // 2
    chips = shards // 2
    far_count = shards - 2

    here = lax.axis_index("context").astype(jnp.int32)
    blocks = jnp.arange(shards, dtype=jnp.int32)
    order = 2 * ((here // 2 - blocks // 2) % chips) + ((here % 2) ^ (blocks % 2))
    groups = 2 * ((blocks // 2 - here // 2) % chips) + ((here % 2) ^ (blocks % 2))
    info = jnp.concatenate([here[None], order, groups])
    ids = route.reshape(shards, 1, tok_rows)
    swap = [(c, c ^ 1) for c in range(shards)]

    def hop(k):
        return [(c, ((c // 2 + k) % chips) * 2 + c % 2) for c in range(shards)]

    def permute(value, pairs):
        return lax.ppermute(value, "context", pairs)

    def spread(value):
        made = [value, permute(value, swap)]
        for k in range(1, chips):
            arrived = permute(value, hop(k))
            made += [arrived, permute(arrived, swap)]
        return made

    def exchange(value):
        return lax.all_to_all(value, "expert", split_axis=0, concat_axis=0, tiled=True)

    w_flat = w_inner[0].reshape(width, 2 * chans)
    steps_t = jnp.concatenate(spread(tie(w_step[0].T, w_flat)))
    all_heads = shards * heads
    w_side = jnp.concatenate(
        [w_state[0], jnp.pad(steps_t, ((0, LANES - all_heads), (0, 0))).T], axis=1
    )

    outgoing = call(
        functools.partial(dispatch_kernel, experts, cap),
        [info, ids, tokens[0]],
        [shape(slots, width)],
        flops=2 * slots * tok_rows * width,
    )[0]
    own = exchange(outgoing.reshape(experts, cap, width)).reshape(slots, width)
    own = tie(own, w_flat, w_side)
    swapped = permute(own, swap)
    near = call(
        functools.partial(project_kernel, 2, experts, cap, chans),
        [info, own, swapped, w_flat, w_side],
        [shape(experts, 2, cap, chans + LANES)],
        flops=4 * slots * width * (chans + LANES),
    )[0]
    distant = []
    for k in range(1, chips):
        arrived = permute(own, hop(k))
        distant += [arrived, permute(tie(arrived, near), swap)]
    far = call(
        functools.partial(project_kernel, far_count, experts, cap, chans),
        [info, *distant, w_flat],
        [shape(experts, far_count, cap, chans)],
        flops=2 * far_count * slots * width * chans,
    )[0]
    near_back = exchange(near)
    far_back = exchange(far)

    side = call(
        functools.partial(side_kernel, experts, cap, chans),
        [info, ids, near_back],
        [shape(tok_rows, 2 * LANES)],
        after=[far],
        flops=2 * slots * tok_rows * 2 * LANES,
    )[0]
    sides = jnp.stack(spread(side))

    def padded_heads(row):
        return jnp.pad(row, (0, LANES - heads))[None, :]

    head_rows = jnp.concatenate(
        [padded_heads(step_bias), padded_heads(-jnp.exp(decay_log)), jnp.zeros((6, LANES), F32)]
    )
    chan_rows = jnp.concatenate(
        [conv_weight, conv_bias[None, :], jnp.repeat(skip_gain, HEAD_DIM)[None, :]]
    )
    chan_rows = jnp.pad(chan_rows, ((0, 2), (0, 0)))
    def gates(rows):
        return call(
            functools.partial(gate_kernel, len(rows), chans),
            [info, *rows, w_flat],
            [shape(slots, chans)] * len(rows),
            after=[far],
            flops=2 * len(rows) * slots * width * chans,
        )

    gate_far = gates(distant)
    gate_near = gates([own, swapped])
    cfg = (experts, cap, tok_rows, nstate, chans, heads)
    near_out, far_out = call(
        functools.partial(scan_kernel, cfg),
        [info, ids, sides, head_rows, chan_rows, near_back, far_back],
        [shape(experts, 2, cap, chans), shape(experts, far_count, cap, chans)],
        after=[gate_far[0], gate_near[0]],
        scratch=[
            pltpu.VMEM((slots, chans), BF16 if cap % 16 == 0 else F32),
            pltpu.VMEM((nstate, chans), F32),
            pltpu.VMEM((8, chans), F32),
        ],
        flops=2 * shards * tok_rows * chans * (2 * slots + 2 * nstate + 2 * tok_rows + 768),
        exps=shards * tok_rows * tok_rows * heads,
    )
    far_ret = exchange(far_out)
    near_ret = exchange(near_out)

    def outputs(scanned, gate, first, after=()):
        return call(
            functools.partial(output_kernel, len(gate), first),
            [info, scanned, *gate, w_out[0]],
            [shape(slots, width)] * len(gate),
            after=after,
            flops=2 * len(gate) * slots * width * chans,
        )

    parts_far = outputs(far_ret, gate_far, 0)
    pairs = []
    for k in range(1, chips):
        mine, other = parts_far[2 * k - 2], parts_far[2 * k - 1]
        pairs.append((mine.astype(F32) + permute(other, swap).astype(F32)).astype(BF16))
    hopped = [permute(pair, hop(chips - k)) for k, pair in enumerate(pairs, 1)]
    part_swap = outputs(near_ret, gate_near[1:], 1)[0]
    part_own = outputs(near_ret, gate_near[:1], 0, hopped)[0]
    summed = call(
        sum_kernel, [info, part_own, permute(part_swap, swap), *hopped], [shape(slots, width)]
    )[0]
    returned = exchange(summed.reshape(experts, cap, width)).reshape(slots, width)
    result = call(
        functools.partial(collect_kernel, experts, cap),
        [info, ids, returned],
        [shape(tok_rows, width)],
        flops=2 * slots * tok_rows * width,
    )[0]
    return result[None]


def solution(mesh):
    in_specs = (
        P("expert", "context", None),
        P("expert", None, None),
        P("expert", None, None, "context"),
        P("expert", None, None),
        P("expert", None, "context"),
        P("context"),
        P("context"),
        P("context"),
        P(None, "context"),
        P("context"),
        P("expert", "context", None),
    )
    out_specs = P("expert", "context", None)
    return jax.shard_map(
        per_device, mesh=mesh, in_specs=in_specs, out_specs=out_specs, check_vma=False
    )
```

```python
import functools

import jax
import jax.numpy as jnp
from jax import lax
from jax.experimental import pallas as pl
from jax.experimental.pallas import tpu as pltpu
from jax.sharding import PartitionSpec as P

HEAD_DIM = 64
LANES = 128
BF16 = jnp.bfloat16
F32 = jnp.float32


def iota(shape, axis):
    return lax.broadcasted_iota(jnp.int32, shape, axis)


def dot(a, b):
    return jnp.dot(a, b, preferred_element_type=F32)


def flat_rows(pieces):
    count, rows, lanes = pieces.shape
    if rows % 16:
        return pieces.astype(F32).reshape(count * rows, lanes).astype(BF16)
    return pieces.reshape(count * rows, lanes)


def slot_rows(ids, experts, cap):
    tok_rows = ids.shape[1]
    onehot = jnp.where(iota((experts, tok_rows), 0) == ids, 1.0, 0.0)
    upto = jnp.where(iota((tok_rows, tok_rows), 0) <= iota((tok_rows, tok_rows), 1), 1.0, 0.0)
    before = dot(onehot.astype(BF16), upto.astype(BF16))
    rank = jnp.sum(onehot * before, axis=0, keepdims=True) - 1.0
    slot = ids * cap + rank.astype(jnp.int32)
    return jnp.where(iota((experts * cap, tok_rows), 0) == slot, 1.0, 0.0)


VMEM = pl.BlockSpec(memory_space=pltpu.VMEM)
SMEM = pl.BlockSpec(memory_space=pltpu.SMEM)
ANY = pl.BlockSpec(memory_space=pl.ANY)


def call(kernel, inputs, outputs, streamed=(), after=(), scratch=(), flops=0, exps=0):
    moved = sum(2 * a.size for a in (*streamed, *inputs[1:])) + sum(2 * o.size for o in outputs)
    count = len(streamed) + len(inputs)

    def body(*refs):
        kernel(*refs[:count], *refs[count + len(after) :])

    return pl.pallas_call(
        body,
        out_shape=outputs,
        in_specs=[ANY] * len(streamed) + [SMEM] + [VMEM] * (len(inputs) - 1) + [ANY] * len(after),
        out_specs=[VMEM] * len(outputs),
        scratch_shapes=list(scratch),
        compiler_params=pltpu.CompilerParams(vmem_limit_bytes=24 << 20),
        cost_estimate=pl.CostEstimate(flops=flops, bytes_accessed=moved, transcendentals=exps),
    )(*streamed, *inputs, *after)


def tiles_of(source, held, sems, first, tile):
    count = held.shape[1] // tile
    copies = [
        pltpu.make_async_copy(
            source.at[:, pl.ds(first + t * tile, tile)], held.at[:, pl.ds(t * tile, tile)], sems.at[t]
        )
        for t in range(count)
    ]
    for copy in copies:
        copy.start()

    def tile_at(t):
        copies[t].wait()
        return held[:, t * tile : (t + 1) * tile]

    return tile_at


def held_weight(rows, columns, tile):
    return [pltpu.VMEM((rows, columns), BF16), pltpu.SemaphoreType.DMA((columns // tile,))]


def shape(*dims):
    return jax.ShapeDtypeStruct(dims, BF16)


def tie(value, *after):
    return pl.pallas_call(
        lambda *refs: None,
        out_shape=jax.ShapeDtypeStruct(value.shape, value.dtype),
        in_specs=[ANY] * (1 + len(after)),
        out_specs=ANY,
        input_output_aliases={0: 0},
    )(value, *after)


def dispatch_kernel(experts, cap, info_ref, ids_ref, tokens_ref, out_ref):
    place = slot_rows(ids_ref[info_ref[0]], experts, cap).astype(BF16)
    out_ref[...] = dot(place, tokens_ref[...]).astype(BF16)


def collect_kernel(experts, cap, info_ref, ids_ref, rows_ref, out_ref):
    place = slot_rows(ids_ref[info_ref[0]], experts, cap).T.astype(BF16)
    out_ref[...] = dot(place, rows_ref[...]).astype(BF16)


def side_kernel(experts, cap, chans, info_ref, ids_ref, near_ref, out_ref):
    place = slot_rows(ids_ref[info_ref[0]], experts, cap).T.astype(BF16)
    for i in range(2):
        rows = flat_rows(near_ref[:, i, :, chans:])
        out_ref[:, i * LANES : (i + 1) * LANES] = dot(place, rows).astype(BF16)


def sum_kernel(info_ref, *refs):
    total = refs[0][...].astype(F32)
    for ref in refs[1:-1]:
        total = total + ref[...].astype(F32)
    refs[-1][...] = total.astype(BF16)


def project_kernel(places, experts, cap, chans, weight_ref, info_ref, *refs):
    rows, sides, (out_ref, held, sems) = refs[:places], refs[places:-3], refs[-3:]
    tile = 256
    tile_at = tiles_of(weight_ref, held, sems, chans, tile)

    def store(at, lo, made):
        made = made.astype(BF16)
        for e in range(experts):
            out_ref[e, at, :, lo : lo + made.shape[1]] = made[e * cap : (e + 1) * cap, :]

    if sides:
        store(0, chans, dot(rows[0][...], sides[0][...]))
        steps = [ref[...].astype(F32) for ref in sides[1:]]
        spare = LANES - sum(part.shape[0] for part in steps)
        steps.append(jnp.zeros((spare, steps[0].shape[1]), F32))
        steps = jnp.concatenate(steps, axis=0).astype(BF16)
        made = lax.dot_general(
            rows[0][...], steps, (((1,), (1,)), ((), ())), preferred_element_type=F32
        )
        store(1, chans, made)
    for t in range(chans // tile):
        weight = tile_at(t)
        for at in range(places):
            store(at, t * tile, dot(rows[at][...], weight))


def gate_kernel(places, chans, weight_ref, info_ref, *refs):
    rows, outs, (held, sems) = refs[:places], refs[places:-2], refs[-2:]
    tile = 256
    tile_at = tiles_of(weight_ref, held, sems, 0, tile)
    for t in range(chans // tile):
        weight = tile_at(t)
        for at in range(places):
            outs[at][:, t * tile : (t + 1) * tile] = dot(rows[at][...], weight).astype(BF16)


def output_kernel(places, weight_ref, info_ref, scanned_ref, *refs):
    count = len(places)
    gates, outs, (held, sems) = refs[:count], refs[count:-2], refs[-2:]
    tile = 512
    tile_at = tiles_of(weight_ref, held, sems, 0, tile)
    gated = []
    for gate_ref, at in zip(gates, places):
        scanned = flat_rows(scanned_ref[:, at]).astype(F32)
        gated.append((scanned * jax.nn.silu(gate_ref[...].astype(F32))).astype(BF16))
    for t in range(held.shape[1] // tile):
        weight = tile_at(t)
        for rows, out in zip(gated, outs):
            out[:, t * tile : (t + 1) * tile] = dot(rows, weight).astype(BF16)


def scan_kernel(
    cfg,
    info_ref,
    ids_ref,
    side_ref,
    head_ref,
    chan_ref,
    near_ref,
    far_ref,
    out_near_ref,
    out_far_ref,
    inner_ref,
    made_ref,
):
    experts, cap, tok_rows, nstate, chn, heads = cfg
    blocks = ids_ref.shape[0]
    taps = 4
    inner_ref[:8, :] = jnp.zeros((8, chn), F32)

    for q in range(blocks):
        b = info_ref[1 + q]
        place = slot_rows(ids_ref[b], experts, cap).T.astype(BF16)
        rows = flat_rows(near_ref[:, q, :, :chn] if q < 2 else far_ref[:, q - 2])
        inner_ref[pl.ds(8 + b * tok_rows, tok_rows), :] = dot(place, rows)

    lower = iota((tok_rows, tok_rows), 0) >= iota((tok_rows, tok_rows), 1)
    ones = jnp.where(lower, 1.0, 0.0)
    first = iota((tok_rows, LANES), 1) < HEAD_DIM
    spread = jnp.where(
        iota((2 * LANES, chn), 0) % LANES == iota((2 * LANES, chn), 1) // HEAD_DIM, 1.0, 0.0
    ).astype(BF16)

    def widen(values):
        high = values.astype(BF16)
        low = (values - high.astype(F32)).astype(BF16)
        return dot(jnp.concatenate([high, low], axis=1), spread)

    state = jnp.zeros((nstate, chn), F32)
    for b in range(blocks):
        q = info_ref[1 + blocks + b]
        total = chan_ref[taps : taps + 1, :]
        for j in range(taps):
            start = 8 + b * tok_rows - (taps - 1) + j
            total = total + chan_ref[j : j + 1, :] * inner_ref[start : start + tok_rows, :]
        signal = jax.nn.silu(total)

        own_head = iota((LANES, LANES), 0) == iota((LANES, LANES), 1) + info_ref[
            1 + 2 * blocks + b
        ] * heads
        own_head = jnp.where(own_head & (iota((LANES, LANES), 1) < heads), 1.0, 0.0)
        raw = dot(side_ref[q, :, LANES:], own_head.astype(BF16))
        step = jax.nn.softplus(raw + head_ref[0:1, :])
        summed = jnp.dot(
            ones,
            step * head_ref[1:2, :],
            preferred_element_type=F32,
            precision=lax.Precision.HIGHEST,
        )
        source = summed - jnp.log(step)
        source_t = source.T
        kept = widen(jnp.exp(summed))
        tail = widen(jnp.exp(summed[tok_rows - 1 :, :] - source))

        both = side_ref[q, :, :LANES]
        keys_t = both.astype(F32).T.astype(BF16)[:nstate, :]
        queries = both[:, nstate:]
        scores = dot(queries, keys_t)
        rest = chan_ref[taps + 1 : taps + 2, :] * signal
        if b > 0:
            rest = rest + dot(queries, state.astype(BF16)) * kept
        if b < blocks - 1:
            state = kept[tok_rows - 1 :, :] * state + dot(keys_t, (signal * tail).astype(BF16))

        for pair in range(heads // 2):
            lanes = slice(pair * LANES, (pair + 1) * LANES)
            values = signal[:, lanes]
            values = jnp.concatenate(
                [jnp.where(first, values, 0.0), jnp.where(first, 0.0, values)], axis=0
            ).astype(BF16)
            weights = []
            for h in (2 * pair, 2 * pair + 1):
                gaps = summed[:, h : h + 1] - source_t[h : h + 1, :]
                decay = jnp.exp(jnp.where(lower, gaps, -jnp.inf))
                weights.append((scores * decay).astype(BF16))
            local = dot(jnp.concatenate(weights, axis=1), values)
            made_ref[b * tok_rows : (b + 1) * tok_rows, lanes] = (rest[:, lanes] + local).astype(BF16)

    for q in range(blocks):
        b = info_ref[1 + q]
        place = slot_rows(ids_ref[b], experts, cap).astype(BF16)
        start = pl.multiple_of(b * tok_rows, tok_rows)
        leaving = dot(place, made_ref[pl.ds(start, tok_rows), :]).astype(BF16)
        for e in range(experts):
            piece = leaving[e * cap : (e + 1) * cap, :]
            if q < 2:
                out_near_ref[e, q] = piece
            else:
                out_far_ref[e, q - 2] = piece


def per_device(
    tokens,
    route,
    w_inner,
    w_state,
    w_step,
    step_bias,
    decay_log,
    skip_gain,
    conv_weight,
    conv_bias,
    w_out,
):
    tok_rows, width = tokens.shape[1], tokens.shape[2]
    experts = lax.axis_size("expert")
    shards = lax.axis_size("context")
    cap = 2 * tok_rows // experts
    slots = experts * cap
    chans = w_inner.shape[3]
    heads = w_step.shape[2]
    nstate = w_state.shape[2] // 2
    chips = shards // 2
    far_count = shards - 2

    here = lax.axis_index("context").astype(jnp.int32)
    blocks = jnp.arange(shards, dtype=jnp.int32)
    order = 2 * ((here // 2 - blocks // 2) % chips) + ((here % 2) ^ (blocks % 2))
    groups = 2 * ((blocks // 2 - here // 2) % chips) + ((here % 2) ^ (blocks % 2))
    block_at = 2 * ((here // 2 - blocks // 2) % chips) + ((here % 2) ^ (blocks % 2))
    info = jnp.concatenate([here[None], block_at, order, groups])
    ids = route.reshape(shards, 1, tok_rows)
    swap = [(c, c ^ 1) for c in range(shards)]

    def hop(k):
        return [(c, ((c // 2 + k) % chips) * 2 + c % 2) for c in range(shards)]

    def permute(value, pairs):
        return lax.ppermute(value, "context", pairs)

    def spread(value):
        made = [value, permute(value, swap)]
        for k in range(1, chips):
            arrived = permute(value, hop(k))
            made += [arrived, permute(arrived, swap)]
        return made

    def exchange(value):
        return lax.all_to_all(value, "expert", split_axis=0, concat_axis=0, tiled=True)

    w_flat = w_inner[0].reshape(width, 2 * chans)

    outgoing = call(
        functools.partial(dispatch_kernel, experts, cap),
        [info, ids, tokens[0]],
        [shape(slots, width)],
        flops=2 * slots * tok_rows * width,
    )[0]
    own = exchange(outgoing.reshape(experts, cap, width)).reshape(slots, width)
    steps = spread(tie(w_step[0].T, outgoing))
    own = tie(own, w_flat, *steps)
    swapped = permute(own, swap)
    near = call(
        functools.partial(project_kernel, 2, experts, cap, chans),
        [info, own, swapped, w_state[0], *steps],
        [shape(experts, 2, cap, chans + LANES)],
        streamed=[w_flat],
        scratch=held_weight(width, chans, 256),
        flops=4 * slots * width * (chans + LANES),
    )[0]
    distant = []
    for k in range(1, chips):
        arrived = permute(own, hop(k))
        distant += [arrived, permute(tie(arrived, near), swap)]
    far = call(
        functools.partial(project_kernel, far_count, experts, cap, chans),
        [info, *distant],
        [shape(experts, far_count, cap, chans)],
        streamed=[w_flat],
        scratch=held_weight(width, chans, 256),
        flops=2 * far_count * slots * width * chans,
    )[0]
    near_back = exchange(near)
    far_back = exchange(far)

    side = call(
        functools.partial(side_kernel, experts, cap, chans),
        [info, ids, near_back],
        [shape(tok_rows, 2 * LANES)],
        after=[far],
        flops=2 * slots * tok_rows * 2 * LANES,
    )[0]
    sides = jnp.stack(spread(side))

    def padded_heads(row):
        return jnp.pad(row, (0, LANES - heads))[None, :]

    head_rows = jnp.concatenate(
        [padded_heads(step_bias), padded_heads(-jnp.exp(decay_log)), jnp.zeros((6, LANES), F32)]
    )
    chan_rows = jnp.concatenate(
        [conv_weight, conv_bias[None, :], jnp.repeat(skip_gain, HEAD_DIM)[None, :]]
    )
    chan_rows = jnp.pad(chan_rows, ((0, 2), (0, 0)))
    def gates(rows):
        return call(
            functools.partial(gate_kernel, len(rows), chans),
            [info, *rows],
            [shape(slots, chans)] * len(rows),
            streamed=[w_flat],
            scratch=held_weight(width, chans, 256),
            after=[far],
            flops=2 * len(rows) * slots * width * chans,
        )

    gate_far = gates(distant)
    gate_near = gates([own, swapped])
    cfg = (experts, cap, tok_rows, nstate, chans, heads)
    near_out, far_out = call(
        functools.partial(scan_kernel, cfg),
        [info, ids, sides, head_rows, chan_rows, near_back, far_back],
        [shape(experts, 2, cap, chans), shape(experts, far_count, cap, chans)],
        after=[gate_far[0], gate_near[0]],
        scratch=[
            pltpu.VMEM((8 + shards * tok_rows, chans), F32),
            pltpu.VMEM((shards * tok_rows, chans), BF16),
        ],
        flops=2 * shards * tok_rows * chans * (2 * slots + 2 * nstate + 2 * tok_rows + 768),
        exps=shards * tok_rows * tok_rows * heads,
    )
    far_ret = exchange(far_out)
    near_ret = exchange(near_out)

    def outputs(scanned, gate, places, after=()):
        return call(
            functools.partial(output_kernel, places),
            [info, scanned, *(gate[at] for at in places)],
            [shape(slots, width)] * len(places),
            streamed=[w_out[0]],
            after=after,
            scratch=held_weight(chans, width, 512),
            flops=2 * len(places) * slots * width * chans,
        )

    parts_other = outputs(far_ret, gate_far, range(1, far_count, 2))
    parts_other = [permute(part, swap) for part in parts_other]
    parts_mine = outputs(far_ret, gate_far, range(0, far_count, 2))
    hopped = []
    for k in range(1, chips):
        pair = parts_mine[k - 1].astype(F32) + parts_other[k - 1].astype(F32)
        hopped.append(permute(pair.astype(BF16), hop(chips - k)))
    part_swap = outputs(near_ret, gate_near, [1])[0]
    part_own = outputs(near_ret, gate_near, [0], hopped)[0]
    summed = call(
        sum_kernel, [info, part_own, permute(part_swap, swap), *hopped], [shape(slots, width)]
    )[0]
    returned = exchange(summed.reshape(experts, cap, width)).reshape(slots, width)
    result = call(
        functools.partial(collect_kernel, experts, cap),
        [info, ids, returned],
        [shape(tok_rows, width)],
        flops=2 * slots * tok_rows * width,
    )[0]
    return result[None]


def solution(mesh):
    in_specs = (
        P("expert", "context", None),
        P("expert", None, None),
        P("expert", None, None, "context"),
        P("expert", None, None),
        P("expert", None, "context"),
        P("context"),
        P("context"),
        P("context"),
        P(None, "context"),
        P("context"),
        P("expert", "context", None),
    )
    out_specs = P("expert", "context", None)
    return jax.shard_map(
        per_device, mesh=mesh, in_specs=in_specs, out_specs=out_specs, check_vma=False
    )
```

```python
import functools

import jax
import jax.numpy as jnp
from jax import lax
from jax.experimental import pallas as pl
from jax.experimental.pallas import tpu as pltpu
from jax.sharding import PartitionSpec as P

HEAD_DIM = 64
LANES = 128
BF16 = jnp.bfloat16
F32 = jnp.float32


def iota(shape, axis):
    return lax.broadcasted_iota(jnp.int32, shape, axis)


def dot(a, b):
    return jnp.dot(a, b, preferred_element_type=F32)


def flat_rows(pieces):
    count, rows, lanes = pieces.shape
    if rows % 16:
        return pieces.astype(F32).reshape(count * rows, lanes).astype(BF16)
    return pieces.reshape(count * rows, lanes)


def slot_rows(ids, experts, cap):
    tok_rows = ids.shape[1]
    onehot = jnp.where(iota((experts, tok_rows), 0) == ids, 1.0, 0.0)
    upto = jnp.where(iota((tok_rows, tok_rows), 0) <= iota((tok_rows, tok_rows), 1), 1.0, 0.0)
    before = dot(onehot.astype(BF16), upto.astype(BF16))
    rank = jnp.sum(onehot * before, axis=0, keepdims=True) - 1.0
    slot = ids * cap + rank.astype(jnp.int32)
    return jnp.where(iota((experts * cap, tok_rows), 0) == slot, 1.0, 0.0)


VMEM = pl.BlockSpec(memory_space=pltpu.VMEM)
SMEM = pl.BlockSpec(memory_space=pltpu.SMEM)
HBM = pl.BlockSpec(memory_space=pltpu.HBM)


class Fetched:
    def __init__(self, source, held, sems, pieces):
        self.held = held
        self.copies = [
            pltpu.make_async_copy(source.at[there], held.at[here], sems.at[t])
            for t, (there, here) in enumerate(pieces)
        ]
        self.waited = [False] * len(pieces)
        for copy in self.copies:
            copy.start()

    def piece(self, t):
        if not self.waited[t]:
            self.copies[t].wait()
            self.waited[t] = True
        return self.held

    def whole(self):
        for t in range(len(self.copies)):
            self.piece(t)
        return self.held


class Sent:
    def __init__(self, target, held, sems, pieces):
        self.held = held
        self.copies = [
            pltpu.make_async_copy(held.at[at], target.at[at], sems.at[t])
            for t, at in enumerate(pieces)
        ]

    def send(self, t):
        self.copies[t].start()

    def finish(self):
        for copy in self.copies:
            copy.wait()


def full(array):
    return (array, array.shape, [(Ellipsis, Ellipsis)])


def firsts(array):
    return (array, array.shape, [(t, t) for t in range(array.shape[0])])


def columns(array, start, count, tile):
    cuts = [
        ((slice(None), pl.ds(start + lo, tile)), (slice(None), pl.ds(lo, tile)))
        for lo in range(0, count, tile)
    ]
    return (array, (array.shape[0], count), cuts)


def place_of(array, at):
    held = (array.shape[0], *array.shape[2:])
    return (array, held, [((slice(None), at), Ellipsis)])


def call(kernel, info, small, big, outs, after=(), scratch=(), flops=0, exps=0, limit=32):
    moved = sum(2 * a.size for a, _, _ in big) + sum(2 * o.size for o, _ in outs)
    held = []
    for array, dims, pieces in big:
        held += [pltpu.VMEM(dims, array.dtype), pltpu.SemaphoreType.DMA((len(pieces),))]
    for out, pieces in outs:
        held += [pltpu.VMEM(out.shape, out.dtype), pltpu.SemaphoreType.DMA((len(pieces),))]

    def body(*refs):
        refs = list(refs)

        def take(count):
            taken = refs[:count]
            del refs[:count]
            return taken

        info_ref = take(1)[0]
        small_refs, big_refs = take(len(small)), take(len(big))
        take(len(after))
        out_refs = take(len(outs))
        fetched = [
            Fetched(ref, *take(2), pieces) for ref, (_, _, pieces) in zip(big_refs, big)
        ]
        sent = [Sent(ref, *take(2), pieces) for ref, (_, pieces) in zip(out_refs, outs)]
        kernel(info_ref, *small_refs, *fetched, *sent, *refs)
        for item in fetched:
            item.whole()
        for item in sent:
            item.finish()

    return pl.pallas_call(
        body,
        out_shape=[out for out, _ in outs],
        in_specs=[SMEM] + [VMEM] * len(small) + [HBM] * (len(big) + len(after)),
        out_specs=[HBM] * len(outs),
        scratch_shapes=held + list(scratch),
        compiler_params=pltpu.CompilerParams(vmem_limit_bytes=limit << 20),
        cost_estimate=pl.CostEstimate(flops=flops, bytes_accessed=moved, transcendentals=exps),
    )(info, *small, *(array for array, _, _ in big), *after)


def shape(*dims):
    return jax.ShapeDtypeStruct(dims, BF16)


def tie(value, *after):
    return pl.pallas_call(
        lambda *refs: None,
        out_shape=jax.ShapeDtypeStruct(value.shape, value.dtype),
        in_specs=[HBM] * (1 + len(after)),
        out_specs=HBM,
        input_output_aliases={0: 0},
    )(value, *after)


def dispatch_kernel(experts, cap, info_ref, ids, tokens, out):
    place = slot_rows(ids.whole()[info_ref[0]], experts, cap).astype(BF16)
    out.held[...] = dot(place, tokens.whole()[...]).astype(BF16)
    out.send(0)


def collect_kernel(experts, cap, info_ref, ids_ref, rows, out):
    place = slot_rows(ids_ref[info_ref[0]], experts, cap).T.astype(BF16)
    out.held[...] = dot(place, rows.whole()[...]).astype(BF16)
    out.send(0)


def side_kernel(experts, cap, info_ref, ids_ref, near, out):
    place = slot_rows(ids_ref[info_ref[0]], experts, cap).T.astype(BF16)
    rows_ref = near.whole()
    for i in range(2):
        rows = flat_rows(rows_ref[:, i])
        out.held[:, i * LANES : (i + 1) * LANES] = dot(place, rows).astype(BF16)
    out.send(0)


def project_kernel(places, experts, cap, chans, info_ref, *refs):
    rows, weight, sides, out = refs[:places], refs[places], refs[places + 1 : -1], refs[-1]
    tile = 256

    def store(at, lo, made):
        made = made.astype(BF16)
        for e in range(experts):
            out.held[e, at, :, lo : lo + made.shape[1]] = made[e * cap : (e + 1) * cap, :]

    for t in range(chans // tile):
        lo = t * tile
        for at in range(places):
            store(at, lo, dot(rows[at].whole()[...], weight.piece(t)[:, lo : lo + tile]))
        out.send(t)
    if sides:
        first = rows[0].whole()[...]
        store(0, chans, dot(first, sides[0].whole()[...]))
        steps = [ref.whole()[...].astype(F32) for ref in sides[1:]]
        spare = LANES - sum(part.shape[0] for part in steps)
        steps.append(jnp.zeros((spare, steps[0].shape[1]), F32))
        steps = jnp.concatenate(steps, axis=0).astype(BF16)
        made = lax.dot_general(
            first, steps, (((1,), (1,)), ((), ())), preferred_element_type=F32
        )
        store(1, chans, made)
        out.send(chans // tile)


def gate_kernel(places, chans, info_ref, *refs):
    rows, weight, outs = refs[:places], refs[places], refs[places + 1 :]
    tile = 256
    for t in range(chans // tile):
        lo = t * tile
        for at in range(places):
            made = dot(rows[at].whole()[...], weight.piece(t)[:, lo : lo + tile])
            outs[at].held[:, lo : lo + tile] = made.astype(BF16)
    for out in outs:
        out.send(0)


def output_kernel(count, info_ref, *refs):
    scanned, gates, weight, outs = refs[:count], refs[count : 2 * count], refs[2 * count], refs[2 * count + 1 :]
    tile = 512
    gated = []
    for rows, gate in zip(scanned, gates):
        gate = jax.nn.silu(gate.whole()[...].astype(F32))
        gated.append((flat_rows(rows.whole()[...]).astype(F32) * gate).astype(BF16))
    for lo in range(0, weight.held.shape[1], tile):
        for rows, out in zip(gated, outs):
            part = weight.piece(lo // tile)[:, lo : lo + tile]
            out.held[:, lo : lo + tile] = dot(rows, part).astype(BF16)
            out.send(lo // tile)


def factors_kernel(cfg, info_ref, ids_ref, head_ref, near, side, weights, kept, tail, last, placed):
    experts, cap, tok_rows, nstate, chn, heads = cfg
    blocks = ids_ref.shape[0]
    lower = iota((tok_rows, tok_rows), 0) >= iota((tok_rows, tok_rows), 1)
    ones = jnp.where(lower, 1.0, 0.0)
    first = iota((tok_rows, LANES), 1) < HEAD_DIM
    spread = jnp.where(
        iota((2 * LANES, chn), 0) % LANES == iota((2 * LANES, chn), 1) // HEAD_DIM, 1.0, 0.0
    ).astype(BF16)
    for q in range(2):
        place = slot_rows(ids_ref[info_ref[1 + q]], experts, cap).T.astype(BF16)
        placed.held[q] = dot(place, flat_rows(near.whole()[:, q, :, :chn])).astype(BF16)
    placed.send(0)
    side_ref = side.whole()
    for b in range(blocks):
        q = info_ref[1 + blocks + b]
        own_head = iota((LANES, LANES), 0) == iota((LANES, LANES), 1) + info_ref[
            1 + 2 * blocks + b
        ] * heads
        own_head = jnp.where(own_head & (iota((LANES, LANES), 1) < heads), 1.0, 0.0)
        raw = dot(side_ref[q, :, LANES:], own_head.astype(BF16))
        step = jax.nn.softplus(raw + head_ref[0:1, :])
        summed = jnp.dot(
            ones,
            step * head_ref[1:2, :],
            preferred_element_type=F32,
            precision=lax.Precision.HIGHEST,
        )
        source = summed - jnp.log(step)
        source_t = source.T
        left = jnp.exp(summed[tok_rows - 1 :, :] - source)
        high = left.astype(BF16)
        low = (left - high.astype(F32)).astype(BF16)
        tail.held[b] = dot(jnp.concatenate([high, low], axis=1), spread).astype(BF16)
        tail.send(b)

        both = side_ref[q, :, :LANES]
        keys_t = both.astype(F32).T.astype(BF16)[:nstate, :]
        scores = dot(both[:, nstate:], keys_t)
        for pair in range(heads // 2):
            lanes = slice(pair * LANES, (pair + 1) * LANES)
            wide = []
            for h in (2 * pair, 2 * pair + 1):
                wide.append(jnp.broadcast_to(summed[:, h : h + 1], (tok_rows, tok_rows)))
                gaps = wide[-1] - source_t[h : h + 1, :]
                decay = jnp.exp(jnp.where(lower, gaps, -jnp.inf))
                at = (h % 2) * tok_rows
                weights.held[b, pair, :, at : at + tok_rows] = (scores * decay).astype(BF16)
            both_wide = jnp.exp(jnp.where(first, wide[0], wide[1]))
            kept.held[b, :, lanes] = both_wide.astype(BF16)
            last.held[b, :, lanes] = both_wide[tok_rows - 8 :, :]
        weights.send(b)
        kept.send(b)
        last.send(b)


def scan_kernel(
    cfg,
    info_ref,
    ids_ref,
    chan_ref,
    placed,
    far,
    side,
    weights,
    kept,
    tail,
    last,
    out_near,
    out_far,
    inner_ref,
    made_ref,
):
    experts, cap, tok_rows, nstate, chn, heads = cfg
    blocks = ids_ref.shape[0]
    taps = 4
    inner_ref[:8, :] = jnp.zeros((8, chn), F32)

    for q in range(blocks):
        b = info_ref[1 + q]
        at = pl.ds(8 + b * tok_rows, tok_rows)
        if q < 2:
            inner_ref[at, :] = placed.whole()[q].astype(F32)
        else:
            place = slot_rows(ids_ref[b], experts, cap).T.astype(BF16)
            inner_ref[at, :] = dot(place, flat_rows(far.whole()[:, q - 2]))

    first = iota((tok_rows, LANES), 1) < HEAD_DIM
    state = jnp.zeros((nstate, chn), F32)
    side_ref = side.whole()
    for b in range(blocks):
        q = info_ref[1 + blocks + b]
        total = chan_ref[taps : taps + 1, :]
        for j in range(taps):
            start = 8 + b * tok_rows - (taps - 1) + j
            total = total + chan_ref[j : j + 1, :] * inner_ref[start : start + tok_rows, :]
        signal = jax.nn.silu(total)

        both = side_ref[q, :, :LANES]
        keys_t = both.astype(F32).T.astype(BF16)[:nstate, :]
        rest = chan_ref[taps + 1 : taps + 2, :] * signal
        if b > 0:
            carried = dot(both[:, nstate:], state.astype(BF16))
            rest = rest + carried * kept.piece(b)[b].astype(F32)
        if b < blocks - 1:
            added = dot(keys_t, (signal * tail.piece(b)[b].astype(F32)).astype(BF16))
            state = last.piece(b)[b, 7:8, :] * state + added

        for pair in range(heads // 2):
            lanes = slice(pair * LANES, (pair + 1) * LANES)
            values = signal[:, lanes]
            values = jnp.concatenate(
                [jnp.where(first, values, 0.0), jnp.where(first, 0.0, values)], axis=0
            ).astype(BF16)
            local = dot(weights.piece(b)[b, pair], values)
            made_ref[b * tok_rows : (b + 1) * tok_rows, lanes] = (rest[:, lanes] + local).astype(BF16)

    for q in range(blocks - 1, -1, -1):
        b = info_ref[1 + q]
        place = slot_rows(ids_ref[b], experts, cap).astype(BF16)
        start = pl.multiple_of(b * tok_rows, tok_rows)
        leaving = dot(place, made_ref[pl.ds(start, tok_rows), :]).astype(BF16)
        for e in range(experts):
            piece = leaving[e * cap : (e + 1) * cap, :]
            if q < 2:
                out_near.held[e, q] = piece
            else:
                out_far.held[e, q - 2] = piece
        if q == 2:
            out_far.send(0)
    out_near.send(0)


def per_device(
    tokens,
    route,
    w_inner,
    w_state,
    w_step,
    step_bias,
    decay_log,
    skip_gain,
    conv_weight,
    conv_bias,
    w_out,
):
    tok_rows, width = tokens.shape[1], tokens.shape[2]
    experts = lax.axis_size("expert")
    shards = lax.axis_size("context")
    cap = 2 * tok_rows // experts
    slots = experts * cap
    chans = w_inner.shape[3]
    heads = w_step.shape[2]
    nstate = w_state.shape[2] // 2
    chips = shards // 2
    far_count = shards - 2

    here = lax.axis_index("context").astype(jnp.int32)
    blocks = jnp.arange(shards, dtype=jnp.int32)
    order = 2 * ((here // 2 - blocks // 2) % chips) + ((here % 2) ^ (blocks % 2))
    groups = 2 * ((blocks // 2 - here // 2) % chips) + ((here % 2) ^ (blocks % 2))
    block_at = 2 * ((here // 2 - blocks // 2) % chips) + ((here % 2) ^ (blocks % 2))
    info = jnp.concatenate([here[None], block_at, order, groups])
    ids = route.reshape(shards, 1, tok_rows)
    swap = [(c, c ^ 1) for c in range(shards)]

    def hop(k):
        return [(c, ((c // 2 + k) % chips) * 2 + c % 2) for c in range(shards)]

    def permute(value, pairs):
        return lax.ppermute(value, "context", pairs)

    def spread(value):
        made = [value, permute(value, swap)]
        for k in range(1, chips):
            arrived = permute(value, hop(k))
            made += [arrived, permute(arrived, swap)]
        return made

    def exchange(value):
        return lax.all_to_all(value, "expert", split_axis=0, concat_axis=0, tiled=True)

    w_flat = w_inner[0].reshape(width, 2 * chans)

    once = [Ellipsis]
    outgoing = call(
        functools.partial(dispatch_kernel, experts, cap),
        info, [], [full(ids), full(tokens[0])], [(shape(slots, width), once)],
        flops=2 * slots * tok_rows * width,
    )[0]
    own = exchange(outgoing.reshape(experts, cap, width)).reshape(slots, width)
    steps = spread(tie(w_step[0], outgoing).T)
    own = tie(own, w_flat, *steps)
    swapped = permute(own, swap)

    def inner_cuts(extra):
        cuts = [(slice(None),) * 3 + (pl.ds(lo, 256),) for lo in range(0, chans, 256)]
        return cuts + [(slice(None),) * 3 + (pl.ds(chans, LANES),)] * extra

    near = call(
        functools.partial(project_kernel, 2, experts, cap, chans),
        info, [],
        [full(own), full(swapped), columns(w_flat, chans, chans, 256), full(w_state[0])]
        + [full(part) for part in steps],
        [(shape(experts, 2, cap, chans + LANES), inner_cuts(1))],
        flops=4 * slots * width * (chans + LANES),
    )[0]
    distant = []
    for k in range(1, chips):
        arrived = permute(own, hop(k))
        distant += [arrived, permute(tie(arrived, near), swap)]
    far = call(
        functools.partial(project_kernel, far_count, experts, cap, chans),
        info, [],
        [full(rows) for rows in distant] + [columns(w_flat, chans, chans, 256)],
        [(shape(experts, far_count, cap, chans), inner_cuts(0))],
        flops=2 * far_count * slots * width * chans,
    )[0]
    near_back = exchange(near)
    far_back = exchange(far)

    lanes = (slice(None),) * 3 + (pl.ds(chans, LANES),)
    side = call(
        functools.partial(side_kernel, experts, cap),
        info, [ids],
        [(near_back, (experts, 2, cap, LANES), [(lanes, Ellipsis)])],
        [(shape(tok_rows, 2 * LANES), once)],
        after=[far],
        flops=2 * slots * tok_rows * 2 * LANES,
    )[0]
    sides = jnp.stack(spread(side))

    def padded_heads(row):
        return jnp.pad(row, (0, LANES - heads))[None, :]

    head_rows = jnp.concatenate(
        [padded_heads(step_bias), padded_heads(-jnp.exp(decay_log)), jnp.zeros((6, LANES), F32)]
    )
    chan_rows = jnp.concatenate(
        [conv_weight, conv_bias[None, :], jnp.repeat(skip_gain, HEAD_DIM)[None, :]]
    )
    chan_rows = jnp.pad(chan_rows, ((0, 2), (0, 0)))
    def gates(rows):
        return call(
            functools.partial(gate_kernel, len(rows), chans),
            info, [],
            [full(part) for part in rows] + [columns(w_flat, 0, chans, 256)],
            [(shape(slots, chans), once)] * len(rows),
            after=[far],
            flops=2 * len(rows) * slots * width * chans,
        )

    gate_far = gates(distant)
    gate_near = gates([own, swapped])
    cfg = (experts, cap, tok_rows, nstate, chans, heads)
    each = list(range(shards))
    weights, kept, tail, last, placed = call(
        functools.partial(factors_kernel, cfg),
        info, [ids, head_rows], [full(near_back), full(sides)],
        [
            (shape(shards, heads // 2, tok_rows, 2 * tok_rows), each),
            (shape(shards, tok_rows, chans), each),
            (shape(shards, tok_rows, chans), each),
            (jax.ShapeDtypeStruct((shards, 8, chans), F32), each),
            (shape(2, tok_rows, chans), once),
        ],
        flops=2 * tok_rows * chans * (2 * slots + shards * 512),
        exps=shards * tok_rows * tok_rows * heads,
    )
    near_out, far_out = call(
        functools.partial(scan_kernel, cfg),
        info, [ids, chan_rows],
        [full(placed), full(far_back), full(sides), firsts(weights), firsts(kept), firsts(tail), firsts(last)],
        [
            (shape(experts, 2, cap, chans), once),
            (shape(experts, far_count, cap, chans), once),
        ],
        after=[gate_far[0], gate_near[0]],
        scratch=[
            pltpu.VMEM((8 + shards * tok_rows, chans), F32),
            pltpu.VMEM((shards * tok_rows, chans), BF16),
        ],
        flops=2 * shards * tok_rows * chans * (2 * slots + 2 * nstate + 2 * tok_rows),
    )
    far_ret = exchange(far_out)
    near_ret = exchange(near_out)

    def outputs(scanned, gate, places, after=()):
        cuts = [(slice(None), pl.ds(lo, 512)) for lo in range(0, width, 512)]
        return call(
            functools.partial(output_kernel, len(places)),
            info, [],
            [place_of(scanned, at) for at in places]
            + [full(gate[at]) for at in places]
            + [columns(w_out[0], 0, width, 512)],
            [(shape(slots, width), cuts)] * len(places),
            after=after,
            flops=2 * len(places) * slots * width * chans,
        )

    parts_other = outputs(far_ret, gate_far, range(1, far_count, 2))
    parts_other = [permute(part, swap) for part in parts_other]
    parts_mine = outputs(far_ret, gate_far, range(0, far_count, 2))
    hopped = []
    for k in range(1, chips):
        pair = parts_mine[k - 1].astype(F32) + parts_other[k - 1].astype(F32)
        hopped.append(permute(pair.astype(BF16), hop(chips - k)))
    part_swap = outputs(near_ret, gate_near, [1])[0]
    part_own = outputs(near_ret, gate_near, [0], hopped)[0]
    summed = part_own.astype(F32) + permute(part_swap, swap).astype(F32)
    for part in hopped:
        summed = summed + part.astype(F32)
    returned = exchange(summed.astype(BF16).reshape(experts, cap, width)).reshape(slots, width)
    result = call(
        functools.partial(collect_kernel, experts, cap),
        info, [ids], [full(returned)], [(shape(tok_rows, width), once)],
        flops=2 * slots * tok_rows * width,
    )[0]
    return result[None]


def solution(mesh):
    in_specs = (
        P("expert", "context", None),
        P("expert", None, None),
        P("expert", None, None, "context"),
        P("expert", None, None),
        P("expert", None, "context"),
        P("context"),
        P("context"),
        P("context"),
        P(None, "context"),
        P("context"),
        P("expert", "context", None),
    )
    out_specs = P("expert", "context", None)
    return jax.shard_map(
        per_device, mesh=mesh, in_specs=in_specs, out_specs=out_specs, check_vma=False
    )
```

```python
import functools

import jax
import jax.numpy as jnp
from jax import lax
from jax.experimental import pallas as pl
from jax.experimental.pallas import tpu as pltpu
from jax.sharding import PartitionSpec as P

HEAD_DIM = 64
LANES = 128
BF16 = jnp.bfloat16
F32 = jnp.float32


def iota(shape, axis):
    return lax.broadcasted_iota(jnp.int32, shape, axis)


def dot(a, b):
    return jnp.dot(a, b, preferred_element_type=F32)


def flat_rows(pieces):
    count, rows, lanes = pieces.shape
    if rows % 16:
        return pieces.astype(F32).reshape(count * rows, lanes).astype(BF16)
    return pieces.reshape(count * rows, lanes)


def slot_rows(ids, experts, cap):
    tok_rows = ids.shape[1]
    onehot = jnp.where(iota((experts, tok_rows), 0) == ids, 1.0, 0.0)
    upto = jnp.where(iota((tok_rows, tok_rows), 0) <= iota((tok_rows, tok_rows), 1), 1.0, 0.0)
    before = dot(onehot.astype(BF16), upto.astype(BF16))
    rank = jnp.sum(onehot * before, axis=0, keepdims=True) - 1.0
    slot = ids * cap + rank.astype(jnp.int32)
    return jnp.where(iota((experts * cap, tok_rows), 0) == slot, 1.0, 0.0)


VMEM = pl.BlockSpec(memory_space=pltpu.VMEM)
SMEM = pl.BlockSpec(memory_space=pltpu.SMEM)
HBM = pl.BlockSpec(memory_space=pltpu.HBM)


def in_vmem(array):
    return pltpu.with_memory_space_constraint(array, pltpu.VMEM)


def in_hbm(array):
    return pltpu.with_memory_space_constraint(array, pltpu.HBM)


def call(kernel, info, inputs, outs, after=(), scratch=(), flops=0, exps=0, limit=24, pin=pltpu.VMEM):
    moved = sum(2 * a.size for a in inputs) + sum(2 * o.size for o in outs)
    count = 1 + len(inputs)

    def body(*refs):
        kernel(*refs[:count], *refs[count + len(after) :])

    return pl.pallas_call(
        body,
        out_shape=[pin(out.shape, out.dtype) for out in outs],
        in_specs=[SMEM] + [VMEM] * (len(inputs) + len(after)),
        out_specs=[VMEM] * len(outs),
        scratch_shapes=list(scratch),
        compiler_params=pltpu.CompilerParams(vmem_limit_bytes=limit << 20),
        cost_estimate=pl.CostEstimate(flops=flops, bytes_accessed=moved, transcendentals=exps),
    )(info, *(in_vmem(array) for array in (*inputs, *after)))


def stage(array, start, count, after=()):
    def body(*refs):
        source, target, sem = refs[0], refs[-2], refs[-1]
        copy = pltpu.make_async_copy(source.at[:, pl.ds(start, count)], target, sem)
        copy.start()
        copy.wait()

    return pl.pallas_call(
        body,
        out_shape=pltpu.VMEM((array.shape[0], count), array.dtype),
        in_specs=[HBM] + [VMEM] * len(after),
        out_specs=VMEM,
        scratch_shapes=[pltpu.SemaphoreType.DMA],
        compiler_params=pltpu.CompilerParams(vmem_limit_bytes=4 << 20),
        cost_estimate=pl.CostEstimate(
            flops=0, bytes_accessed=4 * array.shape[0] * count, transcendentals=0
        ),
    )(in_hbm(array), *(in_vmem(item) for item in after))


def shape(*dims):
    return jax.ShapeDtypeStruct(dims, BF16)


def tie(value, *after):
    return pl.pallas_call(
        lambda *refs: None,
        out_shape=pltpu.VMEM(value.shape, value.dtype),
        in_specs=[VMEM] * (1 + len(after)),
        out_specs=VMEM,
        input_output_aliases={0: 0},
        compiler_params=pltpu.CompilerParams(vmem_limit_bytes=4 << 20),
    )(*(in_vmem(array) for array in (value, *after)))


def dispatch_kernel(experts, cap, info_ref, ids_ref, tokens_ref, out_ref):
    place = slot_rows(ids_ref[info_ref[0]], experts, cap).astype(BF16)
    out_ref[...] = dot(place, tokens_ref[...]).astype(BF16)


def collect_kernel(experts, cap, info_ref, ids_ref, rows_ref, out_ref):
    place = slot_rows(ids_ref[info_ref[0]], experts, cap).T.astype(BF16)
    out_ref[...] = dot(place, rows_ref[...]).astype(BF16)


def side_kernel(experts, cap, chans, info_ref, ids_ref, near_ref, out_ref):
    place = slot_rows(ids_ref[info_ref[0]], experts, cap).T.astype(BF16)
    for i in range(2):
        rows = flat_rows(near_ref[:, i, :, chans:])
        out_ref[:, i * LANES : (i + 1) * LANES] = dot(place, rows).astype(BF16)


def project_kernel(places, experts, cap, chans, info_ref, *refs):
    rows, weight, sides, out_ref = refs[:places], refs[places], refs[places + 1 : -1], refs[-1]
    tile = 256

    def store(at, lo, made):
        made = made.astype(BF16)
        for e in range(experts):
            out_ref[e, at, :, lo : lo + made.shape[1]] = made[e * cap : (e + 1) * cap, :]

    for lo in range(0, chans, tile):
        for at in range(places):
            store(at, lo, dot(rows[at][...], weight[:, lo : lo + tile]))
    if sides:
        first = rows[0][...]
        store(0, chans, dot(first, sides[0][...]))
        steps = [ref[...].astype(F32) for ref in sides[1:]]
        spare = LANES - sum(part.shape[0] for part in steps)
        steps.append(jnp.zeros((spare, steps[0].shape[1]), F32))
        steps = jnp.concatenate(steps, axis=0).astype(BF16)
        made = lax.dot_general(
            first, steps, (((1,), (1,)), ((), ())), preferred_element_type=F32
        )
        store(1, chans, made)


def gate_kernel(places, chans, info_ref, *refs):
    rows, weight, outs = refs[:places], refs[places], refs[places + 1 :]
    tile = 256
    for lo in range(0, chans, tile):
        for at in range(places):
            outs[at][:, lo : lo + tile] = dot(rows[at][...], weight[:, lo : lo + tile]).astype(BF16)


def output_kernel(places, info_ref, scanned_ref, *refs):
    count = len(places)
    gates, weight, outs = refs[:count], refs[count], refs[count + 1 :]
    tile = 512
    gated = []
    for gate_ref, at in zip(gates, places):
        gate = jax.nn.silu(gate_ref[...].astype(F32))
        gated.append((flat_rows(scanned_ref[:, at]).astype(F32) * gate).astype(BF16))
    for lo in range(0, weight.shape[1], tile):
        for rows, out in zip(gated, outs):
            out[:, lo : lo + tile] = dot(rows, weight[:, lo : lo + tile]).astype(BF16)


def factors_kernel(cfg, info_ref, ids_ref, head_ref, near, side, weights, kept, tail, last, placed):
    experts, cap, tok_rows, nstate, chn, heads = cfg
    blocks = ids_ref.shape[0]
    lower = iota((tok_rows, tok_rows), 0) >= iota((tok_rows, tok_rows), 1)
    ones = jnp.where(lower, 1.0, 0.0)
    first = iota((tok_rows, LANES), 1) < HEAD_DIM
    spread = jnp.where(
        iota((2 * LANES, chn), 0) % LANES == iota((2 * LANES, chn), 1) // HEAD_DIM, 1.0, 0.0
    ).astype(BF16)
    for q in range(2):
        place = slot_rows(ids_ref[info_ref[1 + q]], experts, cap).T.astype(BF16)
        placed[q] = dot(place, flat_rows(near[:, q, :, :chn])).astype(BF16)
    side_ref = side
    for b in range(blocks):
        q = info_ref[1 + blocks + b]
        own_head = iota((LANES, LANES), 0) == iota((LANES, LANES), 1) + info_ref[
            1 + 2 * blocks + b
        ] * heads
        own_head = jnp.where(own_head & (iota((LANES, LANES), 1) < heads), 1.0, 0.0)
        raw = dot(side_ref[q, :, LANES:], own_head.astype(BF16))
        step = jax.nn.softplus(raw + head_ref[0:1, :])
        summed = jnp.dot(
            ones,
            step * head_ref[1:2, :],
            preferred_element_type=F32,
            precision=lax.Precision.HIGHEST,
        )
        source = summed - jnp.log(step)
        source_t = source.T
        left = jnp.exp(summed[tok_rows - 1 :, :] - source)
        high = left.astype(BF16)
        low = (left - high.astype(F32)).astype(BF16)
        tail[b] = dot(jnp.concatenate([high, low], axis=1), spread).astype(BF16)

        both = side_ref[q, :, :LANES]
        keys_t = both.astype(F32).T.astype(BF16)[:nstate, :]
        scores = dot(both[:, nstate:], keys_t)
        for pair in range(heads // 2):
            lanes = slice(pair * LANES, (pair + 1) * LANES)
            wide = []
            for h in (2 * pair, 2 * pair + 1):
                wide.append(jnp.broadcast_to(summed[:, h : h + 1], (tok_rows, tok_rows)))
                gaps = wide[-1] - source_t[h : h + 1, :]
                decay = jnp.exp(jnp.where(lower, gaps, -jnp.inf))
                at = (h % 2) * tok_rows
                weights[b, pair, :, at : at + tok_rows] = (scores * decay).astype(BF16)
            both_wide = jnp.exp(jnp.where(first, wide[0], wide[1]))
            kept[b, :, lanes] = both_wide.astype(BF16)
            last[b, :, lanes] = both_wide[tok_rows - 8 :, :]


def scan_kernel(
    cfg,
    info_ref,
    ids_ref,
    chan_ref,
    placed,
    far,
    side,
    weights,
    kept,
    tail,
    last,
    out_near,
    out_far,
    inner_ref,
    made_ref,
):
    experts, cap, tok_rows, nstate, chn, heads = cfg
    blocks = ids_ref.shape[0]
    taps = 4
    inner_ref[:8, :] = jnp.zeros((8, chn), F32)

    for q in range(blocks):
        b = info_ref[1 + q]
        at = pl.ds(8 + b * tok_rows, tok_rows)
        if q < 2:
            inner_ref[at, :] = placed[q].astype(F32)
        else:
            place = slot_rows(ids_ref[b], experts, cap).T.astype(BF16)
            inner_ref[at, :] = dot(place, flat_rows(far[:, q - 2]))

    first = iota((tok_rows, LANES), 1) < HEAD_DIM
    state = jnp.zeros((nstate, chn), F32)
    side_ref = side
    for b in range(blocks):
        q = info_ref[1 + blocks + b]
        total = chan_ref[taps : taps + 1, :]
        for j in range(taps):
            start = 8 + b * tok_rows - (taps - 1) + j
            total = total + chan_ref[j : j + 1, :] * inner_ref[start : start + tok_rows, :]
        signal = jax.nn.silu(total)

        both = side_ref[q, :, :LANES]
        keys_t = both.astype(F32).T.astype(BF16)[:nstate, :]
        rest = chan_ref[taps + 1 : taps + 2, :] * signal
        if b > 0:
            carried = dot(both[:, nstate:], state.astype(BF16))
            rest = rest + carried * kept[b].astype(F32)
        if b < blocks - 1:
            added = dot(keys_t, (signal * tail[b].astype(F32)).astype(BF16))
            state = last[b, 7:8, :] * state + added

        for pair in range(heads // 2):
            lanes = slice(pair * LANES, (pair + 1) * LANES)
            values = signal[:, lanes]
            values = jnp.concatenate(
                [jnp.where(first, values, 0.0), jnp.where(first, 0.0, values)], axis=0
            ).astype(BF16)
            local = dot(weights[b, pair], values)
            made_ref[b * tok_rows : (b + 1) * tok_rows, lanes] = (rest[:, lanes] + local).astype(BF16)

    for q in range(blocks - 1, -1, -1):
        b = info_ref[1 + q]
        place = slot_rows(ids_ref[b], experts, cap).astype(BF16)
        start = pl.multiple_of(b * tok_rows, tok_rows)
        leaving = dot(place, made_ref[pl.ds(start, tok_rows), :]).astype(BF16)
        for e in range(experts):
            piece = leaving[e * cap : (e + 1) * cap, :]
            if q < 2:
                out_near[e, q] = piece
            else:
                out_far[e, q - 2] = piece


def per_device(
    tokens,
    route,
    w_inner,
    w_state,
    w_step,
    step_bias,
    decay_log,
    skip_gain,
    conv_weight,
    conv_bias,
    w_out,
):
    tok_rows, width = tokens.shape[1], tokens.shape[2]
    experts = lax.axis_size("expert")
    shards = lax.axis_size("context")
    cap = 2 * tok_rows // experts
    slots = experts * cap
    chans = w_inner.shape[3]
    heads = w_step.shape[2]
    nstate = w_state.shape[2] // 2
    chips = shards // 2
    far_count = shards - 2

    here = lax.axis_index("context").astype(jnp.int32)
    blocks = jnp.arange(shards, dtype=jnp.int32)
    order = 2 * ((here // 2 - blocks // 2) % chips) + ((here % 2) ^ (blocks % 2))
    groups = 2 * ((blocks // 2 - here // 2) % chips) + ((here % 2) ^ (blocks % 2))
    block_at = 2 * ((here // 2 - blocks // 2) % chips) + ((here % 2) ^ (blocks % 2))
    info = jnp.concatenate([here[None], block_at, order, groups])
    ids = route.reshape(shards, 1, tok_rows)
    swap = [(c, c ^ 1) for c in range(shards)]

    def hop(k):
        return [(c, ((c // 2 + k) % chips) * 2 + c % 2) for c in range(shards)]

    def permute(value, pairs):
        return lax.ppermute(value, "context", pairs)

    def spread(value):
        made = [value, permute(value, swap)]
        for k in range(1, chips):
            arrived = permute(value, hop(k))
            made += [arrived, permute(arrived, swap)]
        return made

    def exchange(value):
        return lax.all_to_all(value, "expert", split_axis=0, concat_axis=0, tiled=True)

    w_flat = w_inner[0].reshape(width, 2 * chans)

    outgoing = call(
        functools.partial(dispatch_kernel, experts, cap),
        info, [ids, tokens[0]], [shape(slots, width)],
        flops=2 * slots * tok_rows * width,
    )[0]
    own = exchange(outgoing.reshape(experts, cap, width)).reshape(slots, width)
    steps = spread(tie(w_step[0], outgoing).T)
    inner_weight = stage(w_flat, chans, chans)
    own = tie(own, inner_weight, *steps)
    swapped = permute(own, swap)
    near = call(
        functools.partial(project_kernel, 2, experts, cap, chans),
        info, [own, swapped, inner_weight, w_state[0], *steps],
        [shape(experts, 2, cap, chans + LANES)],
        flops=4 * slots * width * (chans + LANES),
    )[0]
    distant = []
    for k in range(1, chips):
        arrived = tie(permute(own, hop(k)), near)
        distant += [arrived, permute(arrived, swap)]
    far = call(
        functools.partial(project_kernel, far_count, experts, cap, chans),
        info, [*distant, inner_weight], [shape(experts, far_count, cap, chans)],
        flops=2 * far_count * slots * width * chans,
    )[0]
    near_back = exchange(near)
    far_back = exchange(far)

    side = call(
        functools.partial(side_kernel, experts, cap, chans),
        info, [ids, near_back], [shape(tok_rows, 2 * LANES)],
        after=[far],
        flops=2 * slots * tok_rows * 2 * LANES,
    )[0]
    sides = jnp.stack(spread(side))

    def padded_heads(row):
        return jnp.pad(row, (0, LANES - heads))[None, :]

    head_rows = jnp.concatenate(
        [padded_heads(step_bias), padded_heads(-jnp.exp(decay_log)), jnp.zeros((6, LANES), F32)]
    )
    chan_rows = jnp.concatenate(
        [conv_weight, conv_bias[None, :], jnp.repeat(skip_gain, HEAD_DIM)[None, :]]
    )
    chan_rows = jnp.pad(chan_rows, ((0, 2), (0, 0)))
    gate_weight = stage(w_flat, 0, chans)
    out_weight = stage(w_out[0], 0, width, [far])

    def gates(rows):
        return call(
            functools.partial(gate_kernel, len(rows), chans),
            info, [*rows, gate_weight], [shape(slots, chans)] * len(rows),
            after=[far],
            flops=2 * len(rows) * slots * width * chans,
        )

    gate_far = gates(distant)
    gate_near = gates([own, swapped])
    cfg = (experts, cap, tok_rows, nstate, chans, heads)
    factors = call(
        functools.partial(factors_kernel, cfg),
        info, [ids, head_rows, near_back, sides],
        [
            shape(shards, heads // 2, tok_rows, 2 * tok_rows),
            shape(shards, tok_rows, chans),
            shape(shards, tok_rows, chans),
            jax.ShapeDtypeStruct((shards, 8, chans), F32),
            shape(2, tok_rows, chans),
        ],
        flops=2 * tok_rows * chans * (2 * slots + shards * 512),
        exps=shards * tok_rows * tok_rows * heads,
    )
    weights, kept, tail, last, placed = factors
    near_out, far_out = call(
        functools.partial(scan_kernel, cfg),
        info, [ids, chan_rows, placed, far_back, sides, weights, kept, tail, last],
        [shape(experts, 2, cap, chans), shape(experts, far_count, cap, chans)],
        after=[gate_far[0], gate_near[0], out_weight],
        scratch=[
            pltpu.VMEM((8 + shards * tok_rows, chans), F32),
            pltpu.VMEM((shards * tok_rows, chans), BF16),
        ],
        flops=2 * shards * tok_rows * chans * (2 * slots + 2 * nstate + 2 * tok_rows),
    )
    far_ret = exchange(far_out)
    near_ret = exchange(near_out)

    def outputs(scanned, gate, places, after=()):
        return call(
            functools.partial(output_kernel, places),
            info, [scanned, *(gate[at] for at in places), out_weight],
            [shape(slots, width)] * len(places),
            after=after,
            flops=2 * len(places) * slots * width * chans,
        )

    parts_other = outputs(far_ret, gate_far, range(1, far_count, 2))
    parts_other = [permute(part, swap) for part in parts_other]
    parts_mine = outputs(far_ret, gate_far, range(0, far_count, 2))
    hopped = []
    for k in range(1, chips):
        pair = parts_mine[k - 1].astype(F32) + parts_other[k - 1].astype(F32)
        hopped.append(permute(pair.astype(BF16), hop(chips - k)))
    part_swap = outputs(near_ret, gate_near, [1])[0]
    part_own = outputs(near_ret, gate_near, [0], hopped)[0]
    summed = part_own.astype(F32) + permute(part_swap, swap).astype(F32)
    for part in hopped:
        summed = summed + part.astype(F32)
    returned = exchange(summed.astype(BF16).reshape(experts, cap, width)).reshape(slots, width)
    result = call(
        functools.partial(collect_kernel, experts, cap),
        info, [ids, returned], [shape(tok_rows, width)],
        pin=jax.ShapeDtypeStruct,
        flops=2 * slots * tok_rows * width,
    )[0]
    return result[None]


def solution(mesh):
    in_specs = (
        P("expert", "context", None),
        P("expert", None, None),
        P("expert", None, None, "context"),
        P("expert", None, None),
        P("expert", None, "context"),
        P("context"),
        P("context"),
        P("context"),
        P(None, "context"),
        P("context"),
        P("expert", "context", None),
    )
    out_specs = P("expert", "context", None)
    return jax.shard_map(
        per_device, mesh=mesh, in_specs=in_specs, out_specs=out_specs, check_vma=False
    )
```

```python
import functools

import jax
import jax.numpy as jnp
from jax import lax
from jax.experimental import pallas as pl
from jax.experimental.pallas import tpu as pltpu
from jax.sharding import PartitionSpec as P

HEAD_DIM = 64
LANES = 128
BF16 = jnp.bfloat16
F32 = jnp.float32


def iota(shape, axis):
    return lax.broadcasted_iota(jnp.int32, shape, axis)


def dot(a, b):
    return jnp.dot(a, b, preferred_element_type=F32)


def flat_rows(pieces):
    count, rows, lanes = pieces.shape
    if rows % 16:
        return pieces.astype(F32).reshape(count * rows, lanes).astype(BF16)
    return pieces.reshape(count * rows, lanes)


def slot_rows(ids, experts, cap):
    tok_rows = ids.shape[1]
    onehot = jnp.where(iota((experts, tok_rows), 0) == ids, 1.0, 0.0)
    upto = jnp.where(iota((tok_rows, tok_rows), 0) <= iota((tok_rows, tok_rows), 1), 1.0, 0.0)
    before = dot(onehot.astype(BF16), upto.astype(BF16))
    rank = jnp.sum(onehot * before, axis=0, keepdims=True) - 1.0
    slot = ids * cap + rank.astype(jnp.int32)
    return jnp.where(iota((experts * cap, tok_rows), 0) == slot, 1.0, 0.0)


VMEM = pl.BlockSpec(memory_space=pltpu.VMEM)
SMEM = pl.BlockSpec(memory_space=pltpu.SMEM)
HBM = pl.BlockSpec(memory_space=pltpu.HBM)


class Stream:
    def __init__(self, copies, ahead):
        self.copies, self.ahead, self.started, self.done = copies, ahead, 0, set()
        self.start(ahead)

    def start(self, upto):
        while self.started < min(upto, len(self.copies)):
            self.copies[self.started].start()
            self.started += 1

    def need(self, i):
        self.start(i + self.ahead)
        if i not in self.done:
            self.copies[i].wait()
            self.done.add(i)


class Operand:
    def __init__(self, held, stream=None, first=0, count=0):
        self.held, self.stream, self.first, self.count = held, stream, first, count

    def piece(self, t):
        if self.stream:
            self.stream.need(self.first + t)
        return self.held

    def whole(self):
        for t in range(self.count):
            self.piece(t)
        return self.held


class Result:
    def __init__(self, held, copies=()):
        self.held, self.copies = held, copies

    def send(self, t):
        if self.copies:
            self.copies[t].start()

    def finish(self):
        for copy in self.copies:
            copy.wait()


def in_hbm(array):
    return pltpu.with_memory_space_constraint(array, pltpu.HBM)


def in_vmem(array):
    return pltpu.with_memory_space_constraint(array, pltpu.VMEM)


def kept_in_vmem(array):
    return (array, None, None)


def full(array):
    return (array, array.shape, [(Ellipsis, Ellipsis)])


def firsts(array):
    return (array, array.shape, [(t, t) for t in range(array.shape[0])])


def columns(array, start, count, tile):
    cuts = [
        ((slice(None), pl.ds(start + lo, tile)), (slice(None), pl.ds(lo, tile)))
        for lo in range(0, count, tile)
    ]
    return (array, (array.shape[0], count), cuts)


def place_of(array, at):
    held = (array.shape[0], *array.shape[2:])
    return (array, held, [((slice(None), at), Ellipsis)])


def call(
    kernel, info, big, outs, small=(), after=(), alias=None, scratch=(), flops=0, exps=0, limit=32
):
    moved = sum(2 * a.size for a, _, _ in big) + sum(2 * o.size for o, _ in outs)
    held = []
    for array, dims, pieces in big:
        if pieces:
            held.append(pltpu.VMEM(dims, array.dtype))
    for out, pieces in outs:
        if pieces:
            held.append(pltpu.VMEM(out.shape, out.dtype))
    fetches = sum(len(pieces or ()) for _, _, pieces in big)
    sends = sum(len(pieces or ()) for _, pieces in outs)
    held += [pltpu.SemaphoreType.DMA((max(count, 1),)) for count in (fetches, sends)]

    def body(*refs):
        refs = list(refs)

        def take(count):
            taken = refs[:count]
            del refs[:count]
            return taken

        info_ref = take(1)[0]
        small_refs, big_refs = take(len(small)), take(len(big))
        take(len(after) + (alias is not None))
        out_refs = take(len(outs))
        held_refs = [take(1)[0] if pieces else ref for ref, (_, _, pieces) in zip(big_refs, big)]
        made_refs = [take(1)[0] if pieces else ref for ref, (_, pieces) in zip(out_refs, outs)]
        fetch_sems, send_sems = take(2)
        copies, spans = [], []
        for source, target, (_, _, pieces) in zip(big_refs, held_refs, big):
            spans.append((len(copies), len(pieces or ())))
            for there, here in pieces or ():
                sem = fetch_sems.at[len(copies)]
                copies.append(pltpu.make_async_copy(source.at[there], target.at[here], sem))
        stream = Stream(copies, 3)
        operands = [
            Operand(ref, stream if count else None, at, count)
            for ref, (at, count) in zip(held_refs, spans)
        ]
        results, used = [], 0
        for target, source, (_, pieces) in zip(out_refs, made_refs, outs):
            sent = []
            for at in pieces or ():
                sent.append(pltpu.make_async_copy(source.at[at], target.at[at], send_sems.at[used]))
                used += 1
            results.append(Result(source, sent))
        kernel(info_ref, *small_refs, *operands, *results, *refs)
        for i in range(len(copies)):
            stream.need(i)
        for result in results:
            result.finish()

    arrays = [in_hbm(a) if pieces else in_vmem(a) for a, _, pieces in big]
    arrays += [in_hbm(array) for array in after] + ([in_hbm(alias)] if alias is not None else [])
    return pl.pallas_call(
        body,
        out_shape=[(pltpu.HBM if pieces else pltpu.VMEM)(o.shape, o.dtype) for o, pieces in outs],
        in_specs=[SMEM]
        + [VMEM] * len(small)
        + [HBM if pieces else VMEM for _, _, pieces in big]
        + [HBM] * (len(after) + (alias is not None)),
        out_specs=[HBM if pieces else VMEM for _, pieces in outs],
        scratch_shapes=held + list(scratch),
        input_output_aliases={len(small) + len(arrays): 0} if alias is not None else {},
        compiler_params=pltpu.CompilerParams(vmem_limit_bytes=limit << 20),
        cost_estimate=pl.CostEstimate(flops=flops, bytes_accessed=moved, transcendentals=exps),
    )(info, *small, *arrays)


def shape(*dims):
    return jax.ShapeDtypeStruct(dims, BF16)


def tie(value, *after):
    return pl.pallas_call(
        lambda *refs: None,
        out_shape=pltpu.VMEM(value.shape, value.dtype),
        in_specs=[VMEM] + [HBM] * len(after),
        out_specs=VMEM,
        input_output_aliases={0: 0},
        compiler_params=pltpu.CompilerParams(vmem_limit_bytes=4 << 20),
    )(in_vmem(value), *(in_hbm(array) for array in after))


def dispatch_kernel(experts, cap, info_ref, ids, tokens, out):
    place = slot_rows(ids.whole()[info_ref[0]], experts, cap).astype(BF16)
    out.held[...] = dot(place, tokens.whole()[...]).astype(BF16)
    out.send(0)


def collect_kernel(experts, cap, info_ref, ids_ref, rows, out):
    place = slot_rows(ids_ref[info_ref[0]], experts, cap).T.astype(BF16)
    out.held[...] = dot(place, rows.whole()[...]).astype(BF16)
    out.send(0)


def side_kernel(experts, cap, info_ref, ids_ref, near, out):
    place = slot_rows(ids_ref[info_ref[0]], experts, cap).T.astype(BF16)
    rows_ref = near.whole()
    for i in range(2):
        rows = flat_rows(rows_ref[:, i])
        out.held[:, i * LANES : (i + 1) * LANES] = dot(place, rows).astype(BF16)
    out.send(0)


def project_rows(places, experts, cap, rows, weight, out, tile):
    chans = weight.held.shape[1]
    for lo in range(0, chans, tile):
        part = weight.piece(lo // tile)[:, lo : lo + tile]
        for at, block in zip(places, rows):
            store_rows(out, at, lo, dot(block.whole()[...], part), experts, cap)
        out.send(lo // tile)


def store_rows(out, at, lo, made, experts, cap):
    made = made.astype(BF16)
    for e in range(experts):
        out.held[e, at, :, lo : lo + made.shape[1]] = made[e * cap : (e + 1) * cap, :]


def own_kernel(experts, cap, tile, info_ref, rows, weight, states, *refs):
    steps, out = refs[:-1], refs[-1]
    chans = weight.held.shape[1]
    project_rows([0], experts, cap, [rows], weight, out, tile)
    first = rows.whole()[...]
    store_rows(out, 0, chans, dot(first, states.whole()[...]), experts, cap)
    steps = [ref.whole()[...].astype(F32) for ref in steps]
    spare = LANES - sum(part.shape[0] for part in steps)
    steps.append(jnp.zeros((spare, steps[0].shape[1]), F32))
    steps = jnp.concatenate(steps, axis=0).astype(BF16)
    made = lax.dot_general(first, steps, (((1,), (1,)), ((), ())), preferred_element_type=F32)
    store_rows(out, 1, chans, made, experts, cap)
    out.send(chans // tile)


def project_kernel(places, experts, cap, tile, info_ref, *refs):
    rows, weight, out = refs[: len(places)], refs[-2], refs[-1]
    project_rows(places, experts, cap, rows, weight, out, tile)


def gate_kernel(tile, info_ref, *refs):
    count = len(refs) // 2
    rows, weight, outs = refs[:count], refs[count], refs[count + 1 :]
    for lo in range(0, weight.held.shape[1], tile):
        for block, out in zip(rows, outs):
            made = dot(block.whole()[...], weight.piece(lo // tile)[:, lo : lo + tile])
            out.held[:, lo : lo + tile] = made.astype(BF16)
    for out in outs:
        out.send(0)


def output_kernel(tile, info_ref, scanned, gate, weight, out):
    gates = jax.nn.silu(gate.whole()[...].astype(F32))
    gated = (flat_rows(scanned.whole()[...]).astype(F32) * gates).astype(BF16)
    for lo in range(0, weight.held.shape[1], tile):
        part = weight.piece(lo // tile)[:, lo : lo + tile]
        out.held[:, lo : lo + tile] = dot(gated, part).astype(BF16)


def factors_kernel(cfg, info_ref, ids_ref, head_ref, near, side, weights, kept, tail, last, placed):
    experts, cap, tok_rows, nstate, chn, heads = cfg
    blocks = ids_ref.shape[0]
    lower = iota((tok_rows, tok_rows), 0) >= iota((tok_rows, tok_rows), 1)
    ones = jnp.where(lower, 1.0, 0.0)
    first = iota((tok_rows, LANES), 1) < HEAD_DIM
    spread = jnp.where(
        iota((2 * LANES, chn), 0) % LANES == iota((2 * LANES, chn), 1) // HEAD_DIM, 1.0, 0.0
    ).astype(BF16)
    for q in range(2):
        place = slot_rows(ids_ref[info_ref[1 + q]], experts, cap).T.astype(BF16)
        placed.held[q] = dot(place, flat_rows(near.whole()[:, q, :, :chn])).astype(BF16)
    placed.send(0)
    side_ref = side.whole()
    for b in range(blocks):
        q = info_ref[1 + blocks + b]
        own_head = iota((LANES, LANES), 0) == iota((LANES, LANES), 1) + info_ref[
            1 + 2 * blocks + b
        ] * heads
        own_head = jnp.where(own_head & (iota((LANES, LANES), 1) < heads), 1.0, 0.0)
        raw = dot(side_ref[q, :, LANES:], own_head.astype(BF16))
        step = jax.nn.softplus(raw + head_ref[0:1, :])
        summed = jnp.dot(
            ones,
            step * head_ref[1:2, :],
            preferred_element_type=F32,
            precision=lax.Precision.HIGHEST,
        )
        source = summed - jnp.log(step)
        source_t = source.T
        left = jnp.exp(summed[tok_rows - 1 :, :] - source)
        high = left.astype(BF16)
        low = (left - high.astype(F32)).astype(BF16)
        tail.held[b] = dot(jnp.concatenate([high, low], axis=1), spread).astype(BF16)
        tail.send(b)

        both = side_ref[q, :, :LANES]
        keys_t = both.astype(F32).T.astype(BF16)[:nstate, :]
        scores = dot(both[:, nstate:], keys_t)
        for pair in range(heads // 2):
            lanes = slice(pair * LANES, (pair + 1) * LANES)
            wide = []
            for h in (2 * pair, 2 * pair + 1):
                wide.append(jnp.broadcast_to(summed[:, h : h + 1], (tok_rows, tok_rows)))
                gaps = wide[-1] - source_t[h : h + 1, :]
                decay = jnp.exp(jnp.where(lower, gaps, -jnp.inf))
                at = (h % 2) * tok_rows
                weights.held[b, pair, :, at : at + tok_rows] = (scores * decay).astype(BF16)
            both_wide = jnp.exp(jnp.where(first, wide[0], wide[1]))
            kept.held[b, :, lanes] = both_wide.astype(BF16)
            last.held[b, :, lanes] = both_wide[tok_rows - 8 :, :]
        weights.send(b)
        kept.send(b)
        last.send(b)


def scan_kernel(
    cfg,
    info_ref,
    ids_ref,
    chan_ref,
    side,
    placed,
    far,
    *refs,
):
    experts, cap, tok_rows, nstate, chn, heads = cfg
    out_near, out_far, inner_ref, made_ref = refs[-4:]
    blocks = ids_ref.shape[0]
    taps = 4
    inner_ref[:8, :] = jnp.zeros((8, chn), F32)

    for q in range(blocks):
        b = info_ref[1 + q]
        at = pl.ds(8 + b * tok_rows, tok_rows)
        if q < 2:
            inner_ref[at, :] = placed.whole()[q].astype(F32)
        else:
            place = slot_rows(ids_ref[b], experts, cap).T.astype(BF16)
            inner_ref[at, :] = dot(place, flat_rows(far.whole()[:, q - 2]))

    first = iota((tok_rows, LANES), 1) < HEAD_DIM
    state = jnp.zeros((nstate, chn), F32)
    side_ref = side.whole()
    for b in range(blocks):
        q = info_ref[1 + blocks + b]
        weights, kept, tail, last = refs[4 * b : 4 * b + 4]
        total = chan_ref[taps : taps + 1, :]
        for j in range(taps):
            start = 8 + b * tok_rows - (taps - 1) + j
            total = total + chan_ref[j : j + 1, :] * inner_ref[start : start + tok_rows, :]
        signal = jax.nn.silu(total)

        both = side_ref[q, :, :LANES]
        keys_t = both.astype(F32).T.astype(BF16)[:nstate, :]
        rest = chan_ref[taps + 1 : taps + 2, :] * signal
        if b > 0:
            carried = dot(both[:, nstate:], state.astype(BF16))
            rest = rest + carried * kept.whole()[0].astype(F32)
        if b < blocks - 1:
            added = dot(keys_t, (signal * tail.whole()[0].astype(F32)).astype(BF16))
            state = last.whole()[0, 7:8, :] * state + added

        for pair in range(heads // 2):
            lanes = slice(pair * LANES, (pair + 1) * LANES)
            values = signal[:, lanes]
            values = jnp.concatenate(
                [jnp.where(first, values, 0.0), jnp.where(first, 0.0, values)], axis=0
            ).astype(BF16)
            local = dot(weights.whole()[0, pair], values)
            made_ref[b * tok_rows : (b + 1) * tok_rows, lanes] = (rest[:, lanes] + local).astype(BF16)

    for q in range(blocks - 1, -1, -1):
        b = info_ref[1 + q]
        place = slot_rows(ids_ref[b], experts, cap).astype(BF16)
        start = pl.multiple_of(b * tok_rows, tok_rows)
        leaving = dot(place, made_ref[pl.ds(start, tok_rows), :]).astype(BF16)
        for e in range(experts):
            piece = leaving[e * cap : (e + 1) * cap, :]
            if q < 2:
                out_near.held[e, q] = piece
            else:
                out_far.held[e, q - 2] = piece
        if q == 2:
            out_far.send(0)
    out_near.send(0)


def per_device(
    tokens,
    route,
    w_inner,
    w_state,
    w_step,
    step_bias,
    decay_log,
    skip_gain,
    conv_weight,
    conv_bias,
    w_out,
):
    tok_rows, width = tokens.shape[1], tokens.shape[2]
    experts = lax.axis_size("expert")
    shards = lax.axis_size("context")
    cap = 2 * tok_rows // experts
    slots = experts * cap
    chans = w_inner.shape[3]
    heads = w_step.shape[2]
    nstate = w_state.shape[2] // 2
    chips = shards // 2
    far_count = shards - 2

    here = lax.axis_index("context").astype(jnp.int32)
    blocks = jnp.arange(shards, dtype=jnp.int32)
    order = 2 * ((here // 2 - blocks // 2) % chips) + ((here % 2) ^ (blocks % 2))
    groups = 2 * ((blocks // 2 - here // 2) % chips) + ((here % 2) ^ (blocks % 2))
    block_at = 2 * ((here // 2 - blocks // 2) % chips) + ((here % 2) ^ (blocks % 2))
    info = jnp.concatenate([here[None], block_at, order, groups])
    ids = route.reshape(shards, 1, tok_rows)
    swap = [(c, c ^ 1) for c in range(shards)]

    def hop(k):
        return [(c, ((c // 2 + k) % chips) * 2 + c % 2) for c in range(shards)]

    def permute(value, pairs):
        return lax.ppermute(value, "context", pairs)

    def spread(value):
        made = [value, permute(value, swap)]
        for k in range(1, chips):
            arrived = permute(value, hop(k))
            made += [arrived, permute(arrived, swap)]
        return made

    def exchange(value):
        return lax.all_to_all(value, "expert", split_axis=0, concat_axis=0, tiled=True)

    w_flat = w_inner[0].reshape(width, 2 * chans)

    once = [Ellipsis]
    outgoing = call(
        functools.partial(dispatch_kernel, experts, cap),
        info, [full(ids), full(tokens[0])], [(shape(slots, width), once)],
        flops=2 * slots * tok_rows * width,
    )[0]
    own = exchange(outgoing.reshape(experts, cap, width)).reshape(slots, width)
    steps = spread(tie(w_step[0], outgoing).T)
    own = tie(own, w_flat, *steps)
    swapped = permute(own, swap)
    everything = (slice(None),) * 3

    def inner_cuts(place, extra):
        at = (slice(None), place, slice(None))
        cuts = [at + (pl.ds(lo, 256),) for lo in range(0, chans, 256)]
        return cuts + [everything + (pl.ds(chans, LANES),)] * extra

    near_shape = shape(experts, 2, cap, chans + LANES)
    own_part = call(
        functools.partial(own_kernel, experts, cap, 256),
        info,
        [kept_in_vmem(own), columns(w_flat, chans, chans, 256), full(w_state[0])]
        + [full(part) for part in steps],
        [(near_shape, inner_cuts(0, 1))],
        flops=2 * slots * width * (chans + 2 * LANES),
    )[0]
    near = call(
        functools.partial(project_kernel, [1], experts, cap, 256),
        info,
        [kept_in_vmem(swapped), columns(w_flat, chans, chans, 256)],
        [(near_shape, inner_cuts(1, 0))],
        alias=own_part,
        flops=2 * slots * width * chans,
    )[0]
    distant = []
    for k in range(1, chips):
        arrived = tie(permute(own, hop(k)), near)
        distant += [arrived, permute(arrived, swap)]
    far = call(
        functools.partial(project_kernel, range(far_count), experts, cap, 256),
        info,
        [kept_in_vmem(rows) for rows in distant] + [columns(w_flat, chans, chans, 256)],
        [(shape(experts, far_count, cap, chans), inner_cuts(slice(None), 0))],
        flops=2 * far_count * slots * width * chans,
    )[0]
    near_back = exchange(near)
    far_back = exchange(far)

    lanes = everything + (pl.ds(chans, LANES),)
    side = call(
        functools.partial(side_kernel, experts, cap),
        info,
        [(near_back, (experts, 2, cap, LANES), [(lanes, Ellipsis)])],
        [(shape(tok_rows, 2 * LANES), once)],
        small=[ids],
        after=[far],
        flops=2 * slots * tok_rows * 2 * LANES,
    )[0]
    sides = jnp.stack(spread(side))

    def padded_heads(row):
        return jnp.pad(row, (0, LANES - heads))[None, :]

    head_rows = jnp.concatenate(
        [padded_heads(step_bias), padded_heads(-jnp.exp(decay_log)), jnp.zeros((6, LANES), F32)]
    )
    chan_rows = jnp.concatenate(
        [conv_weight, conv_bias[None, :], jnp.repeat(skip_gain, HEAD_DIM)[None, :]]
    )
    chan_rows = jnp.pad(chan_rows, ((0, 2), (0, 0)))
    def gates(rows):
        return call(
            functools.partial(gate_kernel, 256),
            info,
            [full(part) for part in rows] + [columns(w_flat, 0, chans, 256)],
            [(shape(slots, chans), once)] * len(rows),
            after=[far],
            flops=2 * len(rows) * slots * width * chans,
        )

    gate_far = gates(distant)
    gate_near = gates([own, swapped])
    cfg = (experts, cap, tok_rows, nstate, chans, heads)
    each = list(range(shards))
    weights, kept, tail, last, placed = call(
        functools.partial(factors_kernel, cfg),
        info, [full(near_back), full(sides)],
        [
            (shape(shards, heads // 2, tok_rows, 2 * tok_rows), each),
            (shape(shards, tok_rows, chans), each),
            (shape(shards, tok_rows, chans), each),
            (jax.ShapeDtypeStruct((shards, 8, chans), F32), each),
            (shape(2, tok_rows, chans), once),
        ],
        small=[ids, head_rows],
        flops=2 * tok_rows * chans * (2 * slots + shards * 512),
        exps=shards * tok_rows * tok_rows * heads,
    )
    in_turn = [
        (array, (1, *array.shape[1:]), [(pl.ds(b, 1), Ellipsis)])
        for b in range(shards)
        for array in (weights, kept, tail, last)
    ]
    near_out, far_out = call(
        functools.partial(scan_kernel, cfg),
        info,
        [full(sides), full(placed), full(far_back)] + in_turn,
        [
            (shape(experts, 2, cap, chans), None),
            (shape(experts, far_count, cap, chans), None),
        ],
        small=[ids, chan_rows],
        after=[gate_far[0], gate_near[0]],
        scratch=[
            pltpu.VMEM((8 + shards * tok_rows, chans), F32),
            pltpu.VMEM((shards * tok_rows, chans), BF16),
        ],
        flops=2 * shards * tok_rows * chans * (2 * slots + 2 * nstate + 2 * tok_rows),
    )
    far_ret = exchange(far_out)
    near_ret = exchange(near_out)

    def output(scanned, at, after=()):
        gate = (gate_near + gate_far)[at]
        return call(
            functools.partial(output_kernel, 512),
            info,
            [place_of(scanned, at % 2 if at < 2 else at - 2), full(gate), columns(w_out[0], 0, width, 512)],
            [(shape(slots, width), None)],
            after=after,
            flops=2 * slots * width * chans,
        )[0]

    hopped = []
    others = [permute(output(far_ret, 2 * k + 1), swap) for k in range(1, chips)]
    for k in range(1, chips):
        pair = output(far_ret, 2 * k).astype(F32) + others[k - 1].astype(F32)
        hopped.append(permute(pair.astype(BF16), hop(chips - k)))
    part_swap = permute(output(near_ret, 1), swap)
    part_own = output(near_ret, 0, hopped)
    summed = part_own.astype(F32) + part_swap.astype(F32)
    for part in hopped:
        summed = summed + part.astype(F32)
    returned = exchange(summed.astype(BF16).reshape(experts, cap, width)).reshape(slots, width)
    result = call(
        functools.partial(collect_kernel, experts, cap),
        info, [kept_in_vmem(returned)], [(shape(tok_rows, width), once)],
        small=[ids],
        flops=2 * slots * tok_rows * width,
    )[0]
    return result[None]


def solution(mesh):
    in_specs = (
        P("expert", "context", None),
        P("expert", None, None),
        P("expert", None, None, "context"),
        P("expert", None, None),
        P("expert", None, "context"),
        P("context"),
        P("context"),
        P("context"),
        P(None, "context"),
        P("context"),
        P("expert", "context", None),
    )
    out_specs = P("expert", "context", None)
    return jax.shard_map(
        per_device, mesh=mesh, in_specs=in_specs, out_specs=out_specs, check_vma=False
    )
```

```python
import functools

import jax
import jax.numpy as jnp
from jax import lax
from jax.experimental import pallas as pl
from jax.experimental.pallas import tpu as pltpu
from jax.sharding import PartitionSpec as P

HEAD_DIM = 64
LANES = 128
BF16 = jnp.bfloat16
F32 = jnp.float32


def iota(shape, axis):
    return lax.broadcasted_iota(jnp.int32, shape, axis)


def dot(a, b):
    return jnp.dot(a, b, preferred_element_type=F32)


def flat_rows(pieces):
    count, rows, lanes = pieces.shape
    if rows % 16:
        return pieces.astype(F32).reshape(count * rows, lanes).astype(BF16)
    return pieces.reshape(count * rows, lanes)


def slot_rows(ids, experts, cap, me=0):
    tok_rows = ids.shape[1]
    onehot = jnp.where(iota((experts, tok_rows), 0) == ids, 1.0, 0.0)
    upto = jnp.where(iota((tok_rows, tok_rows), 0) <= iota((tok_rows, tok_rows), 1), 1.0, 0.0)
    before = dot(onehot.astype(BF16), upto.astype(BF16))
    rank = jnp.sum(onehot * before, axis=0, keepdims=True) - 1.0
    slot = (ids ^ me) * cap + rank.astype(jnp.int32)
    return jnp.where(iota((experts * cap, tok_rows), 0) == slot, 1.0, 0.0)


VMEM = pl.BlockSpec(memory_space=pltpu.VMEM)
SMEM = pl.BlockSpec(memory_space=pltpu.SMEM)
HBM = pl.BlockSpec(memory_space=pltpu.HBM)
ANY = pl.BlockSpec(memory_space=pl.ANY)


class Stream:
    def __init__(self, copies, ahead):
        self.copies, self.ahead, self.started, self.done = copies, ahead, 0, set()
        self.start(ahead)

    def start(self, upto):
        while self.started < min(upto, len(self.copies)):
            self.copies[self.started].start()
            self.started += 1

    def need(self, i):
        self.start(i + self.ahead)
        if i not in self.done:
            self.copies[i].wait()
            self.done.add(i)


class Operand:
    def __init__(self, held, stream=None, first=0, count=0):
        self.held, self.stream, self.first, self.count = held, stream, first, count

    def piece(self, t):
        if self.stream:
            self.stream.need(self.first + t)
        return self.held

    def whole(self):
        for t in range(self.count):
            self.piece(t)
        return self.held


class Result:
    def __init__(self, held, copies=()):
        self.held, self.copies = held, copies

    def send(self, t):
        if self.copies:
            self.copies[t].start()

    def finish(self):
        for copy in self.copies:
            copy.wait()


def in_hbm(array):
    return pltpu.with_memory_space_constraint(array, pltpu.HBM)


def in_vmem(array):
    return pltpu.with_memory_space_constraint(array, pltpu.VMEM)


def kept_in_vmem(array):
    return (array, None, None)


def full(array):
    return (array, array.shape, [(Ellipsis, Ellipsis)])


def firsts(array):
    return (array, array.shape, [(t, t) for t in range(array.shape[0])])


def columns(array, start, count):
    return (array, (array.shape[0], count), [((slice(None), pl.ds(start, count)), Ellipsis)])


def call(
    kernel, info, big, outs, small=(), after=(), alias=None, scratch=(), flops=0, exps=0, limit=32
):
    moved = sum(2 * a.size for a, _, _ in big) + sum(2 * o.size for o, _ in outs)
    held = []
    for array, dims, pieces in big:
        if pieces:
            held.append(pltpu.VMEM(dims, array.dtype))
    for out, pieces in outs:
        if pieces:
            held.append(pltpu.VMEM(out.shape, out.dtype))
    fetches = sum(len(pieces or ()) for _, _, pieces in big)
    sends = sum(len(pieces or ()) for _, pieces in outs)
    held += [pltpu.SemaphoreType.DMA((max(count, 1),)) for count in (fetches, sends)]

    def body(*refs):
        refs = list(refs)

        def take(count):
            taken = refs[:count]
            del refs[:count]
            return taken

        info_ref = take(1)[0]
        small_refs, big_refs = take(len(small)), take(len(big))
        take(len(after) + (alias is not None))
        out_refs = take(len(outs))
        held_refs = [take(1)[0] if pieces else ref for ref, (_, _, pieces) in zip(big_refs, big)]
        made_refs = [take(1)[0] if pieces else ref for ref, (_, pieces) in zip(out_refs, outs)]
        fetch_sems, send_sems = take(2)
        copies, spans = [], []
        for source, target, (_, _, pieces) in zip(big_refs, held_refs, big):
            spans.append((len(copies), len(pieces or ())))
            for there, here in pieces or ():
                sem = fetch_sems.at[len(copies)]
                copies.append(pltpu.make_async_copy(source.at[there], target.at[here], sem))
        stream = Stream(copies, 3)
        operands = [
            Operand(ref, stream if count else None, at, count)
            for ref, (at, count) in zip(held_refs, spans)
        ]
        results, used = [], 0
        for target, source, (_, pieces) in zip(out_refs, made_refs, outs):
            sent = []
            for at in pieces or ():
                sent.append(pltpu.make_async_copy(source.at[at], target.at[at], send_sems.at[used]))
                used += 1
            results.append(Result(source, sent))
        kernel(info_ref, *small_refs, *operands, *results, *refs)
        for i in range(len(copies)):
            stream.need(i)
        for result in results:
            result.finish()

    arrays = [in_hbm(a) if pieces else in_vmem(a) for a, _, pieces in big]
    arrays += list(after) + ([in_hbm(alias)] if alias is not None else [])
    return pl.pallas_call(
        body,
        out_shape=[(pltpu.HBM if pieces else pltpu.VMEM)(o.shape, o.dtype) for o, pieces in outs],
        in_specs=[SMEM]
        + [VMEM] * len(small)
        + [HBM if pieces else VMEM for _, _, pieces in big]
        + [ANY] * len(after)
        + [HBM] * (alias is not None),
        out_specs=[HBM if pieces else VMEM for _, pieces in outs],
        scratch_shapes=held + list(scratch),
        input_output_aliases={len(small) + len(arrays): 0} if alias is not None else {},
        compiler_params=pltpu.CompilerParams(vmem_limit_bytes=limit << 20),
        cost_estimate=pl.CostEstimate(flops=flops, bytes_accessed=moved, transcendentals=exps),
    )(info, *small, *arrays)


def shape(*dims):
    return jax.ShapeDtypeStruct(dims, BF16)


def tie(values, *after, hbm=False):
    count = len(values)
    space, spec, pin = (pltpu.HBM, HBM, in_hbm) if hbm else (pltpu.VMEM, VMEM, in_vmem)
    return pl.pallas_call(
        lambda *refs: None,
        out_shape=[space(value.shape, value.dtype) for value in values],
        in_specs=[spec] * count + [ANY] * len(after),
        out_specs=[spec] * count,
        input_output_aliases={i: i for i in range(count)},
        compiler_params=pltpu.CompilerParams(vmem_limit_bytes=4 << 20),
    )(*(pin(value) for value in values), *after)


def staged(array, start, count, after):
    def body(source, _, target, sem):
        copy = pltpu.make_async_copy(source.at[:, pl.ds(start, count)], target, sem)
        copy.start()
        copy.wait()

    return pl.pallas_call(
        body,
        out_shape=pltpu.VMEM((array.shape[0], count), array.dtype),
        in_specs=[HBM, ANY],
        out_specs=VMEM,
        scratch_shapes=[pltpu.SemaphoreType.DMA],
        compiler_params=pltpu.CompilerParams(vmem_limit_bytes=4 << 20),
        cost_estimate=pl.CostEstimate(
            flops=0, bytes_accessed=4 * array.shape[0] * count, transcendentals=0
        ),
    )(in_hbm(array), after)


def peer_rows(ref, me):
    return flat_rows(jnp.stack([ref[r ^ me] for r in range(ref.shape[0])]))


def dispatch_kernel(experts, cap, info_ref, ids, tokens, out):
    place = slot_rows(ids.whole()[info_ref[0]], experts, cap).astype(BF16)
    out.held[...] = dot(place, tokens.whole()[...]).astype(BF16)
    out.send(0)


def collect_kernel(experts, cap, info_ref, ids_ref, rows, out):
    place = slot_rows(ids_ref[info_ref[0]], experts, cap).T.astype(BF16)
    out.held[...] = dot(place, rows.whole()[...]).astype(BF16)
    out.send(0)


def side_kernel(experts, cap, info_ref, ids_ref, near, out):
    place = slot_rows(ids_ref[info_ref[0]], experts, cap).T.astype(BF16)
    rows_ref = near.whole()
    for i in range(2):
        rows = flat_rows(rows_ref[:, i])
        out.held[:, i * LANES : (i + 1) * LANES] = dot(place, rows).astype(BF16)
    out.send(0)


def project_rows(places, experts, cap, rows, weight, out, tile):
    chans = weight.held.shape[1]
    rows = [flat_rows(block.whole()[...]) for block in rows]
    for lo in range(0, chans, tile):
        part = weight.whole()[:, lo : lo + tile]
        for at, block in zip(places, rows):
            store_rows(out, at, lo, dot(block, part), experts, cap)
        out.send(lo // tile)


def store_rows(out, at, lo, made, experts, cap):
    made = made.astype(BF16)
    for e in range(experts):
        out.held[e, at, :, lo : lo + made.shape[1]] = made[e * cap : (e + 1) * cap, :]


def own_kernel(experts, cap, tile, info_ref, rows, weight, states, *refs):
    steps, out = refs[:-1], refs[-1]
    chans = weight.held.shape[1]
    project_rows([0], experts, cap, [rows], weight, out, tile)
    first = flat_rows(rows.whole()[...])
    store_rows(out, 0, chans, dot(first, states.whole()[...]), experts, cap)
    steps = [ref.whole()[...].astype(F32) for ref in steps]
    spare = LANES - sum(part.shape[0] for part in steps)
    steps.append(jnp.zeros((spare, steps[0].shape[1]), F32))
    steps = jnp.concatenate(steps, axis=0).astype(BF16)
    made = lax.dot_general(first, steps, (((1,), (1,)), ((), ())), preferred_element_type=F32)
    store_rows(out, 1, chans, made, experts, cap)
    out.send(chans // tile)


def project_kernel(places, experts, cap, tile, info_ref, *refs):
    rows, weight, out = refs[: len(places)], refs[-2], refs[-1]
    project_rows(places, experts, cap, rows, weight, out, tile)


def peers_kernel(places, experts, cap, tile, info_ref, *refs):
    weight, outs = refs[places], refs[places + 1 :]
    me = info_ref[info_ref.shape[0] - 1]
    rows = [peer_rows(ref.whole(), me) for ref in refs[:places]]
    for lo in range(0, weight.held.shape[1], tile):
        part = weight.whole()[:, lo : lo + tile]
        for at in range(places):
            made = dot(rows[at], part).astype(BF16)
            for r in range(experts):
                outs[r].held[at, :, lo : lo + tile] = made[r * cap : (r + 1) * cap, :]
    for out in outs:
        out.send(0)


def gate_kernel(tile, by_peer, info_ref, *refs):
    count = len(refs) // 2
    weight, outs = refs[count], refs[count + 1 :]
    if by_peer:
        rows = [peer_rows(ref.whole(), info_ref[info_ref.shape[0] - 1]) for ref in refs[:count]]
    else:
        rows = [flat_rows(ref.whole()[...]) for ref in refs[:count]]
    for lo in range(0, weight.held.shape[1], tile):
        part = weight.whole()[:, lo : lo + tile]
        for block, out in zip(rows, outs):
            out.held[:, lo : lo + tile] = dot(block, part).astype(BF16)
    for out in outs:
        out.send(0)


def output_kernel(at, experts, cap, tile, info_ref, *refs):
    scanned, gate, weight, out = refs[:-3], refs[-3], refs[-2].held, refs[-1].held
    if len(scanned) > 1:
        me = info_ref[info_ref.shape[0] - 1]
        rows = flat_rows(jnp.stack([ref.held[at] for ref in scanned]))
    else:
        me = 0
        rows = flat_rows(scanned[0].held[:, at])
    gates = jax.nn.silu(gate.whole()[...].astype(F32))
    gated = (rows.astype(F32) * gates).astype(BF16)
    for lo in range(0, weight.shape[1], tile):
        made = dot(gated, weight[:, lo : lo + tile]).astype(BF16)
        for r in range(experts):
            out[r ^ me, :, lo : lo + tile] = made[r * cap : (r + 1) * cap, :]


def factors_kernel(cfg, info_ref, ids_ref, head_ref, near, side, weights, kept, tail, last, placed):
    experts, cap, tok_rows, nstate, chn, heads = cfg
    blocks = ids_ref.shape[0]
    lower = iota((tok_rows, tok_rows), 0) >= iota((tok_rows, tok_rows), 1)
    ones = jnp.where(lower, 1.0, 0.0)
    first = iota((tok_rows, LANES), 1) < HEAD_DIM
    spread = jnp.where(
        iota((2 * LANES, chn), 0) % LANES == iota((2 * LANES, chn), 1) // HEAD_DIM, 1.0, 0.0
    ).astype(BF16)
    for q in range(2):
        place = slot_rows(ids_ref[info_ref[1 + q]], experts, cap).T.astype(BF16)
        placed.held[q] = dot(place, flat_rows(near.whole()[:, q, :, :chn])).astype(BF16)
    placed.send(0)
    side_ref = side.whole()
    for b in range(blocks):
        q = info_ref[1 + blocks + b]
        own_head = iota((LANES, LANES), 0) == iota((LANES, LANES), 1) + info_ref[
            1 + 2 * blocks + b
        ] * heads
        own_head = jnp.where(own_head & (iota((LANES, LANES), 1) < heads), 1.0, 0.0)
        raw = dot(side_ref[q, :, LANES:], own_head.astype(BF16))
        step = jax.nn.softplus(raw + head_ref[0:1, :])
        summed = jnp.dot(
            ones,
            step * head_ref[1:2, :],
            preferred_element_type=F32,
            precision=lax.Precision.HIGHEST,
        )
        source = summed - jnp.log(step)
        source_t = source.T
        left = jnp.exp(summed[tok_rows - 1 :, :] - source)
        high = left.astype(BF16)
        low = (left - high.astype(F32)).astype(BF16)
        tail.held[b] = dot(jnp.concatenate([high, low], axis=1), spread).astype(BF16)
        tail.send(b)

        both = side_ref[q, :, :LANES]
        keys_t = both.astype(F32).T.astype(BF16)[:nstate, :]
        scores = dot(both[:, nstate:], keys_t)
        for pair in range(heads // 2):
            lanes = slice(pair * LANES, (pair + 1) * LANES)
            wide = []
            for h in (2 * pair, 2 * pair + 1):
                wide.append(jnp.broadcast_to(summed[:, h : h + 1], (tok_rows, tok_rows)))
                gaps = wide[-1] - source_t[h : h + 1, :]
                decay = jnp.exp(jnp.where(lower, gaps, -jnp.inf))
                at = (h % 2) * tok_rows
                weights.held[b, pair, :, at : at + tok_rows] = (scores * decay).astype(BF16)
            both_wide = jnp.exp(jnp.where(first, wide[0], wide[1]))
            kept.held[b, :, lanes] = both_wide.astype(BF16)
            last.held[b, :, lanes] = both_wide[tok_rows - 8 :, :]
        weights.send(b)
        kept.send(b)
        last.send(b)


def scan_kernel(
    cfg,
    info_ref,
    ids_ref,
    chan_ref,
    side,
    placed,
    *refs,
):
    experts, cap, tok_rows, nstate, chn, heads = cfg
    far, refs = refs[:experts], refs[experts:]
    weights, kept, tail, last = refs[:4]
    out_near, (out_far, inner_ref, made_ref) = refs[4 : 4 + experts], refs[4 + experts :]
    me = info_ref[info_ref.shape[0] - 1]
    blocks = ids_ref.shape[0]
    taps = 4
    inner_ref[:8, :] = jnp.zeros((8, chn), F32)

    for q in range(blocks):
        b = info_ref[1 + q]
        at = pl.ds(8 + b * tok_rows, tok_rows)
        if q < 2:
            inner_ref[at, :] = placed.whole()[q].astype(F32)
        else:
            place = slot_rows(ids_ref[b], experts, cap, me).T.astype(BF16)
            rows = jnp.stack([far[r].whole()[q - 2] for r in range(experts)])
            inner_ref[at, :] = dot(place, flat_rows(rows))

    first = iota((tok_rows, LANES), 1) < HEAD_DIM
    state = jnp.zeros((nstate, chn), F32)
    side_ref = side.whole()
    for b in range(blocks):
        q = info_ref[1 + blocks + b]
        total = chan_ref[taps : taps + 1, :]
        for j in range(taps):
            start = 8 + b * tok_rows - (taps - 1) + j
            total = total + chan_ref[j : j + 1, :] * inner_ref[start : start + tok_rows, :]
        signal = jax.nn.silu(total)

        both = side_ref[q, :, :LANES]
        keys_t = both.astype(F32).T.astype(BF16)[:nstate, :]
        rest = chan_ref[taps + 1 : taps + 2, :] * signal
        if b > 0:
            carried = dot(both[:, nstate:], state.astype(BF16))
            rest = rest + carried * kept.held[b].astype(F32)
        if b < blocks - 1:
            added = dot(keys_t, (signal * tail.held[b].astype(F32)).astype(BF16))
            state = last.held[b, 7:8, :] * state + added

        for pair in range(heads // 2):
            lanes = slice(pair * LANES, (pair + 1) * LANES)
            values = signal[:, lanes]
            values = jnp.concatenate(
                [jnp.where(first, values, 0.0), jnp.where(first, 0.0, values)], axis=0
            ).astype(BF16)
            local = dot(weights.held[b, pair], values)
            made_ref[b * tok_rows : (b + 1) * tok_rows, lanes] = (rest[:, lanes] + local).astype(BF16)

    for q in range(blocks - 1, -1, -1):
        b = info_ref[1 + q]
        place = slot_rows(ids_ref[b], experts, cap, me if q < 2 else 0).astype(BF16)
        start = pl.multiple_of(b * tok_rows, tok_rows)
        leaving = dot(place, made_ref[pl.ds(start, tok_rows), :]).astype(BF16)
        for e in range(experts):
            piece = leaving[e * cap : (e + 1) * cap, :]
            if q < 2:
                out_near[e].held[q] = piece
            else:
                out_far.held[e, q - 2] = piece


def per_device(
    tokens,
    route,
    w_inner,
    w_state,
    w_step,
    step_bias,
    decay_log,
    skip_gain,
    conv_weight,
    conv_bias,
    w_out,
):
    tok_rows, width = tokens.shape[1], tokens.shape[2]
    experts = lax.axis_size("expert")
    shards = lax.axis_size("context")
    cap = 2 * tok_rows // experts
    slots = experts * cap
    chans = w_inner.shape[3]
    heads = w_step.shape[2]
    nstate = w_state.shape[2] // 2
    chips = shards // 2
    far_count = shards - 2

    here = lax.axis_index("context").astype(jnp.int32)
    blocks = jnp.arange(shards, dtype=jnp.int32)
    order = 2 * ((here // 2 - blocks // 2) % chips) + ((here % 2) ^ (blocks % 2))
    groups = 2 * ((blocks // 2 - here // 2) % chips) + ((here % 2) ^ (blocks % 2))
    block_at = 2 * ((here // 2 - blocks // 2) % chips) + ((here % 2) ^ (blocks % 2))
    me = lax.axis_index("expert").astype(jnp.int32)
    info = jnp.concatenate([here[None], block_at, order, groups, me[None]])
    ids = route.reshape(shards, 1, tok_rows)
    swap = [(c, c ^ 1) for c in range(shards)]

    def hop(k):
        return [(c, ((c // 2 + k) % chips) * 2 + c % 2) for c in range(shards)]

    def permute(value, pairs):
        return lax.ppermute(value, "context", pairs)

    def spread(value):
        made = [value, permute(value, swap)]
        for k in range(1, chips):
            arrived = permute(value, hop(k))
            made += [arrived, permute(arrived, swap)]
        return made

    def exchange(value):
        return lax.all_to_all(value, "expert", split_axis=0, concat_axis=0, tiled=True)

    def exchange_peers(pieces):
        sent = [
            lax.ppermute(pieces[r], "expert", [(e, e ^ r) for e in range(experts)])
            for r in range(experts - 1, 0, -1)
        ]
        return [pieces[0]] + sent[::-1]

    w_flat = w_inner[0].reshape(width, 2 * chans)

    once = [Ellipsis]
    outgoing = call(
        functools.partial(dispatch_kernel, experts, cap),
        info, [full(ids), full(tokens[0])], [(shape(slots, width), once)],
        flops=2 * slots * tok_rows * width,
    )[0]
    own = exchange(outgoing.reshape(experts, cap, width))
    steps = spread(tie([w_step[0]], outgoing)[0].T)
    own = tie([own], w_flat, *steps)[0]
    w_in = staged(w_flat, chans, chans, own)
    swapped = permute(own, swap)
    everything = (slice(None),) * 3

    def inner_cuts(place, extra):
        at = (slice(None), place, slice(None))
        cuts = [at + (pl.ds(lo, 256),) for lo in range(0, chans, 256)]
        return cuts + [everything + (pl.ds(chans, LANES),)] * extra

    near_shape = shape(experts, 2, cap, chans + LANES)
    own_part = call(
        functools.partial(own_kernel, experts, cap, 256),
        info,
        [kept_in_vmem(own), kept_in_vmem(w_in), full(w_state[0])]
        + [full(part) for part in steps],
        [(near_shape, inner_cuts(0, 1))],
        flops=2 * slots * width * (chans + 2 * LANES),
    )[0]
    near = call(
        functools.partial(project_kernel, [1], experts, cap, 256),
        info,
        [kept_in_vmem(swapped), kept_in_vmem(w_in)],
        [(near_shape, inner_cuts(1, 0))],
        alias=own_part,
        flops=2 * slots * width * chans,
    )[0]
    distant = []
    for k in range(1, chips):
        arrived = tie([permute(own, hop(k))], near, hbm=True)[0]
        distant += [arrived, permute(arrived, swap)]
    far = call(
        functools.partial(peers_kernel, far_count, experts, cap, 256),
        info,
        [full(rows) for rows in distant] + [columns(w_flat, chans, chans)],
        [(shape(far_count, cap, chans), once)] * experts,
        flops=2 * far_count * slots * width * chans,
    )
    near_back = exchange(near)
    far_back = exchange_peers(far)

    def gates(rows, by_peer):
        return call(
            functools.partial(gate_kernel, 256, by_peer),
            info,
            [kept_in_vmem(part) if by_peer else full(part) for part in rows]
            + [columns(w_flat, 0, chans)],
            [(shape(slots, chans), once)] * len(rows),
            after=[near],
            flops=2 * len(rows) * slots * width * chans,
        )

    gate_near = gates([own, swapped], True)
    gate_far = gates(distant, False)
    out_weight = staged(w_out[0], 0, width, near_back)

    lanes = everything + (pl.ds(chans, LANES),)
    side = call(
        functools.partial(side_kernel, experts, cap),
        info,
        [(near_back, (experts, 2, cap, LANES), [(lanes, Ellipsis)])],
        [(shape(tok_rows, 2 * LANES), once)],
        small=[ids],
        after=[far[0], gate_near[0], gate_far[0]],
        flops=2 * slots * tok_rows * 2 * LANES,
    )[0]
    sides = jnp.stack(spread(side))

    def padded_heads(row):
        return jnp.pad(row, (0, LANES - heads))[None, :]

    head_rows = jnp.concatenate(
        [padded_heads(step_bias), padded_heads(-jnp.exp(decay_log)), jnp.zeros((6, LANES), F32)]
    )
    chan_rows = jnp.concatenate(
        [conv_weight, conv_bias[None, :], jnp.repeat(skip_gain, HEAD_DIM)[None, :]]
    )
    chan_rows = jnp.pad(chan_rows, ((0, 2), (0, 0)))
    cfg = (experts, cap, tok_rows, nstate, chans, heads)
    each = list(range(shards))
    weights, kept, tail, last, placed = call(
        functools.partial(factors_kernel, cfg),
        info, [full(near_back), kept_in_vmem(sides)],
        [
            (shape(shards, heads // 2, tok_rows, 2 * tok_rows), None),
            (shape(shards, tok_rows, chans), None),
            (shape(shards, tok_rows, chans), None),
            (jax.ShapeDtypeStruct((shards, 8, chans), F32), None),
            (shape(2, tok_rows, chans), None),
        ],
        small=[ids, head_rows],
        flops=2 * tok_rows * chans * (2 * slots + shards * 512),
        exps=shards * tok_rows * tok_rows * heads,
    )
    *near_out, far_out = call(
        functools.partial(scan_kernel, cfg),
        info,
        [kept_in_vmem(sides), kept_in_vmem(placed)]
        + [full(piece) for piece in far_back]
        + [kept_in_vmem(array) for array in (weights, kept, tail, last)],
        [(shape(2, cap, chans), None)] * experts
        + [(shape(experts, far_count, cap, chans), None)],
        small=[ids, chan_rows],
        after=[gate_far[0], gate_near[0], out_weight],
        scratch=[
            pltpu.VMEM((8 + shards * tok_rows, chans), F32),
            pltpu.VMEM((shards * tok_rows, chans), BF16),
        ],
        flops=2 * shards * tok_rows * chans * (2 * slots + 2 * nstate + 2 * tok_rows),
    )
    far_ret = exchange(far_out)
    near_ret = exchange_peers(tie(near_out, far_ret))

    def output(scanned, gate, at, after=()):
        return call(
            functools.partial(output_kernel, at, experts, cap, 512),
            info,
            [kept_in_vmem(part) for part in scanned] + [full(gate), kept_in_vmem(out_weight)],
            [(shape(experts, cap, width), None)],
            after=after,
            flops=2 * slots * width * chans,
        )[0]

    hopped = []
    others = [permute(output([far_ret], gate_far[2 * k - 1], 2 * k - 1), swap) for k in range(1, chips)]
    for k in range(1, chips):
        pair = output([far_ret], gate_far[2 * k - 2], 2 * k - 2).astype(F32) + others[k - 1].astype(F32)
        hopped.append(permute(pair.astype(BF16), hop(chips - k)))
    part_swap = permute(output(near_ret, gate_near[1], 1), swap)
    part_own = output(near_ret, gate_near[0], 0, hopped)
    summed = part_own.astype(F32) + part_swap.astype(F32)
    for part in hopped:
        summed = summed + part.astype(F32)
    returned = exchange(summed.astype(BF16)).reshape(slots, width)
    result = call(
        functools.partial(collect_kernel, experts, cap),
        info, [kept_in_vmem(returned)], [(shape(tok_rows, width), once)],
        small=[ids],
        flops=2 * slots * tok_rows * width,
    )[0]
    return result[None]


def solution(mesh):
    in_specs = (
        P("expert", "context", None),
        P("expert", None, None),
        P("expert", None, None, "context"),
        P("expert", None, None),
        P("expert", None, "context"),
        P("context"),
        P("context"),
        P("context"),
        P(None, "context"),
        P("context"),
        P("expert", "context", None),
    )
    out_specs = P("expert", "context", None)
    return jax.shard_map(
        per_device, mesh=mesh, in_specs=in_specs, out_specs=out_specs, check_vma=False
    )
```

```python
import functools

import jax
import jax.numpy as jnp
from jax import lax
from jax.experimental import pallas as pl
from jax.experimental.pallas import tpu as pltpu
from jax.sharding import PartitionSpec as P

HEAD_DIM = 64
LANES = 128
BF16 = jnp.bfloat16
F32 = jnp.float32


def iota(shape, axis):
    return lax.broadcasted_iota(jnp.int32, shape, axis)


def dot(a, b):
    return jnp.dot(a, b, preferred_element_type=F32)


def flat_rows(pieces):
    count, rows, lanes = pieces.shape
    if rows % 16:
        return pieces.astype(F32).reshape(count * rows, lanes).astype(BF16)
    return pieces.reshape(count * rows, lanes)


def slot_rows(ids, experts, cap, me=0):
    tok_rows = ids.shape[1]
    onehot = jnp.where(iota((experts, tok_rows), 0) == ids, 1.0, 0.0)
    upto = jnp.where(iota((tok_rows, tok_rows), 0) <= iota((tok_rows, tok_rows), 1), 1.0, 0.0)
    before = dot(onehot.astype(BF16), upto.astype(BF16))
    rank = jnp.sum(onehot * before, axis=0, keepdims=True) - 1.0
    slot = (ids ^ me) * cap + rank.astype(jnp.int32)
    return jnp.where(iota((experts * cap, tok_rows), 0) == slot, 1.0, 0.0)


VMEM = pl.BlockSpec(memory_space=pltpu.VMEM)
SMEM = pl.BlockSpec(memory_space=pltpu.SMEM)
HBM = pl.BlockSpec(memory_space=pltpu.HBM)


class Stream:
    def __init__(self, copies, ahead):
        self.copies, self.ahead, self.started, self.done = copies, ahead, 0, set()
        self.start(ahead)

    def start(self, upto):
        while self.started < min(upto, len(self.copies)):
            self.copies[self.started].start()
            self.started += 1

    def need(self, i):
        self.start(i + self.ahead)
        if i not in self.done:
            self.copies[i].wait()
            self.done.add(i)


class Operand:
    def __init__(self, held, stream=None, first=0, count=0):
        self.held, self.stream, self.first, self.count = held, stream, first, count

    def piece(self, t):
        if self.stream:
            self.stream.need(self.first + t)
        return self.held

    def whole(self):
        for t in range(self.count):
            self.piece(t)
        return self.held


class Result:
    def __init__(self, held, copies=()):
        self.held, self.copies = held, copies

    def send(self, t):
        if self.copies:
            self.copies[t].start()

    def finish(self):
        for copy in self.copies:
            copy.wait()


def in_hbm(array):
    return pltpu.with_memory_space_constraint(array, pltpu.HBM)


def in_vmem(array):
    return pltpu.with_memory_space_constraint(array, pltpu.VMEM)


def kept_in_vmem(array):
    return (array, None, None)


def full(array):
    return (array, array.shape, [(Ellipsis, Ellipsis)])


def firsts(array):
    return (array, array.shape, [(t, t) for t in range(array.shape[0])])


def columns(array, start, count):
    return (array, (array.shape[0], count), [((slice(None), pl.ds(start, count)), Ellipsis)])


def call(
    kernel, info, big, outs, small=(), after=(), after_vmem=(), passed=(), scratch=(), flops=0, exps=0, limit=32
):
    moved = sum(2 * a.size for a, _, _ in big) + sum(2 * o.size for o, _ in outs)
    held = []
    for array, dims, pieces in big:
        if pieces:
            held.append(pltpu.VMEM(dims, array.dtype))
    for out, pieces in outs:
        if pieces:
            held.append(pltpu.VMEM(out.shape, out.dtype))
    fetches = sum(len(pieces or ()) for _, _, pieces in big)
    sends = sum(len(pieces or ()) for _, pieces in outs)
    held += [pltpu.SemaphoreType.DMA((max(count, 1),)) for count in (fetches, sends, len(passed))]

    def body(*refs):
        refs = list(refs)

        def take(count):
            taken = refs[:count]
            del refs[:count]
            return taken

        info_ref = take(1)[0]
        small_refs, big_refs = take(len(small)), take(len(big))
        take(len(after) + len(after_vmem))
        pass_refs = take(len(passed))
        out_refs, passed_refs = take(len(outs)), take(len(passed))
        held_refs = [take(1)[0] if pieces else ref for ref, (_, _, pieces) in zip(big_refs, big)]
        made_refs = [take(1)[0] if pieces else ref for ref, (_, pieces) in zip(out_refs, outs)]
        fetch_sems, send_sems, pass_sems = take(3)
        copies, spans = [], []
        for source, target, (_, _, pieces) in zip(big_refs, held_refs, big):
            spans.append((len(copies), len(pieces or ())))
            for there, here in pieces or ():
                sem = fetch_sems.at[len(copies)]
                copies.append(pltpu.make_async_copy(source.at[there], target.at[here], sem))
        stream = Stream(copies, 3)
        passing = [
            pltpu.make_async_copy(source, target, pass_sems.at[i])
            for i, (source, target) in enumerate(zip(pass_refs, passed_refs))
        ]
        for copy in passing:
            copy.start()
        operands = [
            Operand(ref, stream if count else None, at, count)
            for ref, (at, count) in zip(held_refs, spans)
        ]
        results, used = [], 0
        for target, source, (_, pieces) in zip(out_refs, made_refs, outs):
            sent = []
            for at in pieces or ():
                sent.append(pltpu.make_async_copy(source.at[at], target.at[at], send_sems.at[used]))
                used += 1
            results.append(Result(source, sent))
        kernel(info_ref, *small_refs, *operands, *results, *refs)
        for i in range(len(copies)):
            stream.need(i)
        for result in results:
            result.finish()
        for copy in passing:
            copy.wait()

    arrays = [in_hbm(a) if pieces else in_vmem(a) for a, _, pieces in big]
    arrays += [in_hbm(array) for array in after] + [in_vmem(array) for array in after_vmem]
    arrays += [in_hbm(array) for array in passed]
    return pl.pallas_call(
        body,
        out_shape=[(pltpu.HBM if pieces else pltpu.VMEM)(o.shape, o.dtype) for o, pieces in outs]
        + [pltpu.VMEM(array.shape, array.dtype) for array in passed],
        in_specs=[SMEM]
        + [VMEM] * len(small)
        + [HBM if pieces else VMEM for _, _, pieces in big]
        + [HBM] * len(after)
        + [VMEM] * len(after_vmem)
        + [HBM] * len(passed),
        out_specs=[HBM if pieces else VMEM for _, pieces in outs] + [VMEM] * len(passed),
        scratch_shapes=held + list(scratch),
        compiler_params=pltpu.CompilerParams(vmem_limit_bytes=limit << 20),
        cost_estimate=pl.CostEstimate(flops=flops, bytes_accessed=moved, transcendentals=exps),
    )(info, *small, *arrays)


def shape(*dims):
    return jax.ShapeDtypeStruct(dims, BF16)


def tie(values, after=(), after_vmem=(), hbm=False):
    count = len(values)
    space, spec, pin = (pltpu.HBM, HBM, in_hbm) if hbm else (pltpu.VMEM, VMEM, in_vmem)
    return pl.pallas_call(
        lambda *refs: None,
        out_shape=[space(value.shape, value.dtype) for value in values],
        in_specs=[spec] * count + [HBM] * len(after) + [VMEM] * len(after_vmem),
        out_specs=[spec] * count,
        input_output_aliases={i: i for i in range(count)},
        compiler_params=pltpu.CompilerParams(vmem_limit_bytes=4 << 20),
    )(
        *(pin(value) for value in values),
        *(in_hbm(array) for array in after),
        *(in_vmem(array) for array in after_vmem),
    )


def staged(array, start, count, after):
    def body(source, _, target, sem):
        copy = pltpu.make_async_copy(source.at[:, pl.ds(start, count)], target, sem)
        copy.start()
        copy.wait()

    return pl.pallas_call(
        body,
        out_shape=pltpu.VMEM((array.shape[0], count), array.dtype),
        in_specs=[HBM, VMEM],
        out_specs=VMEM,
        scratch_shapes=[pltpu.SemaphoreType.DMA],
        compiler_params=pltpu.CompilerParams(vmem_limit_bytes=4 << 20),
        cost_estimate=pl.CostEstimate(
            flops=0, bytes_accessed=4 * array.shape[0] * count, transcendentals=0
        ),
    )(in_hbm(array), in_vmem(after))


def peer_rows(ref, me):
    return flat_rows(jnp.stack([ref[r ^ me] for r in range(ref.shape[0])]))


def dispatch_kernel(experts, cap, info_ref, ids, tokens, out):
    place = slot_rows(ids.whole()[info_ref[0]], experts, cap).astype(BF16)
    out.held[...] = dot(place, tokens.whole()[...]).astype(BF16)
    out.send(0)


def collect_kernel(experts, cap, info_ref, ids_ref, rows, out):
    place = slot_rows(ids_ref[info_ref[0]], experts, cap).T.astype(BF16)
    out.held[...] = dot(place, rows.whole()[...]).astype(BF16)
    out.send(0)


def side_kernel(experts, cap, info_ref, ids_ref, near, out):
    place = slot_rows(ids_ref[info_ref[0]], experts, cap).T.astype(BF16)
    rows_ref = near.whole()
    for i in range(2):
        rows = flat_rows(rows_ref[:, i])
        out.held[:, i * LANES : (i + 1) * LANES] = dot(place, rows).astype(BF16)
    out.send(0)


def project_kernel(places, experts, cap, tile, info_ref, *refs):
    rows, weight, sides, out = refs[:places], refs[places], refs[places + 1 : -1], refs[-1]
    chans = weight.held.shape[1]

    def store(at, lo, made):
        made = made.astype(BF16)
        for e in range(experts):
            out.held[e, at, :, lo : lo + made.shape[1]] = made[e * cap : (e + 1) * cap, :]

    for lo in range(0, chans, tile):
        for at in range(places):
            block = flat_rows(rows[at].whole()[...])
            store(at, lo, dot(block, weight.whole()[:, lo : lo + tile]))
    if sides:
        first = flat_rows(rows[0].whole()[...])
        store(0, chans, dot(first, sides[0].whole()[...]))
        steps = [ref.whole()[...].astype(F32) for ref in sides[1:]]
        spare = LANES - sum(part.shape[0] for part in steps)
        steps.append(jnp.zeros((spare, steps[0].shape[1]), F32))
        steps = jnp.concatenate(steps, axis=0).astype(BF16)
        made = lax.dot_general(
            first, steps, (((1,), (1,)), ((), ())), preferred_element_type=F32
        )
        store(1, chans, made)
    out.send(0)


def gate_kernel(tile, by_peer, info_ref, *refs):
    count = len(refs) // 2
    weight, outs = refs[count], refs[count + 1 :]
    if by_peer:
        rows = [peer_rows(ref.whole(), info_ref[info_ref.shape[0] - 1]) for ref in refs[:count]]
    else:
        rows = [flat_rows(ref.whole()[...]) for ref in refs[:count]]
    for lo in range(0, weight.held.shape[1], tile):
        part = weight.whole()[:, lo : lo + tile]
        for block, out in zip(rows, outs):
            out.held[:, lo : lo + tile] = dot(block, part).astype(BF16)
    for out in outs:
        out.send(0)


def output_kernel(at, experts, cap, tile, info_ref, *refs):
    scanned, gate, weight, out = refs[:-3], refs[-3], refs[-2].held, refs[-1].held
    if len(scanned) > 1:
        me = info_ref[info_ref.shape[0] - 1]
        rows = flat_rows(jnp.stack([ref.held[at] for ref in scanned]))
    else:
        me = 0
        rows = flat_rows(scanned[0].held[:, at])
    gates = jax.nn.silu(gate.whole()[...].astype(F32))
    gated = (rows.astype(F32) * gates).astype(BF16)
    for lo in range(0, weight.shape[1], tile):
        made = dot(gated, weight[:, lo : lo + tile]).astype(BF16)
        for r in range(experts):
            out[r ^ me, :, lo : lo + tile] = made[r * cap : (r + 1) * cap, :]


def scan_kernel(
    cfg,
    info_ref,
    ids_ref,
    head_ref,
    chan_ref,
    near,
    side,
    far,
    *refs,
):
    experts, cap, tok_rows, nstate, chn, heads = cfg
    blocks = ids_ref.shape[0]
    taps = 4
    out_near, (out_far, inner_ref, made_ref) = refs[:experts], refs[experts:]
    me = info_ref[info_ref.shape[0] - 1]
    near_ref, far_ref, side_ref = near.whole(), far.whole(), side.whole()
    inner_ref[:8, :] = jnp.zeros((8, chn), F32)

    for q in range(blocks):
        b = info_ref[1 + q]
        place = slot_rows(ids_ref[b], experts, cap).T.astype(BF16)
        rows = flat_rows(near_ref[:, q, :, :chn] if q < 2 else far_ref[:, q - 2])
        inner_ref[pl.ds(8 + b * tok_rows, tok_rows), :] = dot(place, rows)

    lower = iota((tok_rows, tok_rows), 0) >= iota((tok_rows, tok_rows), 1)
    ones = jnp.where(lower, 1.0, 0.0)
    first = iota((tok_rows, LANES), 1) < HEAD_DIM
    spread = jnp.where(
        iota((2 * LANES, chn), 0) % LANES == iota((2 * LANES, chn), 1) // HEAD_DIM, 1.0, 0.0
    ).astype(BF16)

    def widen(values):
        high = values.astype(BF16)
        low = (values - high.astype(F32)).astype(BF16)
        return dot(jnp.concatenate([high, low], axis=1), spread)

    state = jnp.zeros((nstate, chn), F32)
    for b in range(blocks):
        q = info_ref[1 + blocks + b]
        total = chan_ref[taps : taps + 1, :]
        for j in range(taps):
            start = 8 + b * tok_rows - (taps - 1) + j
            total = total + chan_ref[j : j + 1, :] * inner_ref[start : start + tok_rows, :]
        signal = jax.nn.silu(total)

        own_head = iota((LANES, LANES), 0) == iota((LANES, LANES), 1) + info_ref[
            1 + 2 * blocks + b
        ] * heads
        own_head = jnp.where(own_head & (iota((LANES, LANES), 1) < heads), 1.0, 0.0)
        raw = dot(side_ref[q, :, LANES:], own_head.astype(BF16))
        step = jax.nn.softplus(raw + head_ref[0:1, :])
        summed = jnp.dot(
            ones,
            step * head_ref[1:2, :],
            preferred_element_type=F32,
            precision=lax.Precision.HIGHEST,
        )
        source = summed - jnp.log(step)
        source_t = source.T
        kept = widen(jnp.exp(summed))
        tail = widen(jnp.exp(summed[tok_rows - 1 :, :] - source))

        both = side_ref[q, :, :LANES]
        keys_t = both.astype(F32).T.astype(BF16)[:nstate, :]
        queries = both[:, nstate:]
        scores = dot(queries, keys_t)
        rest = chan_ref[taps + 1 : taps + 2, :] * signal
        if b > 0:
            rest = rest + dot(queries, state.astype(BF16)) * kept
        if b < blocks - 1:
            state = kept[tok_rows - 1 :, :] * state + dot(keys_t, (signal * tail).astype(BF16))

        for pair in range(heads // 2):
            lanes = slice(pair * LANES, (pair + 1) * LANES)
            values = signal[:, lanes]
            values = jnp.concatenate(
                [jnp.where(first, values, 0.0), jnp.where(first, 0.0, values)], axis=0
            ).astype(BF16)
            weights = []
            for h in (2 * pair, 2 * pair + 1):
                gaps = summed[:, h : h + 1] - source_t[h : h + 1, :]
                decay = jnp.exp(jnp.where(lower, gaps, -jnp.inf))
                weights.append((scores * decay).astype(BF16))
            local = dot(jnp.concatenate(weights, axis=1), values)
            made_ref[b * tok_rows : (b + 1) * tok_rows, lanes] = (rest[:, lanes] + local).astype(BF16)

    for q in range(blocks):
        b = info_ref[1 + q]
        place = slot_rows(ids_ref[b], experts, cap, me if q < 2 else 0).astype(BF16)
        start = pl.multiple_of(b * tok_rows, tok_rows)
        leaving = dot(place, made_ref[pl.ds(start, tok_rows), :]).astype(BF16)
        for e in range(experts):
            piece = leaving[e * cap : (e + 1) * cap, :]
            if q < 2:
                out_near[e].held[q] = piece
            else:
                out_far.held[e, q - 2] = piece


def per_device(
    tokens,
    route,
    w_inner,
    w_state,
    w_step,
    step_bias,
    decay_log,
    skip_gain,
    conv_weight,
    conv_bias,
    w_out,
):
    tok_rows, width = tokens.shape[1], tokens.shape[2]
    experts = lax.axis_size("expert")
    shards = lax.axis_size("context")
    cap = 2 * tok_rows // experts
    slots = experts * cap
    chans = w_inner.shape[3]
    heads = w_step.shape[2]
    nstate = w_state.shape[2] // 2
    chips = shards // 2
    far_count = shards - 2

    here = lax.axis_index("context").astype(jnp.int32)
    blocks = jnp.arange(shards, dtype=jnp.int32)
    order = 2 * ((here // 2 - blocks // 2) % chips) + ((here % 2) ^ (blocks % 2))
    groups = 2 * ((blocks // 2 - here // 2) % chips) + ((here % 2) ^ (blocks % 2))
    block_at = 2 * ((here // 2 - blocks // 2) % chips) + ((here % 2) ^ (blocks % 2))
    me = lax.axis_index("expert").astype(jnp.int32)
    info = jnp.concatenate([here[None], block_at, order, groups, me[None]])
    ids = route.reshape(shards, 1, tok_rows)
    swap = [(c, c ^ 1) for c in range(shards)]

    def hop(k):
        return [(c, ((c // 2 + k) % chips) * 2 + c % 2) for c in range(shards)]

    def permute(value, pairs):
        return lax.ppermute(value, "context", pairs)

    def spread(value):
        made = [value, permute(value, swap)]
        for k in range(1, chips):
            arrived = permute(value, hop(k))
            made += [arrived, permute(arrived, swap)]
        return made

    def exchange(value):
        return lax.all_to_all(value, "expert", split_axis=0, concat_axis=0, tiled=True)

    def exchange_peers(pieces):
        sent = [
            lax.ppermute(pieces[r], "expert", [(e, e ^ r) for e in range(experts)])
            for r in range(experts - 1, 0, -1)
        ]
        return [pieces[0]] + sent[::-1]

    w_flat = w_inner[0].reshape(width, 2 * chans)

    once = [Ellipsis]
    outgoing = call(
        functools.partial(dispatch_kernel, experts, cap),
        info, [full(ids), full(tokens[0])], [(shape(slots, width), once)],
        flops=2 * slots * tok_rows * width,
    )[0]
    own = exchange(outgoing.reshape(experts, cap, width))
    steps = spread(tie([w_step[0]], [outgoing])[0].T)
    own = tie([own], [w_flat], steps)[0]
    w_in = staged(w_flat, chans, chans, own)
    swapped = permute(own, swap)
    near = call(
        functools.partial(project_kernel, 2, experts, cap, 256),
        info,
        [kept_in_vmem(array) for array in (own, swapped, w_in, w_state[0], *steps)],
        [(shape(experts, 2, cap, chans + LANES), once)],
        flops=4 * slots * width * (chans + LANES),
    )[0]
    distant = []
    for k in range(1, chips):
        arrived = tie([permute(own, hop(k))], [near], hbm=True)[0]
        distant += [arrived, permute(arrived, swap)]
    far = call(
        functools.partial(project_kernel, far_count, experts, cap, 256),
        info,
        [full(rows) for rows in distant] + [columns(w_flat, chans, chans)],
        [(shape(experts, far_count, cap, chans), once)],
        flops=2 * far_count * slots * width * chans,
    )[0]
    near_back = exchange(near)
    far_back = exchange(far)

    def gates(rows, by_peer):
        return call(
            functools.partial(gate_kernel, 256, by_peer),
            info,
            [kept_in_vmem(part) if by_peer else full(part) for part in rows]
            + [columns(w_flat, 0, chans)],
            [(shape(slots, chans), once)] * len(rows),
            after=[near],
            flops=2 * len(rows) * slots * width * chans,
        )

    gate_near = gates([own, swapped], True)
    gate_far = gates(distant, False)

    lanes = (slice(None),) * 3 + (pl.ds(chans, LANES),)
    side = call(
        functools.partial(side_kernel, experts, cap),
        info,
        [(near_back, (experts, 2, cap, LANES), [(lanes, Ellipsis)])],
        [(shape(tok_rows, 2 * LANES), once)],
        small=[ids],
        after=[far, gate_near[0], gate_far[0]],
        flops=2 * slots * tok_rows * 2 * LANES,
    )[0]
    sides = jnp.stack(spread(side))

    def padded_heads(row):
        return jnp.pad(row, (0, LANES - heads))[None, :]

    head_rows = jnp.concatenate(
        [padded_heads(step_bias), padded_heads(-jnp.exp(decay_log)), jnp.zeros((6, LANES), F32)]
    )
    chan_rows = jnp.concatenate(
        [conv_weight, conv_bias[None, :], jnp.repeat(skip_gain, HEAD_DIM)[None, :]]
    )
    chan_rows = jnp.pad(chan_rows, ((0, 2), (0, 0)))
    cfg = (experts, cap, tok_rows, nstate, chans, heads)
    each = list(range(shards))
    made = call(
        functools.partial(scan_kernel, cfg),
        info,
        [full(near_back), kept_in_vmem(sides), kept_in_vmem(far_back)],
        [(shape(2, cap, chans), None)] * experts
        + [(shape(experts, far_count, cap, chans), None)],
        small=[ids, head_rows, chan_rows],
        passed=[w_out[0], *gate_near, *gate_far],
        scratch=[
            pltpu.VMEM((8 + shards * tok_rows, chans), F32),
            pltpu.VMEM((shards * tok_rows, chans), BF16),
        ],
        flops=2 * shards * tok_rows * chans * (2 * slots + 2 * nstate + 2 * tok_rows + 768),
        exps=shards * tok_rows * tok_rows * heads,
    )
    near_out, far_out, out_weight = made[:experts], made[experts], made[experts + 1]
    gate_near, gate_far = made[experts + 2 : experts + 4], made[experts + 4 :]
    far_ret = exchange(far_out)
    def output(scanned, gate, at, after=()):
        return call(
            functools.partial(output_kernel, at, experts, cap, 512),
            info,
            [kept_in_vmem(part) for part in scanned] + [kept_in_vmem(gate), kept_in_vmem(out_weight)],
            [(shape(experts, cap, width), None)],
            after_vmem=after,
            flops=2 * slots * width * chans,
        )[0]

    others = [permute(output([far_ret], gate_far[2 * k - 1], 2 * k - 1), swap) for k in range(1, chips)]
    pairs = []
    for k in range(1, chips):
        pair = output([far_ret], gate_far[2 * k - 2], 2 * k - 2).astype(F32) + others[k - 1].astype(F32)
        pairs.append(pair.astype(BF16))
    hopped = [permute(pair, hop(chips - k)) for k, pair in enumerate(pairs, 1)]
    near_out = tie(near_out, after_vmem=[far_ret])
    cut = experts // 2
    near_out = tie(near_out[:cut], after_vmem=pairs) + near_out[cut:]
    near_ret = exchange_peers(near_out)
    part_swap = permute(output(near_ret, gate_near[1], 1), swap)
    part_own = output(near_ret, gate_near[0], 0, hopped)
    summed = part_own.astype(F32) + part_swap.astype(F32)
    for part in hopped:
        summed = summed + part.astype(F32)
    returned = exchange(summed.astype(BF16)).reshape(slots, width)
    result = call(
        functools.partial(collect_kernel, experts, cap),
        info, [kept_in_vmem(returned)], [(shape(tok_rows, width), once)],
        small=[ids],
        flops=2 * slots * tok_rows * width,
    )[0]
    return result[None]


def solution(mesh):
    in_specs = (
        P("expert", "context", None),
        P("expert", None, None),
        P("expert", None, None, "context"),
        P("expert", None, None),
        P("expert", None, "context"),
        P("context"),
        P("context"),
        P("context"),
        P(None, "context"),
        P("context"),
        P("expert", "context", None),
    )
    out_specs = P("expert", "context", None)
    return jax.shard_map(
        per_device, mesh=mesh, in_specs=in_specs, out_specs=out_specs, check_vma=False
    )
```

```python
import functools

import jax
import jax.numpy as jnp
from jax import lax
from jax.experimental import pallas as pl
from jax.experimental.pallas import tpu as pltpu
from jax.sharding import PartitionSpec as P

HEAD_DIM = 64
LANES = 128
BF16 = jnp.bfloat16
F32 = jnp.float32


def iota(shape, axis):
    return lax.broadcasted_iota(jnp.int32, shape, axis)


def dot(a, b):
    return jnp.dot(a, b, preferred_element_type=F32)


def flat_rows(pieces):
    count, rows, lanes = pieces.shape
    if rows % 16:
        return pieces.astype(F32).reshape(count * rows, lanes).astype(BF16)
    return pieces.reshape(count * rows, lanes)


def slot_rows(ids, experts, cap):
    tok_rows = ids.shape[1]
    onehot = jnp.where(iota((experts, tok_rows), 0) == ids, 1.0, 0.0)
    upto = jnp.where(iota((tok_rows, tok_rows), 0) <= iota((tok_rows, tok_rows), 1), 1.0, 0.0)
    before = dot(onehot.astype(BF16), upto.astype(BF16))
    rank = jnp.sum(onehot * before, axis=0, keepdims=True) - 1.0
    slot = ids * cap + rank.astype(jnp.int32)
    return jnp.where(iota((experts * cap, tok_rows), 0) == slot, 1.0, 0.0)


VMEM = pl.BlockSpec(memory_space=pltpu.VMEM)
SMEM = pl.BlockSpec(memory_space=pltpu.SMEM)
HBM = pl.BlockSpec(memory_space=pltpu.HBM)


class Stream:
    def __init__(self, copies, ahead):
        self.copies, self.ahead, self.started, self.done = copies, ahead, 0, set()
        self.start(ahead)

    def start(self, upto):
        while self.started < min(upto, len(self.copies)):
            self.copies[self.started].start()
            self.started += 1

    def need(self, i):
        self.start(i + self.ahead)
        if i not in self.done:
            self.copies[i].wait()
            self.done.add(i)


class Operand:
    def __init__(self, held, stream=None, first=0, count=0):
        self.held, self.stream, self.first, self.count = held, stream, first, count

    def piece(self, t):
        if self.stream:
            self.stream.need(self.first + t)
        return self.held

    def whole(self):
        for t in range(self.count):
            self.piece(t)
        return self.held


class Result:
    def __init__(self, held, copies=()):
        self.held, self.copies = held, copies

    def send(self, t):
        if self.copies:
            self.copies[t].start()

    def finish(self):
        for copy in self.copies:
            copy.wait()


def in_hbm(array):
    return pltpu.with_memory_space_constraint(array, pltpu.HBM)


def in_vmem(array):
    return pltpu.with_memory_space_constraint(array, pltpu.VMEM)


def kept_in_vmem(array):
    return (array, None, None)


def full(array):
    return (array, array.shape, [(Ellipsis, Ellipsis)])


def firsts(array):
    return (array, array.shape, [(t, t) for t in range(array.shape[0])])


def columns(array, start, count):
    return (array, (array.shape[0], count), [((slice(None), pl.ds(start, count)), Ellipsis)])


def call(
    kernel, info, big, outs, small=(), after=(), after_vmem=(), passed=(), scratch=(), flops=0, exps=0, limit=32
):
    moved = sum(2 * a.size for a, _, _ in big) + sum(2 * o.size for o, _ in outs)
    held = []
    for array, dims, pieces in big:
        if pieces:
            held.append(pltpu.VMEM(dims, array.dtype))
    for out, pieces in outs:
        if pieces:
            held.append(pltpu.VMEM(out.shape, out.dtype))
    fetches = sum(len(pieces or ()) for _, _, pieces in big)
    sends = sum(len(pieces or ()) for _, pieces in outs)
    held += [pltpu.SemaphoreType.DMA((max(count, 1),)) for count in (fetches, sends, len(passed))]

    def body(*refs):
        refs = list(refs)

        def take(count):
            taken = refs[:count]
            del refs[:count]
            return taken

        info_ref = take(1)[0]
        small_refs, big_refs = take(len(small)), take(len(big))
        take(len(after) + len(after_vmem))
        pass_refs = take(len(passed))
        out_refs, passed_refs = take(len(outs)), take(len(passed))
        held_refs = [take(1)[0] if pieces else ref for ref, (_, _, pieces) in zip(big_refs, big)]
        made_refs = [take(1)[0] if pieces else ref for ref, (_, pieces) in zip(out_refs, outs)]
        fetch_sems, send_sems, pass_sems = take(3)
        copies, spans = [], []
        for source, target, (_, _, pieces) in zip(big_refs, held_refs, big):
            spans.append((len(copies), len(pieces or ())))
            for there, here in pieces or ():
                sem = fetch_sems.at[len(copies)]
                copies.append(pltpu.make_async_copy(source.at[there], target.at[here], sem))
        stream = Stream(copies, 3)
        passing = [
            pltpu.make_async_copy(source, target, pass_sems.at[i])
            for i, (source, target) in enumerate(zip(pass_refs, passed_refs))
        ]
        for copy in passing:
            copy.start()
        operands = [
            Operand(ref, stream if count else None, at, count)
            for ref, (at, count) in zip(held_refs, spans)
        ]
        results, used = [], 0
        for target, source, (_, pieces) in zip(out_refs, made_refs, outs):
            sent = []
            for at in pieces or ():
                sent.append(pltpu.make_async_copy(source.at[at], target.at[at], send_sems.at[used]))
                used += 1
            results.append(Result(source, sent))
        kernel(info_ref, *small_refs, *operands, *results, *refs)
        for i in range(len(copies)):
            stream.need(i)
        for result in results:
            result.finish()
        for copy in passing:
            copy.wait()

    arrays = [in_hbm(a) if pieces else in_vmem(a) for a, _, pieces in big]
    arrays += [in_hbm(array) for array in after] + [in_vmem(array) for array in after_vmem]
    arrays += [in_hbm(array) for array in passed]
    return pl.pallas_call(
        body,
        out_shape=[(pltpu.HBM if pieces else pltpu.VMEM)(o.shape, o.dtype) for o, pieces in outs]
        + [pltpu.VMEM(array.shape, array.dtype) for array in passed],
        in_specs=[SMEM]
        + [VMEM] * len(small)
        + [HBM if pieces else VMEM for _, _, pieces in big]
        + [HBM] * len(after)
        + [VMEM] * len(after_vmem)
        + [HBM] * len(passed),
        out_specs=[HBM if pieces else VMEM for _, pieces in outs] + [VMEM] * len(passed),
        scratch_shapes=held + list(scratch),
        compiler_params=pltpu.CompilerParams(vmem_limit_bytes=limit << 20),
        cost_estimate=pl.CostEstimate(flops=flops, bytes_accessed=moved, transcendentals=exps),
    )(info, *small, *arrays)


def shape(*dims):
    return jax.ShapeDtypeStruct(dims, BF16)


def tie(values, after=(), after_vmem=(), hbm=False):
    count = len(values)
    space, spec, pin = (pltpu.HBM, HBM, in_hbm) if hbm else (pltpu.VMEM, VMEM, in_vmem)
    return pl.pallas_call(
        lambda *refs: None,
        out_shape=[space(value.shape, value.dtype) for value in values],
        in_specs=[spec] * count + [HBM] * len(after) + [VMEM] * len(after_vmem),
        out_specs=[spec] * count,
        input_output_aliases={i: i for i in range(count)},
        compiler_params=pltpu.CompilerParams(vmem_limit_bytes=4 << 20),
    )(
        *(pin(value) for value in values),
        *(in_hbm(array) for array in after),
        *(in_vmem(array) for array in after_vmem),
    )


def staged(array, start, count, after):
    def body(source, _, target, sem):
        copy = pltpu.make_async_copy(source.at[:, pl.ds(start, count)], target, sem)
        copy.start()
        copy.wait()

    return pl.pallas_call(
        body,
        out_shape=pltpu.VMEM((array.shape[0], count), array.dtype),
        in_specs=[HBM, VMEM],
        out_specs=VMEM,
        scratch_shapes=[pltpu.SemaphoreType.DMA],
        compiler_params=pltpu.CompilerParams(vmem_limit_bytes=4 << 20),
        cost_estimate=pl.CostEstimate(
            flops=0, bytes_accessed=4 * array.shape[0] * count, transcendentals=0
        ),
    )(in_hbm(array), in_vmem(after))


def dispatch_kernel(experts, cap, info_ref, ids, tokens, out):
    place = slot_rows(ids.whole()[info_ref[0]], experts, cap).astype(BF16)
    out.held[...] = dot(place, tokens.whole()[...]).astype(BF16)
    out.send(0)


def collect_kernel(experts, cap, info_ref, ids_ref, rows, out):
    place = slot_rows(ids_ref[info_ref[0]], experts, cap).T.astype(BF16)
    out.held[...] = dot(place, rows.whole()[...]).astype(BF16)
    out.send(0)


def side_kernel(experts, cap, info_ref, ids_ref, near, out):
    place = slot_rows(ids_ref[info_ref[0]], experts, cap).T.astype(BF16)
    rows_ref = near.whole()
    for i in range(2):
        rows = flat_rows(rows_ref[:, i])
        out.held[:, i * LANES : (i + 1) * LANES] = dot(place, rows).astype(BF16)
    out.send(0)


def project_kernel(places, experts, cap, tile, info_ref, *refs):
    rows, weight, sides, out = refs[:places], refs[places], refs[places + 1 : -1], refs[-1]
    chans = weight.held.shape[1]

    def store(at, lo, made):
        made = made.astype(BF16)
        for e in range(experts):
            out.held[e, at, :, lo : lo + made.shape[1]] = made[e * cap : (e + 1) * cap, :]

    for lo in range(0, chans, tile):
        for at in range(places):
            block = flat_rows(rows[at].whole()[...])
            store(at, lo, dot(block, weight.whole()[:, lo : lo + tile]))
    if sides:
        first = flat_rows(rows[0].whole()[...])
        store(0, chans, dot(first, sides[0].whole()[...]))
        steps = [ref.whole()[...].astype(F32) for ref in sides[1:]]
        spare = LANES - sum(part.shape[0] for part in steps)
        steps.append(jnp.zeros((spare, steps[0].shape[1]), F32))
        steps = jnp.concatenate(steps, axis=0).astype(BF16)
        made = lax.dot_general(
            first, steps, (((1,), (1,)), ((), ())), preferred_element_type=F32
        )
        store(1, chans, made)
    out.send(0)


def gate_kernel(tile, info_ref, *refs):
    count = len(refs) // 2
    weight, outs = refs[count], refs[count + 1 :]
    rows = [flat_rows(ref.whole()[...]) for ref in refs[:count]]
    for lo in range(0, weight.held.shape[1], tile):
        part = weight.whole()[:, lo : lo + tile]
        for block, out in zip(rows, outs):
            out.held[:, lo : lo + tile] = dot(block, part).astype(BF16)
    for out in outs:
        out.send(0)


def output_kernel(at, experts, cap, tile, info_ref, scanned, gate, weight, out):
    gates = jax.nn.silu(gate.held[...].astype(F32))
    gated = (flat_rows(scanned.held[:, at]).astype(F32) * gates).astype(BF16)
    for lo in range(0, weight.held.shape[1], tile):
        made = dot(gated, weight.held[:, lo : lo + tile]).astype(BF16)
        for e in range(experts):
            out.held[e, :, lo : lo + tile] = made[e * cap : (e + 1) * cap, :]


def scan_kernel(
    cfg,
    info_ref,
    ids_ref,
    head_ref,
    chan_ref,
    near,
    side,
    far,
    *refs,
):
    experts, cap, tok_rows, nstate, chn, heads = cfg
    blocks = ids_ref.shape[0]
    taps = 4
    out_near, out_far, inner_ref, made_ref = refs
    far_ref, side_ref = far.whole(), side.whole()
    inner_ref[:8, :] = jnp.zeros((8, chn), F32)

    for q in (*range(2, blocks), 0, 1):
        b = info_ref[1 + q]
        place = slot_rows(ids_ref[b], experts, cap).T.astype(BF16)
        rows = flat_rows(near.whole()[:, q, :, :chn] if q < 2 else far_ref[:, q - 2])
        inner_ref[pl.ds(8 + b * tok_rows, tok_rows), :] = dot(place, rows)

    lower = iota((tok_rows, tok_rows), 0) >= iota((tok_rows, tok_rows), 1)
    ones = jnp.where(lower, 1.0, 0.0)
    first = iota((tok_rows, LANES), 1) < HEAD_DIM
    spread = jnp.where(
        iota((2 * LANES, chn), 0) % LANES == iota((2 * LANES, chn), 1) // HEAD_DIM, 1.0, 0.0
    ).astype(BF16)

    def widen(values):
        high = values.astype(BF16)
        low = (values - high.astype(F32)).astype(BF16)
        return dot(jnp.concatenate([high, low], axis=1), spread)

    state = jnp.zeros((nstate, chn), F32)
    for b in range(blocks):
        q = info_ref[1 + blocks + b]
        total = chan_ref[taps : taps + 1, :]
        for j in range(taps):
            start = 8 + b * tok_rows - (taps - 1) + j
            total = total + chan_ref[j : j + 1, :] * inner_ref[start : start + tok_rows, :]
        signal = jax.nn.silu(total)

        own_head = iota((LANES, LANES), 0) == iota((LANES, LANES), 1) + info_ref[
            1 + 2 * blocks + b
        ] * heads
        own_head = jnp.where(own_head & (iota((LANES, LANES), 1) < heads), 1.0, 0.0)
        raw = dot(side_ref[q, :, LANES:], own_head.astype(BF16))
        step = jax.nn.softplus(raw + head_ref[0:1, :])
        summed = jnp.dot(
            ones,
            step * head_ref[1:2, :],
            preferred_element_type=F32,
            precision=lax.Precision.HIGHEST,
        )
        source = summed - jnp.log(step)
        source_t = source.T
        left = jnp.exp(summed[tok_rows - 1 :, :] - source)
        wide = widen(jnp.concatenate([jnp.exp(summed), left], axis=0))
        kept, tail = wide[:tok_rows], wide[tok_rows:]

        both = side_ref[q, :, :LANES]
        keys_t = both.astype(F32).T.astype(BF16)[:nstate, :]
        queries = both[:, nstate:]
        scores = dot(queries, keys_t)
        rest = chan_ref[taps + 1 : taps + 2, :] * signal
        if b > 0:
            rest = rest + dot(queries, state.astype(BF16)) * kept
        if b < blocks - 1:
            state = kept[tok_rows - 1 :, :] * state + dot(keys_t, (signal * tail).astype(BF16))

        for pair in range(heads // 2):
            lanes = slice(pair * LANES, (pair + 1) * LANES)
            values = signal[:, lanes]
            values = jnp.concatenate(
                [jnp.where(first, values, 0.0), jnp.where(first, 0.0, values)], axis=0
            ).astype(BF16)
            weights = []
            for h in (2 * pair, 2 * pair + 1):
                gaps = summed[:, h : h + 1] - source_t[h : h + 1, :]
                decay = jnp.exp(jnp.where(lower, gaps, -jnp.inf))
                weights.append((scores * decay).astype(BF16))
            local = dot(jnp.concatenate(weights, axis=1), values)
            made_ref[b * tok_rows : (b + 1) * tok_rows, lanes] = (rest[:, lanes] + local).astype(BF16)

    for q in range(blocks):
        b = info_ref[1 + q]
        place = slot_rows(ids_ref[b], experts, cap).astype(BF16)
        start = pl.multiple_of(b * tok_rows, tok_rows)
        leaving = dot(place, made_ref[pl.ds(start, tok_rows), :]).astype(BF16)
        for e in range(experts):
            piece = leaving[e * cap : (e + 1) * cap, :]
            if q < 2:
                out_near.held[e, q] = piece
            else:
                out_far.held[e, q - 2] = piece


def per_device(
    tokens,
    route,
    w_inner,
    w_state,
    w_step,
    step_bias,
    decay_log,
    skip_gain,
    conv_weight,
    conv_bias,
    w_out,
):
    tok_rows, width = tokens.shape[1], tokens.shape[2]
    experts = lax.axis_size("expert")
    shards = lax.axis_size("context")
    cap = 2 * tok_rows // experts
    slots = experts * cap
    chans = w_inner.shape[3]
    heads = w_step.shape[2]
    nstate = w_state.shape[2] // 2
    chips = shards // 2
    far_count = shards - 2

    here = lax.axis_index("context").astype(jnp.int32)
    blocks = jnp.arange(shards, dtype=jnp.int32)
    order = 2 * ((here // 2 - blocks // 2) % chips) + ((here % 2) ^ (blocks % 2))
    groups = 2 * ((blocks // 2 - here // 2) % chips) + ((here % 2) ^ (blocks % 2))
    block_at = 2 * ((here // 2 - blocks // 2) % chips) + ((here % 2) ^ (blocks % 2))
    info = jnp.concatenate([here[None], block_at, order, groups])
    ids = route.reshape(shards, 1, tok_rows)
    swap = [(c, c ^ 1) for c in range(shards)]

    def hop(k):
        return [(c, ((c // 2 + k) % chips) * 2 + c % 2) for c in range(shards)]

    def permute(value, pairs):
        return lax.ppermute(value, "context", pairs)

    def spread(value):
        made = [value, permute(value, swap)]
        for k in range(1, chips):
            arrived = permute(value, hop(k))
            made += [arrived, permute(arrived, swap)]
        return made

    def exchange(value):
        return lax.all_to_all(value, "expert", split_axis=0, concat_axis=0, tiled=True)

    w_flat = w_inner[0].reshape(width, 2 * chans)

    once = [Ellipsis]
    outgoing = call(
        functools.partial(dispatch_kernel, experts, cap),
        info, [full(ids), full(tokens[0])], [(shape(slots, width), once)],
        flops=2 * slots * tok_rows * width,
    )[0]
    own = exchange(outgoing.reshape(experts, cap, width))
    steps = spread(tie([w_step[0]], [outgoing])[0].T)
    own = tie([own], [w_flat], steps)[0]
    w_in = staged(w_flat, chans, chans, own)
    swapped = permute(own, swap)
    near = call(
        functools.partial(project_kernel, 2, experts, cap, 256),
        info,
        [kept_in_vmem(array) for array in (own, swapped, w_in, w_state[0], *steps)],
        [(shape(experts, 2, cap, chans + LANES), once)],
        flops=4 * slots * width * (chans + LANES),
    )[0]
    distant = []
    for k in range(1, chips):
        arrived = tie([permute(own, hop(k))], [near], hbm=True)[0]
        distant += [arrived, permute(arrived, swap)]
    far = call(
        functools.partial(project_kernel, far_count, experts, cap, 256),
        info,
        [full(rows) for rows in distant] + [columns(w_flat, chans, chans)],
        [(shape(experts, far_count, cap, chans), once)],
        flops=2 * far_count * slots * width * chans,
    )[0]
    near_back = exchange(near)
    far_back = exchange(far)

    def gates(rows, fetch):
        return call(
            functools.partial(gate_kernel, 256),
            info,
            [fetch(part) for part in rows]
            + [columns(w_flat, 0, chans)],
            [(shape(slots, chans), once)] * len(rows),
            after=[near],
            flops=2 * len(rows) * slots * width * chans,
        )

    gate_near = gates([own, swapped], kept_in_vmem)
    gate_far = gates(distant, full)

    lanes = (slice(None),) * 3 + (pl.ds(chans, LANES),)
    side = call(
        functools.partial(side_kernel, experts, cap),
        info,
        [(near_back, (experts, 2, cap, LANES), [(lanes, Ellipsis)])],
        [(shape(tok_rows, 2 * LANES), once)],
        small=[ids],
        after=[far, gate_near[0], gate_far[0]],
        flops=2 * slots * tok_rows * 2 * LANES,
    )[0]
    sides = jnp.stack(spread(side))

    def padded_heads(row):
        return jnp.pad(row, (0, LANES - heads))[None, :]

    head_rows = jnp.concatenate(
        [padded_heads(step_bias), padded_heads(-jnp.exp(decay_log)), jnp.zeros((6, LANES), F32)]
    )
    chan_rows = jnp.concatenate(
        [conv_weight, conv_bias[None, :], jnp.repeat(skip_gain, HEAD_DIM)[None, :]]
    )
    chan_rows = jnp.pad(chan_rows, ((0, 2), (0, 0)))
    cfg = (experts, cap, tok_rows, nstate, chans, heads)
    each = list(range(shards))
    near_out, far_out = call(
        functools.partial(scan_kernel, cfg),
        info,
        [full(near_back), kept_in_vmem(sides), kept_in_vmem(far_back)],
        [
            (shape(experts, 2, cap, chans), None),
            (shape(experts, far_count, cap, chans), None),
        ],
        small=[ids, head_rows, chan_rows],
        scratch=[
            pltpu.VMEM((8 + shards * tok_rows, chans), F32),
            pltpu.VMEM((shards * tok_rows, chans), BF16),
        ],
        flops=2 * shards * tok_rows * chans * (2 * slots + 2 * nstate + 2 * tok_rows + 768),
        exps=shards * tok_rows * tok_rows * heads,
    )
    far_ret = exchange(far_out)
    near_ret = exchange(near_out)
    def output(scanned, gate, at, after=()):
        return call(
            functools.partial(output_kernel, at, experts, cap, 512),
            info,
            [kept_in_vmem(array) for array in (scanned, gate, w_out[0])],
            [(shape(experts, cap, width), None)],
            after_vmem=after,
            flops=2 * slots * width * chans,
        )[0]

    others = [permute(output(far_ret, gate_far[2 * k - 1], 2 * k - 1), swap) for k in range(1, chips)]
    hopped = []
    for k in range(1, chips):
        pair = output(far_ret, gate_far[2 * k - 2], 2 * k - 2).astype(F32) + others[k - 1].astype(F32)
        hopped.append(permute(pair.astype(BF16), hop(chips - k)))
    part_swap = permute(output(near_ret, gate_near[1], 1), swap)
    part_own = output(near_ret, gate_near[0], 0, hopped)
    summed = part_own.astype(F32) + part_swap.astype(F32)
    for part in hopped:
        summed = summed + part.astype(F32)
    returned = exchange(summed.astype(BF16)).reshape(slots, width)
    result = call(
        functools.partial(collect_kernel, experts, cap),
        info, [kept_in_vmem(returned)], [(shape(tok_rows, width), once)],
        small=[ids],
        flops=2 * slots * tok_rows * width,
    )[0]
    return result[None]


def solution(mesh):
    in_specs = (
        P("expert", "context", None),
        P("expert", None, None),
        P("expert", None, None, "context"),
        P("expert", None, None),
        P("expert", None, "context"),
        P("context"),
        P("context"),
        P("context"),
        P(None, "context"),
        P("context"),
        P("expert", "context", None),
    )
    out_specs = P("expert", "context", None)
    return jax.shard_map(
        per_device, mesh=mesh, in_specs=in_specs, out_specs=out_specs, check_vma=False
    )
```

```python
import functools

import jax
import jax.numpy as jnp
from jax import lax
from jax.experimental import pallas as pl
from jax.experimental.pallas import tpu as pltpu
from jax.sharding import PartitionSpec as P

HEAD_DIM = 64
LANES = 128
BF16 = jnp.bfloat16
F32 = jnp.float32


def iota(shape, axis):
    return lax.broadcasted_iota(jnp.int32, shape, axis)


def dot(a, b):
    return jnp.dot(a, b, preferred_element_type=F32)


def flat_rows(pieces):
    count, rows, lanes = pieces.shape
    if rows % 16:
        return pieces.astype(F32).reshape(count * rows, lanes).astype(BF16)
    return pieces.reshape(count * rows, lanes)


def slot_rows(ids, experts, cap, me=0):
    tok_rows = ids.shape[1]
    onehot = jnp.where(iota((experts, tok_rows), 0) == ids, 1.0, 0.0)
    upto = jnp.where(iota((tok_rows, tok_rows), 0) <= iota((tok_rows, tok_rows), 1), 1.0, 0.0)
    before = dot(onehot.astype(BF16), upto.astype(BF16))
    rank = jnp.sum(onehot * before, axis=0, keepdims=True) - 1.0
    slot = (ids ^ me) * cap + rank.astype(jnp.int32)
    return jnp.where(iota((experts * cap, tok_rows), 0) == slot, 1.0, 0.0)


VMEM = pl.BlockSpec(memory_space=pltpu.VMEM)
SMEM = pl.BlockSpec(memory_space=pltpu.SMEM)
HBM = pl.BlockSpec(memory_space=pltpu.HBM)


class Stream:
    def __init__(self, copies, ahead):
        self.copies, self.ahead, self.started, self.done = copies, ahead, 0, set()
        self.start(ahead)

    def start(self, upto):
        while self.started < min(upto, len(self.copies)):
            self.copies[self.started].start()
            self.started += 1

    def need(self, i):
        self.start(i + self.ahead)
        if i not in self.done:
            self.copies[i].wait()
            self.done.add(i)


class Operand:
    def __init__(self, held, stream=None, first=0, count=0):
        self.held, self.stream, self.first, self.count = held, stream, first, count

    def piece(self, t):
        if self.stream:
            self.stream.need(self.first + t)
        return self.held

    def whole(self):
        for t in range(self.count):
            self.piece(t)
        return self.held


class Result:
    def __init__(self, held, copies=()):
        self.held, self.copies = held, copies

    def send(self, t):
        if self.copies:
            self.copies[t].start()

    def finish(self):
        for copy in self.copies:
            copy.wait()


def in_hbm(array):
    return pltpu.with_memory_space_constraint(array, pltpu.HBM)


def in_vmem(array):
    return pltpu.with_memory_space_constraint(array, pltpu.VMEM)


def kept_in_vmem(array):
    return (array, None, None)


def full(array):
    return (array, array.shape, [(Ellipsis, Ellipsis)])


def firsts(array):
    return (array, array.shape, [(t, t) for t in range(array.shape[0])])


def columns(array, start, count):
    return (array, (array.shape[0], count), [((slice(None), pl.ds(start, count)), Ellipsis)])


def call(
    kernel, info, big, outs, small=(), after=(), after_vmem=(), passed=(), scratch=(), flops=0, exps=0, limit=32
):
    moved = sum(2 * a.size for a, _, _ in big) + sum(2 * o.size for o, _ in outs)
    held = []
    for array, dims, pieces in big:
        if pieces:
            held.append(pltpu.VMEM(dims, array.dtype))
    for out, pieces in outs:
        if pieces:
            held.append(pltpu.VMEM(out.shape, out.dtype))
    fetches = sum(len(pieces or ()) for _, _, pieces in big)
    sends = sum(len(pieces or ()) for _, pieces in outs)
    held += [pltpu.SemaphoreType.DMA((max(count, 1),)) for count in (fetches, sends, len(passed))]

    def body(*refs):
        refs = list(refs)

        def take(count):
            taken = refs[:count]
            del refs[:count]
            return taken

        info_ref = take(1)[0]
        small_refs, big_refs = take(len(small)), take(len(big))
        take(len(after) + len(after_vmem))
        pass_refs = take(len(passed))
        out_refs, passed_refs = take(len(outs)), take(len(passed))
        held_refs = [take(1)[0] if pieces else ref for ref, (_, _, pieces) in zip(big_refs, big)]
        made_refs = [take(1)[0] if pieces else ref for ref, (_, pieces) in zip(out_refs, outs)]
        fetch_sems, send_sems, pass_sems = take(3)
        copies, spans = [], []
        for source, target, (_, _, pieces) in zip(big_refs, held_refs, big):
            spans.append((len(copies), len(pieces or ())))
            for there, here in pieces or ():
                sem = fetch_sems.at[len(copies)]
                copies.append(pltpu.make_async_copy(source.at[there], target.at[here], sem))
        stream = Stream(copies, 3)
        passing = [
            pltpu.make_async_copy(source, target, pass_sems.at[i])
            for i, (source, target) in enumerate(zip(pass_refs, passed_refs))
        ]
        for copy in passing:
            copy.start()
        operands = [
            Operand(ref, stream if count else None, at, count)
            for ref, (at, count) in zip(held_refs, spans)
        ]
        results, used = [], 0
        for target, source, (_, pieces) in zip(out_refs, made_refs, outs):
            sent = []
            for at in pieces or ():
                sent.append(pltpu.make_async_copy(source.at[at], target.at[at], send_sems.at[used]))
                used += 1
            results.append(Result(source, sent))
        kernel(info_ref, *small_refs, *operands, *results, *refs)
        for i in range(len(copies)):
            stream.need(i)
        for result in results:
            result.finish()
        for copy in passing:
            copy.wait()

    arrays = [in_hbm(a) if pieces else in_vmem(a) for a, _, pieces in big]
    arrays += [in_hbm(array) for array in after] + [in_vmem(array) for array in after_vmem]
    arrays += [in_hbm(array) for array in passed]
    return pl.pallas_call(
        body,
        out_shape=[(pltpu.HBM if pieces else pltpu.VMEM)(o.shape, o.dtype) for o, pieces in outs]
        + [pltpu.VMEM(array.shape, array.dtype) for array in passed],
        in_specs=[SMEM]
        + [VMEM] * len(small)
        + [HBM if pieces else VMEM for _, _, pieces in big]
        + [HBM] * len(after)
        + [VMEM] * len(after_vmem)
        + [HBM] * len(passed),
        out_specs=[HBM if pieces else VMEM for _, pieces in outs] + [VMEM] * len(passed),
        scratch_shapes=held + list(scratch),
        compiler_params=pltpu.CompilerParams(vmem_limit_bytes=limit << 20),
        cost_estimate=pl.CostEstimate(flops=flops, bytes_accessed=moved, transcendentals=exps),
    )(info, *small, *arrays)


def shape(*dims):
    return jax.ShapeDtypeStruct(dims, BF16)


def tie(values, after=(), after_vmem=(), hbm=False):
    count = len(values)
    space, spec, pin = (pltpu.HBM, HBM, in_hbm) if hbm else (pltpu.VMEM, VMEM, in_vmem)
    return pl.pallas_call(
        lambda *refs: None,
        out_shape=[space(value.shape, value.dtype) for value in values],
        in_specs=[spec] * count + [HBM] * len(after) + [VMEM] * len(after_vmem),
        out_specs=[spec] * count,
        input_output_aliases={i: i for i in range(count)},
        compiler_params=pltpu.CompilerParams(vmem_limit_bytes=4 << 20),
    )(
        *(pin(value) for value in values),
        *(in_hbm(array) for array in after),
        *(in_vmem(array) for array in after_vmem),
    )


def staged(array, start, count, after):
    def body(source, _, target, sem):
        copy = pltpu.make_async_copy(source.at[:, pl.ds(start, count)], target, sem)
        copy.start()
        copy.wait()

    return pl.pallas_call(
        body,
        out_shape=pltpu.VMEM((array.shape[0], count), array.dtype),
        in_specs=[HBM, VMEM],
        out_specs=VMEM,
        scratch_shapes=[pltpu.SemaphoreType.DMA],
        compiler_params=pltpu.CompilerParams(vmem_limit_bytes=4 << 20),
        cost_estimate=pl.CostEstimate(
            flops=0, bytes_accessed=4 * array.shape[0] * count, transcendentals=0
        ),
    )(in_hbm(array), in_vmem(after))


def dispatch_kernel(experts, cap, info_ref, ids, tokens, out):
    place = slot_rows(ids.whole()[info_ref[0]], experts, cap).astype(BF16)
    out.held[...] = dot(place, tokens.whole()[...]).astype(BF16)
    out.send(0)


def sum_kernel(experts, parts, info_ref, *refs):
    me = info_ref[info_ref.shape[0] - 1]
    for r in range(experts):
        total = refs[0].held[r ^ me].astype(F32)
        for ref in refs[1:parts]:
            total = total + ref.held[r ^ me].astype(F32)
        refs[parts + r].held[...] = total.astype(BF16)


def collect_kernel(experts, cap, info_ref, ids_ref, *refs):
    me = info_ref[info_ref.shape[0] - 1]
    place = slot_rows(ids_ref[info_ref[0]], experts, cap, me).T.astype(BF16)
    rows = flat_rows(jnp.stack([ref.held[...] for ref in refs[:experts]]))
    refs[experts].held[...] = dot(place, rows).astype(BF16)
    refs[experts].send(0)


def side_kernel(experts, cap, info_ref, ids_ref, near, out):
    place = slot_rows(ids_ref[info_ref[0]], experts, cap).T.astype(BF16)
    rows_ref = near.whole()
    for i in range(2):
        rows = flat_rows(rows_ref[:, i])
        out.held[:, i * LANES : (i + 1) * LANES] = dot(place, rows).astype(BF16)
    out.send(0)


def project_kernel(places, experts, cap, tile, info_ref, *refs):
    rows, weight, sides, out = refs[:places], refs[places], refs[places + 1 : -1], refs[-1]
    chans = weight.held.shape[1]

    def store(at, lo, made):
        made = made.astype(BF16)
        for e in range(experts):
            out.held[e, at, :, lo : lo + made.shape[1]] = made[e * cap : (e + 1) * cap, :]

    for lo in range(0, chans, tile):
        for at in range(places):
            block = flat_rows(rows[at].whole()[...])
            store(at, lo, dot(block, weight.whole()[:, lo : lo + tile]))
    if sides:
        first = flat_rows(rows[0].whole()[...])
        store(0, chans, dot(first, sides[0].whole()[...]))
        steps = [ref.whole()[...].astype(F32) for ref in sides[1:]]
        spare = LANES - sum(part.shape[0] for part in steps)
        steps.append(jnp.zeros((spare, steps[0].shape[1]), F32))
        steps = jnp.concatenate(steps, axis=0).astype(BF16)
        made = lax.dot_general(
            first, steps, (((1,), (1,)), ((), ())), preferred_element_type=F32
        )
        store(1, chans, made)
    out.send(0)


def gate_kernel(tile, info_ref, *refs):
    count = len(refs) // 2
    weight, outs = refs[count], refs[count + 1 :]
    rows = [flat_rows(ref.whole()[...]) for ref in refs[:count]]
    for lo in range(0, weight.held.shape[1], tile):
        part = weight.whole()[:, lo : lo + tile]
        for block, out in zip(rows, outs):
            out.held[:, lo : lo + tile] = dot(block, part).astype(BF16)
    for out in outs:
        out.send(0)


def output_kernel(at, experts, cap, tile, info_ref, scanned, gate, weight, out):
    gates = jax.nn.silu(gate.held[...].astype(F32))
    gated = (flat_rows(scanned.held[:, at]).astype(F32) * gates).astype(BF16)
    for lo in range(0, weight.held.shape[1], tile):
        made = dot(gated, weight.held[:, lo : lo + tile]).astype(BF16)
        for e in range(experts):
            out.held[e, :, lo : lo + tile] = made[e * cap : (e + 1) * cap, :]


def scan_kernel(
    cfg,
    info_ref,
    ids_ref,
    head_ref,
    chan_ref,
    near,
    side,
    far,
    *refs,
):
    experts, cap, tok_rows, nstate, chn, heads = cfg
    blocks = ids_ref.shape[0]
    taps = 4
    out_near, out_far, inner_ref, made_ref = refs
    far_ref, side_ref = far.whole(), side.whole()
    inner_ref[:8, :] = jnp.zeros((8, chn), F32)

    for q in (*range(2, blocks), 0, 1):
        b = info_ref[1 + q]
        place = slot_rows(ids_ref[b], experts, cap).T.astype(BF16)
        rows = flat_rows(near.whole()[:, q, :, :chn] if q < 2 else far_ref[:, q - 2])
        inner_ref[pl.ds(8 + b * tok_rows, tok_rows), :] = dot(place, rows)

    lower = iota((tok_rows, tok_rows), 0) >= iota((tok_rows, tok_rows), 1)
    ones = jnp.where(lower, 1.0, 0.0)
    first = iota((tok_rows, LANES), 1) < HEAD_DIM
    spread = jnp.where(
        iota((2 * LANES, chn), 0) % LANES == iota((2 * LANES, chn), 1) // HEAD_DIM, 1.0, 0.0
    ).astype(BF16)

    def widen(values):
        high = values.astype(BF16)
        low = (values - high.astype(F32)).astype(BF16)
        return dot(jnp.concatenate([high, low], axis=1), spread)

    state = jnp.zeros((nstate, chn), F32)
    for b in range(blocks):
        q = info_ref[1 + blocks + b]
        total = chan_ref[taps : taps + 1, :]
        for j in range(taps):
            start = 8 + b * tok_rows - (taps - 1) + j
            total = total + chan_ref[j : j + 1, :] * inner_ref[start : start + tok_rows, :]
        signal = jax.nn.silu(total)

        own_head = iota((LANES, LANES), 0) == iota((LANES, LANES), 1) + info_ref[
            1 + 2 * blocks + b
        ] * heads
        own_head = jnp.where(own_head & (iota((LANES, LANES), 1) < heads), 1.0, 0.0)
        raw = dot(side_ref[q, :, LANES:], own_head.astype(BF16))
        step = jax.nn.softplus(raw + head_ref[0:1, :])
        summed = jnp.dot(
            ones,
            step * head_ref[1:2, :],
            preferred_element_type=F32,
            precision=lax.Precision.HIGHEST,
        )
        source = summed - jnp.log(step)
        source_t = source.T
        left = jnp.exp(summed[tok_rows - 1 :, :] - source)
        wide = widen(jnp.concatenate([jnp.exp(summed), left], axis=0))
        kept, tail = wide[:tok_rows], wide[tok_rows:]

        both = side_ref[q, :, :LANES]
        keys_t = both.astype(F32).T.astype(BF16)[:nstate, :]
        queries = both[:, nstate:]
        scores = dot(queries, keys_t)
        rest = chan_ref[taps + 1 : taps + 2, :] * signal
        if b > 0:
            rest = rest + dot(queries, state.astype(BF16)) * kept
        if b < blocks - 1:
            state = kept[tok_rows - 1 :, :] * state + dot(keys_t, (signal * tail).astype(BF16))

        for pair in range(heads // 2):
            lanes = slice(pair * LANES, (pair + 1) * LANES)
            values = signal[:, lanes]
            values = jnp.concatenate(
                [jnp.where(first, values, 0.0), jnp.where(first, 0.0, values)], axis=0
            ).astype(BF16)
            weights = []
            for h in (2 * pair, 2 * pair + 1):
                gaps = summed[:, h : h + 1] - source_t[h : h + 1, :]
                decay = jnp.exp(jnp.where(lower, gaps, -jnp.inf))
                weights.append((scores * decay).astype(BF16))
            local = dot(jnp.concatenate(weights, axis=1), values)
            made_ref[b * tok_rows : (b + 1) * tok_rows, lanes] = (rest[:, lanes] + local).astype(BF16)

    for q in range(blocks):
        b = info_ref[1 + q]
        place = slot_rows(ids_ref[b], experts, cap).astype(BF16)
        start = pl.multiple_of(b * tok_rows, tok_rows)
        leaving = dot(place, made_ref[pl.ds(start, tok_rows), :]).astype(BF16)
        for e in range(experts):
            piece = leaving[e * cap : (e + 1) * cap, :]
            if q < 2:
                out_near.held[e, q] = piece
            else:
                out_far.held[e, q - 2] = piece


def per_device(
    tokens,
    route,
    w_inner,
    w_state,
    w_step,
    step_bias,
    decay_log,
    skip_gain,
    conv_weight,
    conv_bias,
    w_out,
):
    tok_rows, width = tokens.shape[1], tokens.shape[2]
    experts = lax.axis_size("expert")
    shards = lax.axis_size("context")
    cap = 2 * tok_rows // experts
    slots = experts * cap
    chans = w_inner.shape[3]
    heads = w_step.shape[2]
    nstate = w_state.shape[2] // 2
    chips = shards // 2
    far_count = shards - 2

    here = lax.axis_index("context").astype(jnp.int32)
    blocks = jnp.arange(shards, dtype=jnp.int32)
    order = 2 * ((here // 2 - blocks // 2) % chips) + ((here % 2) ^ (blocks % 2))
    groups = 2 * ((blocks // 2 - here // 2) % chips) + ((here % 2) ^ (blocks % 2))
    block_at = 2 * ((here // 2 - blocks // 2) % chips) + ((here % 2) ^ (blocks % 2))
    me = lax.axis_index("expert").astype(jnp.int32)
    info = jnp.concatenate([here[None], block_at, order, groups, me[None]])
    ids = route.reshape(shards, 1, tok_rows)
    swap = [(c, c ^ 1) for c in range(shards)]

    def hop(k):
        return [(c, ((c // 2 + k) % chips) * 2 + c % 2) for c in range(shards)]

    def permute(value, pairs):
        return lax.ppermute(value, "context", pairs)

    def spread(value):
        made = [value, permute(value, swap)]
        for k in range(1, chips):
            arrived = permute(value, hop(k))
            made += [arrived, permute(arrived, swap)]
        return made

    def exchange(value):
        return lax.all_to_all(value, "expert", split_axis=0, concat_axis=0, tiled=True)

    w_flat = w_inner[0].reshape(width, 2 * chans)

    once = [Ellipsis]
    outgoing = call(
        functools.partial(dispatch_kernel, experts, cap),
        info, [full(ids), full(tokens[0])], [(shape(slots, width), once)],
        flops=2 * slots * tok_rows * width,
    )[0]
    own = exchange(outgoing.reshape(experts, cap, width))
    steps = spread(tie([w_step[0]], [outgoing])[0].T)
    own = tie([own], [w_flat], steps)[0]
    w_in = staged(w_flat, chans, chans, own)
    swapped = permute(own, swap)
    near = call(
        functools.partial(project_kernel, 2, experts, cap, 512),
        info,
        [kept_in_vmem(array) for array in (own, swapped, w_in, w_state[0], *steps)],
        [(shape(experts, 2, cap, chans + LANES), once)],
        flops=4 * slots * width * (chans + LANES),
    )[0]
    distant = []
    for k in range(1, chips):
        arrived = tie([permute(own, hop(k))], [near], hbm=True)[0]
        distant += [arrived, permute(arrived, swap)]
    far = call(
        functools.partial(project_kernel, far_count, experts, cap, 256),
        info,
        [full(rows) for rows in distant] + [columns(w_flat, chans, chans)],
        [(shape(experts, far_count, cap, chans), once)],
        flops=2 * far_count * slots * width * chans,
    )[0]
    near_back = exchange(near)
    far_back = exchange(far)

    def gates(rows, fetch):
        return call(
            functools.partial(gate_kernel, 256),
            info,
            [fetch(part) for part in rows]
            + [columns(w_flat, 0, chans)],
            [(shape(slots, chans), once)] * len(rows),
            after=[near],
            flops=2 * len(rows) * slots * width * chans,
        )

    gate_near = gates([own, swapped], kept_in_vmem)
    gate_far = gates(distant, full)

    lanes = (slice(None),) * 3 + (pl.ds(chans, LANES),)
    side = call(
        functools.partial(side_kernel, experts, cap),
        info,
        [(near_back, (experts, 2, cap, LANES), [(lanes, Ellipsis)])],
        [(shape(tok_rows, 2 * LANES), once)],
        small=[ids],
        after=[far, gate_near[0], gate_far[0]],
        flops=2 * slots * tok_rows * 2 * LANES,
    )[0]
    sides = jnp.stack(spread(side))

    def padded_heads(row):
        return jnp.pad(row, (0, LANES - heads))[None, :]

    head_rows = jnp.concatenate(
        [padded_heads(step_bias), padded_heads(-jnp.exp(decay_log)), jnp.zeros((6, LANES), F32)]
    )
    chan_rows = jnp.concatenate(
        [conv_weight, conv_bias[None, :], jnp.repeat(skip_gain, HEAD_DIM)[None, :]]
    )
    chan_rows = jnp.pad(chan_rows, ((0, 2), (0, 0)))
    cfg = (experts, cap, tok_rows, nstate, chans, heads)
    each = list(range(shards))
    near_out, far_out = call(
        functools.partial(scan_kernel, cfg),
        info,
        [full(near_back), kept_in_vmem(sides), kept_in_vmem(far_back)],
        [
            (shape(experts, 2, cap, chans), None),
            (shape(experts, far_count, cap, chans), None),
        ],
        small=[ids, head_rows, chan_rows],
        scratch=[
            pltpu.VMEM((8 + shards * tok_rows, chans), F32),
            pltpu.VMEM((shards * tok_rows, chans), BF16),
        ],
        flops=2 * shards * tok_rows * chans * (2 * slots + 2 * nstate + 2 * tok_rows + 768),
        exps=shards * tok_rows * tok_rows * heads,
    )
    far_ret = exchange(far_out)
    near_ret = exchange(near_out)
    def output(scanned, gate, at, after=()):
        return call(
            functools.partial(output_kernel, at, experts, cap, 512),
            info,
            [kept_in_vmem(array) for array in (scanned, gate, w_out[0])],
            [(shape(experts, cap, width), None)],
            after_vmem=after,
            flops=2 * slots * width * chans,
        )[0]

    others = [permute(output(far_ret, gate_far[2 * k - 1], 2 * k - 1), swap) for k in range(1, chips)]
    hopped = []
    for k in range(1, chips):
        pair = output(far_ret, gate_far[2 * k - 2], 2 * k - 2).astype(F32) + others[k - 1].astype(F32)
        hopped.append(permute(pair.astype(BF16), hop(chips - k)))
    part_swap = permute(output(near_ret, gate_near[1], 1), swap)
    part_own = output(near_ret, gate_near[0], 0, hopped)
    summed = call(
        functools.partial(sum_kernel, experts, 1 + chips),
        info,
        [kept_in_vmem(part) for part in (part_own, part_swap, *hopped)],
        [(shape(cap, width), None)] * experts,
    )
    returned = [
        lax.ppermute(summed[r], "expert", [(e, e ^ r) for e in range(experts)])
        for r in range(experts - 1, 0, -1)
    ]
    returned = [summed[0]] + returned[::-1]
    result = call(
        functools.partial(collect_kernel, experts, cap),
        info, [kept_in_vmem(part) for part in returned], [(shape(tok_rows, width), once)],
        small=[ids],
        flops=2 * slots * tok_rows * width,
    )[0]
    return result[None]


def solution(mesh):
    in_specs = (
        P("expert", "context", None),
        P("expert", None, None),
        P("expert", None, None, "context"),
        P("expert", None, None),
        P("expert", None, "context"),
        P("context"),
        P("context"),
        P("context"),
        P(None, "context"),
        P("context"),
        P("expert", "context", None),
    )
    out_specs = P("expert", "context", None)
    return jax.shard_map(
        per_device, mesh=mesh, in_specs=in_specs, out_specs=out_specs, check_vma=False
    )
```

```python
import functools

import jax
import jax.numpy as jnp
from jax import lax
from jax.experimental import pallas as pl
from jax.experimental.pallas import tpu as pltpu
from jax.sharding import PartitionSpec as P

HEAD_DIM = 64
LANES = 128
BF16 = jnp.bfloat16
F32 = jnp.float32


def iota(shape, axis):
    return lax.broadcasted_iota(jnp.int32, shape, axis)


def dot(a, b):
    return jnp.dot(a, b, preferred_element_type=F32)


def flat_rows(pieces):
    count, rows, lanes = pieces.shape
    if rows % 16:
        return pieces.astype(F32).reshape(count * rows, lanes).astype(BF16)
    return pieces.reshape(count * rows, lanes)


def slot_rows(ids, experts, cap, me=0):
    tok_rows = ids.shape[1]
    onehot = jnp.where(iota((experts, tok_rows), 0) == ids, 1.0, 0.0)
    upto = jnp.where(iota((tok_rows, tok_rows), 0) <= iota((tok_rows, tok_rows), 1), 1.0, 0.0)
    before = dot(onehot.astype(BF16), upto.astype(BF16))
    rank = jnp.sum(onehot * before, axis=0, keepdims=True) - 1.0
    slot = (ids ^ me) * cap + rank.astype(jnp.int32)
    return jnp.where(iota((experts * cap, tok_rows), 0) == slot, 1.0, 0.0)


VMEM = pl.BlockSpec(memory_space=pltpu.VMEM)
SMEM = pl.BlockSpec(memory_space=pltpu.SMEM)
HBM = pl.BlockSpec(memory_space=pltpu.HBM)


class Stream:
    def __init__(self, copies, ahead):
        self.copies, self.ahead, self.started, self.done = copies, ahead, 0, set()
        self.start(ahead)

    def start(self, upto):
        while self.started < min(upto, len(self.copies)):
            self.copies[self.started].start()
            self.started += 1

    def need(self, i):
        self.start(i + self.ahead)
        if i not in self.done:
            self.copies[i].wait()
            self.done.add(i)


class Operand:
    def __init__(self, held, stream=None, first=0, count=0):
        self.held, self.stream, self.first, self.count = held, stream, first, count

    def piece(self, t):
        if self.stream:
            self.stream.need(self.first + t)
        return self.held

    def whole(self):
        for t in range(self.count):
            self.piece(t)
        return self.held


class Result:
    def __init__(self, held, copies=()):
        self.held, self.copies = held, copies

    def send(self, t):
        if self.copies:
            self.copies[t].start()

    def finish(self):
        for copy in self.copies:
            copy.wait()


def in_hbm(array):
    return pltpu.with_memory_space_constraint(array, pltpu.HBM)


def in_vmem(array):
    return pltpu.with_memory_space_constraint(array, pltpu.VMEM)


def kept_in_vmem(array):
    return (array, None, None)


def full(array):
    return (array, array.shape, [(Ellipsis, Ellipsis)])


def firsts(array):
    return (array, array.shape, [(t, t) for t in range(array.shape[0])])


def columns(array, start, count):
    return (array, (array.shape[0], count), [((slice(None), pl.ds(start, count)), Ellipsis)])


def call(
    kernel, info, big, outs, small=(), after=(), after_vmem=(), passed=(), scratch=(), flops=0, exps=0, limit=32
):
    moved = sum(2 * a.size for a, _, _ in big) + sum(2 * o.size for o, _ in outs)
    held = []
    for array, dims, pieces in big:
        if pieces:
            held.append(pltpu.VMEM(dims, array.dtype))
    for out, pieces in outs:
        if pieces:
            held.append(pltpu.VMEM(out.shape, out.dtype))
    fetches = sum(len(pieces or ()) for _, _, pieces in big)
    sends = sum(len(pieces or ()) for _, pieces in outs)
    held += [pltpu.SemaphoreType.DMA((max(count, 1),)) for count in (fetches, sends, len(passed))]

    def body(*refs):
        refs = list(refs)

        def take(count):
            taken = refs[:count]
            del refs[:count]
            return taken

        info_ref = take(1)[0]
        small_refs, big_refs = take(len(small)), take(len(big))
        take(len(after) + len(after_vmem))
        pass_refs = take(len(passed))
        out_refs, passed_refs = take(len(outs)), take(len(passed))
        held_refs = [take(1)[0] if pieces else ref for ref, (_, _, pieces) in zip(big_refs, big)]
        made_refs = [take(1)[0] if pieces else ref for ref, (_, pieces) in zip(out_refs, outs)]
        fetch_sems, send_sems, pass_sems = take(3)
        copies, spans = [], []
        for source, target, (_, _, pieces) in zip(big_refs, held_refs, big):
            spans.append((len(copies), len(pieces or ())))
            for there, here in pieces or ():
                sem = fetch_sems.at[len(copies)]
                copies.append(pltpu.make_async_copy(source.at[there], target.at[here], sem))
        stream = Stream(copies, 3)
        passing = [
            pltpu.make_async_copy(source, target, pass_sems.at[i])
            for i, (source, target) in enumerate(zip(pass_refs, passed_refs))
        ]
        for copy in passing:
            copy.start()
        operands = [
            Operand(ref, stream if count else None, at, count)
            for ref, (at, count) in zip(held_refs, spans)
        ]
        results, used = [], 0
        for target, source, (_, pieces) in zip(out_refs, made_refs, outs):
            sent = []
            for at in pieces or ():
                sent.append(pltpu.make_async_copy(source.at[at], target.at[at], send_sems.at[used]))
                used += 1
            results.append(Result(source, sent))
        kernel(info_ref, *small_refs, *operands, *results, *refs)
        for i in range(len(copies)):
            stream.need(i)
        for result in results:
            result.finish()
        for copy in passing:
            copy.wait()

    arrays = [in_hbm(a) if pieces else in_vmem(a) for a, _, pieces in big]
    arrays += [in_hbm(array) for array in after] + [in_vmem(array) for array in after_vmem]
    arrays += [in_hbm(array) for array in passed]
    return pl.pallas_call(
        body,
        out_shape=[(pltpu.HBM if pieces else pltpu.VMEM)(o.shape, o.dtype) for o, pieces in outs]
        + [pltpu.VMEM(array.shape, array.dtype) for array in passed],
        in_specs=[SMEM]
        + [VMEM] * len(small)
        + [HBM if pieces else VMEM for _, _, pieces in big]
        + [HBM] * len(after)
        + [VMEM] * len(after_vmem)
        + [HBM] * len(passed),
        out_specs=[HBM if pieces else VMEM for _, pieces in outs] + [VMEM] * len(passed),
        scratch_shapes=held + list(scratch),
        compiler_params=pltpu.CompilerParams(vmem_limit_bytes=limit << 20),
        cost_estimate=pl.CostEstimate(flops=flops, bytes_accessed=moved, transcendentals=exps),
    )(info, *small, *arrays)


def shape(*dims):
    return jax.ShapeDtypeStruct(dims, BF16)


def tie(values, after=(), after_vmem=(), hbm=False):
    count = len(values)
    space, spec, pin = (pltpu.HBM, HBM, in_hbm) if hbm else (pltpu.VMEM, VMEM, in_vmem)
    return pl.pallas_call(
        lambda *refs: None,
        out_shape=[space(value.shape, value.dtype) for value in values],
        in_specs=[spec] * count + [HBM] * len(after) + [VMEM] * len(after_vmem),
        out_specs=[spec] * count,
        input_output_aliases={i: i for i in range(count)},
        compiler_params=pltpu.CompilerParams(vmem_limit_bytes=4 << 20),
    )(
        *(pin(value) for value in values),
        *(in_hbm(array) for array in after),
        *(in_vmem(array) for array in after_vmem),
    )


def staged(array, start, count, after):
    def body(source, _, target, sem):
        copy = pltpu.make_async_copy(source.at[:, pl.ds(start, count)], target, sem)
        copy.start()
        copy.wait()

    return pl.pallas_call(
        body,
        out_shape=pltpu.VMEM((array.shape[0], count), array.dtype),
        in_specs=[HBM, VMEM],
        out_specs=VMEM,
        scratch_shapes=[pltpu.SemaphoreType.DMA],
        compiler_params=pltpu.CompilerParams(vmem_limit_bytes=4 << 20),
        cost_estimate=pl.CostEstimate(
            flops=0, bytes_accessed=4 * array.shape[0] * count, transcendentals=0
        ),
    )(in_hbm(array), in_vmem(after))


def dispatch_kernel(experts, cap, info_ref, ids, tokens, out):
    place = slot_rows(ids.whole()[info_ref[0]], experts, cap).astype(BF16)
    out.held[...] = dot(place, tokens.whole()[...]).astype(BF16)
    out.send(0)


def sum_kernel(experts, parts, info_ref, *refs):
    me = info_ref[info_ref.shape[0] - 1]
    for r in range(experts):
        total = refs[0].held[r ^ me].astype(F32)
        for ref in refs[1:parts]:
            total = total + ref.held[r ^ me].astype(F32)
        refs[parts + r].held[...] = total.astype(BF16)


def collect_kernel(experts, cap, info_ref, ids_ref, *refs):
    me = info_ref[info_ref.shape[0] - 1]
    place = slot_rows(ids_ref[info_ref[0]], experts, cap, me).T.astype(BF16)
    rows = flat_rows(jnp.stack([ref.held[...] for ref in refs[:experts]]))
    refs[experts].held[...] = dot(place, rows).astype(BF16)
    refs[experts].send(0)


def side_kernel(experts, cap, info_ref, ids_ref, near, out):
    place = slot_rows(ids_ref[info_ref[0]], experts, cap).T.astype(BF16)
    rows_ref = near.whole()
    for i in range(2):
        rows = flat_rows(rows_ref[:, i])
        out.held[:, i * LANES : (i + 1) * LANES] = dot(place, rows).astype(BF16)
    out.send(0)


def project_kernel(places, experts, cap, tile, info_ref, *refs):
    rows, weight, sides, out = refs[:places], refs[places], refs[places + 1 : -1], refs[-1]
    chans = weight.held.shape[1]

    def store(at, lo, made):
        made = made.astype(BF16)
        for e in range(experts):
            out.held[e, at, :, lo : lo + made.shape[1]] = made[e * cap : (e + 1) * cap, :]

    for lo in range(0, chans, tile):
        for at in range(places):
            block = flat_rows(rows[at].whole()[...])
            store(at, lo, dot(block, weight.whole()[:, lo : lo + tile]))
    if sides:
        first = flat_rows(rows[0].whole()[...])
        store(0, chans, dot(first, sides[0].whole()[...]))
        steps = [ref.whole()[...].astype(F32) for ref in sides[1:]]
        spare = LANES - sum(part.shape[0] for part in steps)
        steps.append(jnp.zeros((spare, steps[0].shape[1]), F32))
        steps = jnp.concatenate(steps, axis=0).astype(BF16)
        made = lax.dot_general(
            first, steps, (((1,), (1,)), ((), ())), preferred_element_type=F32
        )
        store(1, chans, made)
    out.send(0)


def gate_kernel(tile, by_peer, info_ref, *refs):
    count = len(refs) // 2
    weight, outs = refs[count], refs[count + 1 :]
    rows = [ref.whole() for ref in refs[:count]]
    if by_peer:
        me = info_ref[info_ref.shape[0] - 1]
        rows = [flat_rows(jnp.stack([ref[r ^ me] for r in range(ref.shape[0])])) for ref in rows]
    else:
        rows = [flat_rows(ref[...]) for ref in rows]
    for lo in range(0, weight.held.shape[1], tile):
        part = weight.whole()[:, lo : lo + tile]
        for block, out in zip(rows, outs):
            out.held[:, lo : lo + tile] = dot(block, part).astype(BF16)
    for out in outs:
        out.send(0)


def output_kernel(at, experts, cap, tile, info_ref, *refs):
    scanned, (gate, weight, out) = refs[:-3], refs[-3:]
    if len(scanned) > 1:
        me = info_ref[info_ref.shape[0] - 1]
        rows = flat_rows(jnp.stack([ref.held[at] for ref in scanned]))
    else:
        me = 0
        rows = flat_rows(scanned[0].held[:, at])
    gates = jax.nn.silu(gate.held[...].astype(F32))
    gated = (rows.astype(F32) * gates).astype(BF16)
    for lo in range(0, weight.held.shape[1], tile):
        made = dot(gated, weight.held[:, lo : lo + tile]).astype(BF16)
        for r in range(experts):
            out.held[r ^ me, :, lo : lo + tile] = made[r * cap : (r + 1) * cap, :]


def scan_kernel(
    cfg,
    info_ref,
    ids_ref,
    head_ref,
    chan_ref,
    near,
    side,
    far,
    *refs,
):
    experts, cap, tok_rows, nstate, chn, heads = cfg
    blocks = ids_ref.shape[0]
    taps = 4
    out_near, out_far, (inner_ref, made_ref) = refs[0], refs[1:-2], refs[-2:]
    me = info_ref[info_ref.shape[0] - 1]
    far_ref, side_ref = far.whole(), side.whole()
    inner_ref[:8, :] = jnp.zeros((8, chn), F32)

    for q in (*range(2, blocks), 0, 1):
        b = info_ref[1 + q]
        place = slot_rows(ids_ref[b], experts, cap).T.astype(BF16)
        rows = flat_rows(near.whole()[:, q, :, :chn] if q < 2 else far_ref[:, q - 2])
        inner_ref[pl.ds(8 + b * tok_rows, tok_rows), :] = dot(place, rows)

    lower = iota((tok_rows, tok_rows), 0) >= iota((tok_rows, tok_rows), 1)
    ones = jnp.where(lower, 1.0, 0.0)
    first = iota((tok_rows, LANES), 1) < HEAD_DIM
    spread = jnp.where(
        iota((2 * LANES, chn), 0) % LANES == iota((2 * LANES, chn), 1) // HEAD_DIM, 1.0, 0.0
    ).astype(BF16)

    def widen(values):
        high = values.astype(BF16)
        low = (values - high.astype(F32)).astype(BF16)
        return dot(jnp.concatenate([high, low], axis=1), spread)

    state = jnp.zeros((nstate, chn), F32)
    for b in range(blocks):
        q = info_ref[1 + blocks + b]
        total = chan_ref[taps : taps + 1, :]
        for j in range(taps):
            start = 8 + b * tok_rows - (taps - 1) + j
            total = total + chan_ref[j : j + 1, :] * inner_ref[start : start + tok_rows, :]
        signal = jax.nn.silu(total)

        own_head = iota((LANES, LANES), 0) == iota((LANES, LANES), 1) + info_ref[
            1 + 2 * blocks + b
        ] * heads
        own_head = jnp.where(own_head & (iota((LANES, LANES), 1) < heads), 1.0, 0.0)
        raw = dot(side_ref[q, :, LANES:], own_head.astype(BF16))
        step = jax.nn.softplus(raw + head_ref[0:1, :])
        summed = jnp.dot(
            ones,
            step * head_ref[1:2, :],
            preferred_element_type=F32,
            precision=lax.Precision.HIGHEST,
        )
        source = summed - jnp.log(step)
        source_t = source.T
        left = jnp.exp(summed[tok_rows - 1 :, :] - source)
        wide = widen(jnp.concatenate([jnp.exp(summed), left], axis=0))
        kept, tail = wide[:tok_rows], wide[tok_rows:]

        both = side_ref[q, :, :LANES]
        keys_t = both.astype(F32).T.astype(BF16)[:nstate, :]
        queries = both[:, nstate:]
        scores = dot(queries, keys_t)
        rest = chan_ref[taps + 1 : taps + 2, :] * signal
        if b > 0:
            rest = rest + dot(queries, state.astype(BF16)) * kept
        if b < blocks - 1:
            state = kept[tok_rows - 1 :, :] * state + dot(keys_t, (signal * tail).astype(BF16))

        for pair in range(heads // 2):
            lanes = slice(pair * LANES, (pair + 1) * LANES)
            values = signal[:, lanes]
            values = jnp.concatenate(
                [jnp.where(first, values, 0.0), jnp.where(first, 0.0, values)], axis=0
            ).astype(BF16)
            weights = []
            for h in (2 * pair, 2 * pair + 1):
                gaps = summed[:, h : h + 1] - source_t[h : h + 1, :]
                decay = jnp.exp(jnp.where(lower, gaps, -jnp.inf))
                weights.append((scores * decay).astype(BF16))
            local = dot(jnp.concatenate(weights, axis=1), values)
            made_ref[b * tok_rows : (b + 1) * tok_rows, lanes] = (rest[:, lanes] + local).astype(BF16)

    for q in range(blocks):
        b = info_ref[1 + q]
        place = slot_rows(ids_ref[b], experts, cap, 0 if q < 2 else me).astype(BF16)
        start = pl.multiple_of(b * tok_rows, tok_rows)
        leaving = dot(place, made_ref[pl.ds(start, tok_rows), :]).astype(BF16)
        for e in range(experts):
            piece = leaving[e * cap : (e + 1) * cap, :]
            if q < 2:
                out_near.held[e, q] = piece
            else:
                out_far[e].held[q - 2] = piece


def per_device(
    tokens,
    route,
    w_inner,
    w_state,
    w_step,
    step_bias,
    decay_log,
    skip_gain,
    conv_weight,
    conv_bias,
    w_out,
):
    tok_rows, width = tokens.shape[1], tokens.shape[2]
    experts = lax.axis_size("expert")
    shards = lax.axis_size("context")
    cap = 2 * tok_rows // experts
    slots = experts * cap
    chans = w_inner.shape[3]
    heads = w_step.shape[2]
    nstate = w_state.shape[2] // 2
    chips = shards // 2
    far_count = shards - 2

    here = lax.axis_index("context").astype(jnp.int32)
    blocks = jnp.arange(shards, dtype=jnp.int32)
    order = 2 * ((here // 2 - blocks // 2) % chips) + ((here % 2) ^ (blocks % 2))
    groups = 2 * ((blocks // 2 - here // 2) % chips) + ((here % 2) ^ (blocks % 2))
    block_at = 2 * ((here // 2 - blocks // 2) % chips) + ((here % 2) ^ (blocks % 2))
    me = lax.axis_index("expert").astype(jnp.int32)
    info = jnp.concatenate([here[None], block_at, order, groups, me[None]])
    ids = route.reshape(shards, 1, tok_rows)
    swap = [(c, c ^ 1) for c in range(shards)]

    def hop(k):
        return [(c, ((c // 2 + k) % chips) * 2 + c % 2) for c in range(shards)]

    def permute(value, pairs):
        return lax.ppermute(value, "context", pairs)

    def spread(value):
        made = [value, permute(value, swap)]
        for k in range(1, chips):
            arrived = permute(value, hop(k))
            made += [arrived, permute(arrived, swap)]
        return made

    def exchange(value):
        return lax.all_to_all(value, "expert", split_axis=0, concat_axis=0, tiled=True)

    def to_peers(pieces):
        sent = [
            lax.ppermute(pieces[r], "expert", [(e, e ^ r) for e in range(experts)])
            for r in range(experts - 1, 0, -1)
        ]
        return [pieces[0]] + sent[::-1]

    w_flat = w_inner[0].reshape(width, 2 * chans)

    once = [Ellipsis]
    outgoing = call(
        functools.partial(dispatch_kernel, experts, cap),
        info, [full(ids), full(tokens[0])], [(shape(slots, width), once)],
        flops=2 * slots * tok_rows * width,
    )[0]
    own = exchange(outgoing.reshape(experts, cap, width))
    steps = spread(tie([w_step[0]], [outgoing])[0].T)
    own = tie([own], [w_flat], steps)[0]
    w_in = staged(w_flat, chans, chans, own)
    swapped = permute(own, swap)
    near = call(
        functools.partial(project_kernel, 2, experts, cap, 512),
        info,
        [kept_in_vmem(array) for array in (own, swapped, w_in, w_state[0], *steps)],
        [(shape(experts, 2, cap, chans + LANES), once)],
        flops=4 * slots * width * (chans + LANES),
    )[0]
    distant = []
    for k in range(1, chips):
        arrived = tie([permute(own, hop(k))], [near], hbm=True)[0]
        distant += [arrived, permute(arrived, swap)]
    far = call(
        functools.partial(project_kernel, far_count, experts, cap, 256),
        info,
        [full(rows) for rows in distant] + [columns(w_flat, chans, chans)],
        [(shape(experts, far_count, cap, chans), once)],
        flops=2 * far_count * slots * width * chans,
    )[0]
    near_back = exchange(near)
    far_back = exchange(far)

    def gates(rows, fetch, by_peer):
        return call(
            functools.partial(gate_kernel, 256, by_peer),
            info,
            [fetch(part) for part in rows]
            + [columns(w_flat, 0, chans)],
            [(shape(slots, chans), once)] * len(rows),
            after=[near],
            flops=2 * len(rows) * slots * width * chans,
        )

    gate_near = gates([own, swapped], kept_in_vmem, False)
    gate_far = gates(distant, full, True)

    lanes = (slice(None),) * 3 + (pl.ds(chans, LANES),)
    side = call(
        functools.partial(side_kernel, experts, cap),
        info,
        [(near_back, (experts, 2, cap, LANES), [(lanes, Ellipsis)])],
        [(shape(tok_rows, 2 * LANES), once)],
        small=[ids],
        after=[far, gate_near[0], gate_far[0]],
        flops=2 * slots * tok_rows * 2 * LANES,
    )[0]
    sides = jnp.stack(spread(side))

    def padded_heads(row):
        return jnp.pad(row, (0, LANES - heads))[None, :]

    head_rows = jnp.concatenate(
        [padded_heads(step_bias), padded_heads(-jnp.exp(decay_log)), jnp.zeros((6, LANES), F32)]
    )
    chan_rows = jnp.concatenate(
        [conv_weight, conv_bias[None, :], jnp.repeat(skip_gain, HEAD_DIM)[None, :]]
    )
    chan_rows = jnp.pad(chan_rows, ((0, 2), (0, 0)))
    cfg = (experts, cap, tok_rows, nstate, chans, heads)
    each = list(range(shards))
    near_out, *far_out = call(
        functools.partial(scan_kernel, cfg),
        info,
        [full(near_back), kept_in_vmem(sides), kept_in_vmem(far_back)],
        [
            (shape(experts, 2, cap, chans), None),
            *[(shape(far_count, cap, chans), None)] * experts,
        ],
        small=[ids, head_rows, chan_rows],
        scratch=[
            pltpu.VMEM((8 + shards * tok_rows, chans), F32),
            pltpu.VMEM((shards * tok_rows, chans), BF16),
        ],
        flops=2 * shards * tok_rows * chans * (2 * slots + 2 * nstate + 2 * tok_rows + 768),
        exps=shards * tok_rows * tok_rows * heads,
    )
    far_ret = to_peers(far_out)
    near_ret = exchange(tie([near_out], after_vmem=far_ret, hbm=True)[0])

    def output(scanned, gate, at, after=()):
        return call(
            functools.partial(output_kernel, at, experts, cap, 512),
            info,
            [kept_in_vmem(array) for array in (*scanned, gate, w_out[0])],
            [(shape(experts, cap, width), None)],
            after_vmem=after,
            flops=2 * slots * width * chans,
        )[0]

    others = [permute(output(far_ret, gate_far[2 * k - 1], 2 * k - 1), swap) for k in range(1, chips)]
    hopped = []
    for k in range(1, chips):
        pair = output(far_ret, gate_far[2 * k - 2], 2 * k - 2).astype(F32) + others[k - 1].astype(F32)
        hopped.append(permute(pair.astype(BF16), hop(chips - k)))
    part_swap = permute(output([near_ret], gate_near[1], 1), swap)
    part_own = output([near_ret], gate_near[0], 0, hopped)
    summed = call(
        functools.partial(sum_kernel, experts, 1 + chips),
        info,
        [kept_in_vmem(part) for part in (part_own, part_swap, *hopped)],
        [(shape(cap, width), None)] * experts,
    )
    returned = to_peers(summed)
    result = call(
        functools.partial(collect_kernel, experts, cap),
        info, [kept_in_vmem(part) for part in returned], [(shape(tok_rows, width), once)],
        small=[ids],
        flops=2 * slots * tok_rows * width,
    )[0]
    return result[None]


def solution(mesh):
    in_specs = (
        P("expert", "context", None),
        P("expert", None, None),
        P("expert", None, None, "context"),
        P("expert", None, None),
        P("expert", None, "context"),
        P("context"),
        P("context"),
        P("context"),
        P(None, "context"),
        P("context"),
        P("expert", "context", None),
    )
    out_specs = P("expert", "context", None)
    return jax.shard_map(
        per_device, mesh=mesh, in_specs=in_specs, out_specs=out_specs, check_vma=False
    )
```

```python
import functools

import jax
import jax.numpy as jnp
from jax import lax
from jax.experimental import pallas as pl
from jax.experimental.pallas import tpu as pltpu
from jax.sharding import PartitionSpec as P

HEAD_DIM = 64
LANES = 128
BF16 = jnp.bfloat16
F32 = jnp.float32


def iota(shape, axis):
    return lax.broadcasted_iota(jnp.int32, shape, axis)


def dot(a, b):
    return jnp.dot(a, b, preferred_element_type=F32)


def flat_rows(pieces):
    count, rows, lanes = pieces.shape
    if rows % 16:
        return pieces.astype(F32).reshape(count * rows, lanes).astype(BF16)
    return pieces.reshape(count * rows, lanes)


def slot_rows(ids, experts, cap, me=0):
    tok_rows = ids.shape[1]
    onehot = jnp.where(iota((experts, tok_rows), 0) == ids, 1.0, 0.0)
    upto = jnp.where(iota((tok_rows, tok_rows), 0) <= iota((tok_rows, tok_rows), 1), 1.0, 0.0)
    before = dot(onehot.astype(BF16), upto.astype(BF16))
    rank = jnp.sum(onehot * before, axis=0, keepdims=True) - 1.0
    slot = (ids ^ me) * cap + rank.astype(jnp.int32)
    return jnp.where(iota((experts * cap, tok_rows), 0) == slot, 1.0, 0.0)


VMEM = pl.BlockSpec(memory_space=pltpu.VMEM)
SMEM = pl.BlockSpec(memory_space=pltpu.SMEM)
HBM = pl.BlockSpec(memory_space=pltpu.HBM)


class Stream:
    def __init__(self, copies, ahead):
        self.copies, self.ahead, self.started, self.done = copies, ahead, 0, set()
        self.start(ahead)

    def start(self, upto):
        while self.started < min(upto, len(self.copies)):
            self.copies[self.started].start()
            self.started += 1

    def need(self, i):
        self.start(i + self.ahead)
        if i not in self.done:
            self.copies[i].wait()
            self.done.add(i)


class Operand:
    def __init__(self, held, stream=None, first=0, count=0):
        self.held, self.stream, self.first, self.count = held, stream, first, count

    def piece(self, t):
        if self.stream:
            self.stream.need(self.first + t)
        return self.held

    def whole(self):
        for t in range(self.count):
            self.piece(t)
        return self.held


class Result:
    def __init__(self, held, copies=()):
        self.held, self.copies = held, copies

    def send(self, t):
        if self.copies:
            self.copies[t].start()

    def finish(self):
        for copy in self.copies:
            copy.wait()


def in_hbm(array):
    return pltpu.with_memory_space_constraint(array, pltpu.HBM)


def in_vmem(array):
    return pltpu.with_memory_space_constraint(array, pltpu.VMEM)


def kept_in_vmem(array):
    return (array, None, None)


def full(array):
    return (array, array.shape, [(Ellipsis, Ellipsis)])


def firsts(array):
    return (array, array.shape, [(t, t) for t in range(array.shape[0])])


def columns(array, start, count):
    return (array, (array.shape[0], count), [((slice(None), pl.ds(start, count)), Ellipsis)])


def call(
    kernel, info, big, outs, small=(), after=(), after_vmem=(), passed=(), scratch=(), flops=0, exps=0, limit=32
):
    moved = sum(2 * a.size for a, _, _ in big) + sum(2 * o.size for o, _ in outs)
    held = []
    for array, dims, pieces in big:
        if pieces:
            held.append(pltpu.VMEM(dims, array.dtype))
    for out, pieces in outs:
        if pieces:
            held.append(pltpu.VMEM(out.shape, out.dtype))
    fetches = sum(len(pieces or ()) for _, _, pieces in big)
    sends = sum(len(pieces or ()) for _, pieces in outs)
    held += [pltpu.SemaphoreType.DMA((max(count, 1),)) for count in (fetches, sends, len(passed))]

    def body(*refs):
        refs = list(refs)

        def take(count):
            taken = refs[:count]
            del refs[:count]
            return taken

        info_ref = take(1)[0]
        small_refs, big_refs = take(len(small)), take(len(big))
        take(len(after) + len(after_vmem))
        pass_refs = take(len(passed))
        out_refs, passed_refs = take(len(outs)), take(len(passed))
        held_refs = [take(1)[0] if pieces else ref for ref, (_, _, pieces) in zip(big_refs, big)]
        made_refs = [take(1)[0] if pieces else ref for ref, (_, pieces) in zip(out_refs, outs)]
        fetch_sems, send_sems, pass_sems = take(3)
        copies, spans = [], []
        for source, target, (_, _, pieces) in zip(big_refs, held_refs, big):
            spans.append((len(copies), len(pieces or ())))
            for there, here in pieces or ():
                sem = fetch_sems.at[len(copies)]
                copies.append(pltpu.make_async_copy(source.at[there], target.at[here], sem))
        stream = Stream(copies, 3)
        passing = [
            pltpu.make_async_copy(source, target, pass_sems.at[i])
            for i, (source, target) in enumerate(zip(pass_refs, passed_refs))
        ]
        for copy in passing:
            copy.start()
        operands = [
            Operand(ref, stream if count else None, at, count)
            for ref, (at, count) in zip(held_refs, spans)
        ]
        results, used = [], 0
        for target, source, (_, pieces) in zip(out_refs, made_refs, outs):
            sent = []
            for at in pieces or ():
                sent.append(pltpu.make_async_copy(source.at[at], target.at[at], send_sems.at[used]))
                used += 1
            results.append(Result(source, sent))
        kernel(info_ref, *small_refs, *operands, *results, *refs)
        for i in range(len(copies)):
            stream.need(i)
        for result in results:
            result.finish()
        for copy in passing:
            copy.wait()

    arrays = [in_hbm(a) if pieces else in_vmem(a) for a, _, pieces in big]
    arrays += [in_hbm(array) for array in after] + [in_vmem(array) for array in after_vmem]
    arrays += [in_hbm(array) for array in passed]
    return pl.pallas_call(
        body,
        out_shape=[(pltpu.HBM if pieces else pltpu.VMEM)(o.shape, o.dtype) for o, pieces in outs]
        + [pltpu.VMEM(array.shape, array.dtype) for array in passed],
        in_specs=[SMEM]
        + [VMEM] * len(small)
        + [HBM if pieces else VMEM for _, _, pieces in big]
        + [HBM] * len(after)
        + [VMEM] * len(after_vmem)
        + [HBM] * len(passed),
        out_specs=[HBM if pieces else VMEM for _, pieces in outs] + [VMEM] * len(passed),
        scratch_shapes=held + list(scratch),
        compiler_params=pltpu.CompilerParams(vmem_limit_bytes=limit << 20),
        cost_estimate=pl.CostEstimate(flops=flops, bytes_accessed=moved, transcendentals=exps),
    )(info, *small, *arrays)


def shape(*dims):
    return jax.ShapeDtypeStruct(dims, BF16)


def tie(values, after=(), after_vmem=(), hbm=False):
    count = len(values)
    space, spec, pin = (pltpu.HBM, HBM, in_hbm) if hbm else (pltpu.VMEM, VMEM, in_vmem)
    return pl.pallas_call(
        lambda *refs: None,
        out_shape=[space(value.shape, value.dtype) for value in values],
        in_specs=[spec] * count + [HBM] * len(after) + [VMEM] * len(after_vmem),
        out_specs=[spec] * count,
        input_output_aliases={i: i for i in range(count)},
        compiler_params=pltpu.CompilerParams(vmem_limit_bytes=4 << 20),
    )(
        *(pin(value) for value in values),
        *(in_hbm(array) for array in after),
        *(in_vmem(array) for array in after_vmem),
    )


def staged(array, start, count, after):
    def body(source, _, target, sem):
        copy = pltpu.make_async_copy(source.at[:, pl.ds(start, count)], target, sem)
        copy.start()
        copy.wait()

    return pl.pallas_call(
        body,
        out_shape=pltpu.VMEM((array.shape[0], count), array.dtype),
        in_specs=[HBM, VMEM],
        out_specs=VMEM,
        scratch_shapes=[pltpu.SemaphoreType.DMA],
        compiler_params=pltpu.CompilerParams(vmem_limit_bytes=4 << 20),
        cost_estimate=pl.CostEstimate(
            flops=0, bytes_accessed=4 * array.shape[0] * count, transcendentals=0
        ),
    )(in_hbm(array), in_vmem(after))


def dispatch_kernel(experts, cap, info_ref, ids, tokens, out):
    place = slot_rows(ids.whole()[info_ref[0]], experts, cap).astype(BF16)
    out.held[...] = dot(place, tokens.whole()[...]).astype(BF16)
    out.send(0)


def sum_kernel(experts, parts, info_ref, *refs):
    me = info_ref[info_ref.shape[0] - 1]
    for r in range(experts):
        total = refs[0].held[r ^ me].astype(F32)
        for ref in refs[1:parts]:
            total = total + ref.held[r ^ me].astype(F32)
        refs[parts + r].held[...] = total.astype(BF16)


def collect_kernel(experts, cap, info_ref, ids_ref, *refs):
    me = info_ref[info_ref.shape[0] - 1]
    place = slot_rows(ids_ref[info_ref[0]], experts, cap, me).T.astype(BF16)
    rows = flat_rows(jnp.stack([ref.held[...] for ref in refs[:experts]]))
    refs[experts].held[...] = dot(place, rows).astype(BF16)
    refs[experts].send(0)


def side_kernel(experts, cap, info_ref, ids_ref, near, out):
    place = slot_rows(ids_ref[info_ref[0]], experts, cap).T.astype(BF16)
    rows_ref = near.whole()
    for i in range(2):
        rows = flat_rows(rows_ref[:, i])
        out.held[:, i * LANES : (i + 1) * LANES] = dot(place, rows).astype(BF16)
    out.send(0)


def project_kernel(places, experts, cap, tile, info_ref, *refs):
    rows, weight, sides, out = refs[:places], refs[places], refs[places + 1 : -1], refs[-1]
    chans = weight.held.shape[1]

    def store(at, lo, made):
        made = made.astype(BF16)
        for e in range(experts):
            out.held[e, at, :, lo : lo + made.shape[1]] = made[e * cap : (e + 1) * cap, :]

    for lo in range(0, chans, tile):
        for at in range(places):
            block = flat_rows(rows[at].whole()[...])
            store(at, lo, dot(block, weight.whole()[:, lo : lo + tile]))
    if sides:
        first = flat_rows(rows[0].whole()[...])
        store(0, chans, dot(first, sides[0].whole()[...]))
        steps = [ref.whole()[...].astype(F32) for ref in sides[1:]]
        spare = LANES - sum(part.shape[0] for part in steps)
        steps.append(jnp.zeros((spare, steps[0].shape[1]), F32))
        steps = jnp.concatenate(steps, axis=0).astype(BF16)
        made = lax.dot_general(
            first, steps, (((1,), (1,)), ((), ())), preferred_element_type=F32
        )
        store(1, chans, made)
    out.send(0)


def gate_kernel(tile, by_peer, info_ref, *refs):
    count = len(refs) // 2
    weight, outs = refs[count], refs[count + 1 :]
    rows = [ref.whole() for ref in refs[:count]]
    if by_peer:
        me = info_ref[info_ref.shape[0] - 1]
        rows = [flat_rows(jnp.stack([ref[r ^ me] for r in range(ref.shape[0])])) for ref in rows]
    else:
        rows = [flat_rows(ref[...]) for ref in rows]
    for lo in range(0, weight.held.shape[1], tile):
        part = weight.whole()[:, lo : lo + tile]
        for block, out in zip(rows, outs):
            out.held[:, lo : lo + tile] = dot(block, part).astype(BF16)
    for out in outs:
        out.send(0)


def output_kernel(at, experts, cap, tile, info_ref, *refs):
    scanned, (gate, weight, out) = refs[:-3], refs[-3:]
    if len(scanned) > 1:
        me = info_ref[info_ref.shape[0] - 1]
        rows = flat_rows(jnp.stack([ref.held[at] for ref in scanned]))
    else:
        me = 0
        rows = flat_rows(scanned[0].held[:, at])
    gates = jax.nn.silu(gate.held[...].astype(F32))
    gated = (rows.astype(F32) * gates).astype(BF16)
    for lo in range(0, weight.held.shape[1], tile):
        made = dot(gated, weight.held[:, lo : lo + tile]).astype(BF16)
        for r in range(experts):
            out.held[r ^ me, :, lo : lo + tile] = made[r * cap : (r + 1) * cap, :]


def scan_kernel(
    cfg,
    info_ref,
    ids_ref,
    head_ref,
    chan_ref,
    near,
    side,
    far,
    *refs,
):
    experts, cap, tok_rows, nstate, chn, heads = cfg
    blocks = ids_ref.shape[0]
    taps = 4
    out_near, out_far, (inner_ref, made_ref) = refs[0], refs[1:-2], refs[-2:]
    me = info_ref[info_ref.shape[0] - 1]
    far_ref, side_ref = far.whole(), side.whole()
    inner_ref[:8, :] = jnp.zeros((8, chn), F32)

    for q in (*range(2, blocks), 0, 1):
        b = info_ref[1 + q]
        place = slot_rows(ids_ref[b], experts, cap).T.astype(BF16)
        rows = flat_rows(near.whole()[:, q, :, :chn] if q < 2 else far_ref[:, q - 2])
        inner_ref[pl.ds(8 + b * tok_rows, tok_rows), :] = dot(place, rows)

    lower = iota((tok_rows, tok_rows), 0) >= iota((tok_rows, tok_rows), 1)
    ones = jnp.where(lower, 1.0, 0.0)
    first = iota((tok_rows, LANES), 1) < HEAD_DIM
    spread = jnp.where(
        iota((2 * LANES, chn), 0) % LANES == iota((2 * LANES, chn), 1) // HEAD_DIM, 1.0, 0.0
    ).astype(BF16)

    def widen(values):
        high = values.astype(BF16)
        low = (values - high.astype(F32)).astype(BF16)
        return dot(jnp.concatenate([high, low], axis=1), spread)

    state = jnp.zeros((nstate, chn), F32)
    for b in range(blocks):
        q = info_ref[1 + blocks + b]
        total = chan_ref[taps : taps + 1, :]
        for j in range(taps):
            start = 8 + b * tok_rows - (taps - 1) + j
            total = total + chan_ref[j : j + 1, :] * inner_ref[start : start + tok_rows, :]
        signal = jax.nn.silu(total)

        own_head = iota((LANES, LANES), 0) == iota((LANES, LANES), 1) + info_ref[
            1 + 2 * blocks + b
        ] * heads
        own_head = jnp.where(own_head & (iota((LANES, LANES), 1) < heads), 1.0, 0.0)
        raw = dot(side_ref[q, :, LANES:], own_head.astype(BF16))
        step = jax.nn.softplus(raw + head_ref[0:1, :])
        summed = jnp.dot(
            ones,
            step * head_ref[1:2, :],
            preferred_element_type=F32,
            precision=lax.Precision.HIGHEST,
        )
        source = summed - jnp.log(step)
        source_t = source.T
        left = jnp.exp(summed[tok_rows - 1 :, :] - source)
        wide = widen(jnp.concatenate([jnp.exp(summed), left], axis=0))
        kept, tail = wide[:tok_rows], wide[tok_rows:]

        both = side_ref[q, :, :LANES]
        keys_t = both.astype(F32).T.astype(BF16)[:nstate, :]
        queries = both[:, nstate:]
        scores = dot(queries, keys_t)
        rest = chan_ref[taps + 1 : taps + 2, :] * signal
        if b > 0:
            rest = rest + dot(queries, state.astype(BF16)) * kept
        if b < blocks - 1:
            state = kept[tok_rows - 1 :, :] * state + dot(keys_t, (signal * tail).astype(BF16))

        for pair in range(heads // 2):
            lanes = slice(pair * LANES, (pair + 1) * LANES)
            values = signal[:, lanes]
            values = jnp.concatenate(
                [jnp.where(first, values, 0.0), jnp.where(first, 0.0, values)], axis=0
            ).astype(BF16)
            weights = []
            for h in (2 * pair, 2 * pair + 1):
                gaps = summed[:, h : h + 1] - source_t[h : h + 1, :]
                decay = jnp.exp(jnp.where(lower, gaps, -jnp.inf))
                weights.append((scores * decay).astype(BF16))
            local = dot(jnp.concatenate(weights, axis=1), values)
            made_ref[b * tok_rows : (b + 1) * tok_rows, lanes] = (rest[:, lanes] + local).astype(BF16)

    for q in range(blocks):
        b = info_ref[1 + q]
        place = slot_rows(ids_ref[b], experts, cap, 0 if q < 2 else me).astype(BF16)
        start = pl.multiple_of(b * tok_rows, tok_rows)
        leaving = dot(place, made_ref[pl.ds(start, tok_rows), :]).astype(BF16)
        for e in range(experts):
            piece = leaving[e * cap : (e + 1) * cap, :]
            if q < 2:
                out_near.held[e, q] = piece
            else:
                out_far[e].held[q - 2] = piece
        if q == 1:
            out_near.send(0)


def per_device(
    tokens,
    route,
    w_inner,
    w_state,
    w_step,
    step_bias,
    decay_log,
    skip_gain,
    conv_weight,
    conv_bias,
    w_out,
):
    tok_rows, width = tokens.shape[1], tokens.shape[2]
    experts = lax.axis_size("expert")
    shards = lax.axis_size("context")
    cap = 2 * tok_rows // experts
    slots = experts * cap
    chans = w_inner.shape[3]
    heads = w_step.shape[2]
    nstate = w_state.shape[2] // 2
    chips = shards // 2
    far_count = shards - 2

    here = lax.axis_index("context").astype(jnp.int32)
    blocks = jnp.arange(shards, dtype=jnp.int32)
    order = 2 * ((here // 2 - blocks // 2) % chips) + ((here % 2) ^ (blocks % 2))
    groups = 2 * ((blocks // 2 - here // 2) % chips) + ((here % 2) ^ (blocks % 2))
    block_at = 2 * ((here // 2 - blocks // 2) % chips) + ((here % 2) ^ (blocks % 2))
    me = lax.axis_index("expert").astype(jnp.int32)
    info = jnp.concatenate([here[None], block_at, order, groups, me[None]])
    ids = route.reshape(shards, 1, tok_rows)
    swap = [(c, c ^ 1) for c in range(shards)]

    def hop(k):
        return [(c, ((c // 2 + k) % chips) * 2 + c % 2) for c in range(shards)]

    def permute(value, pairs):
        return lax.ppermute(value, "context", pairs)

    def spread(value):
        made = [value, permute(value, swap)]
        for k in range(1, chips):
            arrived = permute(value, hop(k))
            made += [arrived, permute(arrived, swap)]
        return made

    def exchange(value):
        return lax.all_to_all(value, "expert", split_axis=0, concat_axis=0, tiled=True)

    def to_peers(pieces):
        sent = [
            lax.ppermute(pieces[r], "expert", [(e, e ^ r) for e in range(experts)])
            for r in range(experts - 1, 0, -1)
        ]
        return [pieces[0]] + sent[::-1]

    w_flat = w_inner[0].reshape(width, 2 * chans)

    once = [Ellipsis]
    outgoing = call(
        functools.partial(dispatch_kernel, experts, cap),
        info, [full(ids), full(tokens[0])], [(shape(slots, width), once)],
        flops=2 * slots * tok_rows * width,
    )[0]
    own = exchange(outgoing.reshape(experts, cap, width))
    steps = spread(tie([w_step[0]], [outgoing])[0].T)
    own = tie([own], [w_flat], steps)[0]
    w_in = staged(w_flat, chans, chans, own)
    swapped = permute(own, swap)
    near = call(
        functools.partial(project_kernel, 2, experts, cap, 512),
        info,
        [kept_in_vmem(array) for array in (own, swapped, w_in, w_state[0], *steps)],
        [(shape(experts, 2, cap, chans + LANES), once)],
        flops=4 * slots * width * (chans + LANES),
    )[0]
    distant = []
    for k in range(1, chips):
        arrived = tie([permute(own, hop(k))], [near], hbm=True)[0]
        distant += [arrived, permute(arrived, swap)]
    far = call(
        functools.partial(project_kernel, far_count, experts, cap, 256),
        info,
        [full(rows) for rows in distant] + [columns(w_flat, chans, chans)],
        [(shape(experts, far_count, cap, chans), once)],
        flops=2 * far_count * slots * width * chans,
    )[0]
    near_back = exchange(near)
    far_back = exchange(far)

    def gates(rows, fetch, by_peer):
        return call(
            functools.partial(gate_kernel, 256, by_peer),
            info,
            [fetch(part) for part in rows]
            + [columns(w_flat, 0, chans)],
            [(shape(slots, chans), once)] * len(rows),
            after=[near],
            flops=2 * len(rows) * slots * width * chans,
        )

    gate_near = gates([own, swapped], kept_in_vmem, False)
    gate_far = gates(distant, full, True)

    lanes = (slice(None),) * 3 + (pl.ds(chans, LANES),)
    side = call(
        functools.partial(side_kernel, experts, cap),
        info,
        [(near_back, (experts, 2, cap, LANES), [(lanes, Ellipsis)])],
        [(shape(tok_rows, 2 * LANES), once)],
        small=[ids],
        after=[far, gate_near[0], gate_far[0]],
        flops=2 * slots * tok_rows * 2 * LANES,
    )[0]
    sides = jnp.stack(spread(side))

    def padded_heads(row):
        return jnp.pad(row, (0, LANES - heads))[None, :]

    head_rows = jnp.concatenate(
        [padded_heads(step_bias), padded_heads(-jnp.exp(decay_log)), jnp.zeros((6, LANES), F32)]
    )
    chan_rows = jnp.concatenate(
        [conv_weight, conv_bias[None, :], jnp.repeat(skip_gain, HEAD_DIM)[None, :]]
    )
    chan_rows = jnp.pad(chan_rows, ((0, 2), (0, 0)))
    cfg = (experts, cap, tok_rows, nstate, chans, heads)
    each = list(range(shards))
    near_out, *far_out = call(
        functools.partial(scan_kernel, cfg),
        info,
        [full(near_back), kept_in_vmem(sides), kept_in_vmem(far_back)],
        [
            (shape(experts, 2, cap, chans), once),
            *[(shape(far_count, cap, chans), None)] * experts,
        ],
        small=[ids, head_rows, chan_rows],
        scratch=[
            pltpu.VMEM((8 + shards * tok_rows, chans), F32),
            pltpu.VMEM((shards * tok_rows, chans), BF16),
        ],
        flops=2 * shards * tok_rows * chans * (2 * slots + 2 * nstate + 2 * tok_rows + 768),
        exps=shards * tok_rows * tok_rows * heads,
    )
    far_ret = to_peers(far_out)
    near_ret = exchange(tie([near_out], after_vmem=far_ret, hbm=True)[0])

    def output(scanned, gate, at, after=()):
        return call(
            functools.partial(output_kernel, at, experts, cap, 512),
            info,
            [kept_in_vmem(array) for array in (*scanned, gate, w_out[0])],
            [(shape(experts, cap, width), None)],
            after_vmem=after,
            flops=2 * slots * width * chans,
        )[0]

    others = [permute(output(far_ret, gate_far[2 * k - 1], 2 * k - 1), swap) for k in range(1, chips)]
    hopped = []
    for k in range(1, chips):
        pair = output(far_ret, gate_far[2 * k - 2], 2 * k - 2).astype(F32) + others[k - 1].astype(F32)
        hopped.append(permute(pair.astype(BF16), hop(chips - k)))
    part_swap = permute(output([near_ret], gate_near[1], 1), swap)
    part_own = output([near_ret], gate_near[0], 0, hopped)
    summed = call(
        functools.partial(sum_kernel, experts, 1 + chips),
        info,
        [kept_in_vmem(part) for part in (part_own, part_swap, *hopped)],
        [(shape(cap, width), None)] * experts,
    )
    returned = to_peers(summed)
    result = call(
        functools.partial(collect_kernel, experts, cap),
        info, [kept_in_vmem(part) for part in returned], [(shape(tok_rows, width), once)],
        small=[ids],
        flops=2 * slots * tok_rows * width,
    )[0]
    return result[None]


def solution(mesh):
    in_specs = (
        P("expert", "context", None),
        P("expert", None, None),
        P("expert", None, None, "context"),
        P("expert", None, None),
        P("expert", None, "context"),
        P("context"),
        P("context"),
        P("context"),
        P(None, "context"),
        P("context"),
        P("expert", "context", None),
    )
    out_specs = P("expert", "context", None)
    return jax.shard_map(
        per_device, mesh=mesh, in_specs=in_specs, out_specs=out_specs, check_vma=False
    )
```
